32 devices in a mesh: groups: 2 (over y), sec: 4 (over z), tp: 2 (over x), pp: 2 (over core).
Axes of the slice: x: 2, y: 2, z: 4, core: 2. Of those that a mesh axis runs over, the one named last changes fastest.
Arguments:
- query: bfloat16 [512, 4096], P(('groups', 'sec'), ('tp', 'pp')), parts along dimension 0, may hold values from -8 to 8
- keys: bfloat16 [512, 1024], P(('groups', 'sec'), 'tp'), parts along dimension 0, may hold values from -4 to 4
- values: bfloat16 [512, 1024], P(('groups', 'sec'), 'tp'), parts along dimension 0, may hold values from -6 to 6
- residual: bfloat16 [512, 2048], P(('groups', 'sec')), parts along dimension 0, may hold values from -6 to 6
- out_weight: bfloat16 [4096, 2048], P(('tp', 'pp')), may hold values from -0.09375 to 0.09375
- norm_gain: float32 [2048], replicated, may hold values from 0.1 to 1.9
- expert_ids: int32 [512, 2], P(('groups', 'sec')), parts along dimension 0, may hold values from 0 to 7, all different within a row; in each aligned block of 64 rows (0 to 63, 64 to 127, ...) at most 32 rows name the same one
- gate_codes: int32 [512, 2], P(('groups', 'sec')), parts along dimension 0, may hold values from 1 to 255
- doc_lengths: int32 [16], P('groups'), parts along dimension 0, may hold values from 1 to 128, 256 in all
- w_gate: bfloat16 [4, 2048, 16384], P(('tp', 'pp'), None, 'sec'), may hold values from -0.125 to 0.125
- w_up: bfloat16 [4, 2048, 16384], P(('tp', 'pp'), None, 'sec'), may hold values from -0.125 to 0.125
- w_down: bfloat16 [4, 16384, 2048], P(('tp', 'pp'), 'sec'), may hold values from -0.0625 to 0.0625
Outputs:
- scored: bfloat16 [512, 2048], P(('groups', 'sec', 'tp', 'pp')), parts along dimension 0
The draws below stay inside these ranges and needn't reach their ends.
There are 2 independent parts, one for each index of `groups`. The reference program is written for one: setup_inputs(seed, part) draws one part's arguments, and reference() takes and returns one part's arrays. A program takes and returns all parts, laid end to end along the dimension named above; an argument that names none is the same for every part. Nothing has to cross between parts.
Inputs may be any that keep to these rules, and one draw needn't show every extreme that they name: `expert_ids`: each row names two different experts; in each aligned block of 64 rows no expert is named by more than 32 rows, and some block reaches 32. `doc_lengths`: the lengths sum to 256; the longest is exactly 128.
All inputs are finite; a program needn't handle non-finite values.
Results may differ from the reference program's by a relative error of at most 0.015.
Values may be sent and summed in bfloat16 or wider, within the bound.
No kernel may reach another device: no remote copies, remote signals or barrier semaphores. Data moves between devices by JAX's collectives and lax.ppermute only.
A program may use at most 128 MiB of HBM per device.

```python
import math
import jax
import jax.numpy as jnp
import numpy as np
from jax import lax

D = 2048
FF = 8192
QUERY_HEAD_COUNT = 32
KEY_VALUE_HEADS = 8
HEAD_DIMENSION = 128
E = 8
DOCS = 8
BLK = 64
MOSTB = 32
SEQUENCE_TOKENS = 256
TPP = 4


def shared_keys(key):
    normal_portion = jnp.clip(jax.random.normal(jax.random.fold_in(key, 11), (SEQUENCE_TOKENS, KEY_VALUE_HEADS * HEAD_DIMENSION), jnp.float32), -4.0, 4.0)
    return normal_portion


def draw_keys(key, part):
    normal_portion = shared_keys(key)
    return normal_portion.astype(jnp.bfloat16)


def draw_query(key, part):
    drawn = jnp.clip(jax.random.normal(jax.random.fold_in(key, 12), (SEQUENCE_TOKENS, QUERY_HEAD_COUNT * HEAD_DIMENSION), jnp.float32), -4.0, 4.0)
    return drawn.astype(jnp.bfloat16)


def set_ends(result, rng, low, high):
    longest = result.shape.index(max(result.shape))
    spots = []
    for shift in (0, 1):
        where = [jax.random.randint(jax.random.fold_in(rng, axis), (), 0, length) for axis, length in enumerate(result.shape)]
        where[longest] = (where[longest] + shift) % result.shape[longest]
        spots.append(tuple(where))
    return result.at[spots[0]].set(low).at[spots[1]].set(high)


def block_levels(stream_key, dims, cuts, least, largest):
    loudness = 1.0
    for dim, blocks in cuts:
        draws = jax.random.uniform(jax.random.fold_in(jax.random.fold_in(stream_key, 6), dim), (blocks,), jnp.float32, least / len(cuts), largest / len(cuts))
        loudness = loudness * jnp.repeat(jnp.exp(draws), dims[dim] // blocks).reshape((-1,) + (1,) * (len(dims) - 1 - dim))
    return loudness


def profile(number_of, total, bound, slope):
    weights = [(1 << 20) // math.isqrt(standing ** slope) + 1 for standing in range(2, number_of + 1)]
    surplus, counts = total - bound - (number_of - 1), [1] * (number_of - 1)
    while surplus > 0:
        movable = [i for i in range(number_of - 1) if counts[i] < bound]
        mass, left = sum([weights[i] for i in movable]), surplus
        for i in movable:
            extra = min(bound - counts[i], max(1, left * weights[i] // mass), surplus)
            counts[i] = counts[i] + extra
            surplus = surplus - extra
    return np.array([bound] + counts)


def uneven(stream_key, amount, total, most, slope):
    if amount == 2:
        one = jax.random.randint(stream_key, (), max(1, total - most), min(most, total - 1) + 1)
        return jnp.stack([one, total - one])
    lengths = jnp.asarray(profile(amount, total, most, slope), jnp.int32)
    twos = (amount - 1) // 2
    source_of, sink = lengths[1:1 + 2 * twos:2], lengths[2:2 + 2 * twos:2]
    slack = jnp.minimum(source_of - 1, most - sink)
    passed = jax.random.randint(jax.random.fold_in(stream_key, 1), (twos,), 0, 1 << 20) % (slack + 1)
    lengths = lengths.at[1:1 + 2 * twos:2].set(source_of - passed).at[2:2 + 2 * twos:2].set(sink + passed)
    return lengths[jax.random.permutation(jax.random.fold_in(stream_key, 2), amount)]


def shared_out(own_key, own, number, rows, count, top, reach, slope):
    sequence = jax.random.permutation(own_key, count)
    heavy_load, ordinary = shares(count, rows * top, reach, slope, True), shares(count, rows * top, reach, slope, False)
    places = jnp.arange(count)

    def named(tallies, turn):
        used = int((tallies > 0).sum())
        fixed = max(1, used // 4)
        moved = fixed + (places - fixed + turn * (used - fixed)) % max(1, count - fixed)
        return jnp.zeros((count,), jnp.int32).at[sequence[jnp.where(places < fixed, places, moved)]].set(jnp.asarray(tallies, jnp.int32))

    tallies = jnp.where(number % 4 == 0, named(heavy_load, number // 4), named(ordinary, number - number // 4 - 1))
    mixed = jax.random.permutation(jax.random.fold_in(own, 3), count)
    source_of, taker = mixed[0:count // 2 * 2:2], mixed[1:count // 2 * 2:2]
    slack = jnp.minimum(tallies[source_of] - 1, reach - tallies[taker]) // 2
    slack = jnp.where((source_of == sequence[0]) | (taker == sequence[0]) | (tallies[taker] == 0), 0, jnp.maximum(slack, 0))
    moved = jax.random.randint(jax.random.fold_in(own, 4), (count // 2,), 0, 1 << 20) % (slack + 1)
    tallies = tallies.at[source_of].add(-moved).at[taker].add(moved)
    members = jnp.searchsorted(jnp.cumsum(tallies), jnp.arange(rows * top), side="right").astype(jnp.int32)
    listing = members.reshape(top, rows).T
    listing = listing[jax.random.permutation(jax.random.fold_in(own, 1), rows)]
    turn = jax.random.randint(jax.random.fold_in(own, 2), (rows, 1), 0, top)
    return jnp.take_along_axis(listing, (jnp.arange(top)[None, :] + turn) % top, axis=1)


def shares(number_of, total, reach, skew, full):
    weights = [(1 << 20) // math.isqrt(grade ** skew) + 1 for grade in range(1, number_of + 1)]
    largest = reach if full else min(reach, max(-(-total // number_of), total * weights[0] // sum(weights)))
    least = 1 if total - largest >= number_of - 1 else 0
    holding, spare = [largest] + [least] * (number_of - 1), total - largest - least * (number_of - 1)
    while spare > 0:
        movable = [i for i in range(1, number_of) if holding[i] < largest] or [i for i in range(1, number_of) if holding[i] < reach]
        pool, remaining = sum([weights[i] for i in movable]), spare
        for i in movable:
            addition = min(reach - holding[i], max(1, remaining * weights[i] // pool), spare)
            holding[i] = holding[i] + addition
            spare = spare - addition
    return np.array(holding)


def noise(rng, shape, width, bound, shards=(), held_as=jnp.bfloat16):
    loudness = block_levels(rng, shape, shards, -0.22, 0.18) if shards else 1.0
    array = jax.random.normal(rng, shape, jnp.float32) * width * loudness
    return jnp.minimum(jnp.maximum(array, -bound), bound).astype(held_as)


def setup_inputs(seed: int = 0, part: int = 0) -> dict:
    splits = jax.random.split(jax.random.key(seed), 13)
    part_splits = jax.random.split(jax.random.fold_in(splits[12], part), 13)
    query = draw_query(jax.random.fold_in(jax.random.fold_in(splits[12], part), 71), part)
    keys = draw_keys(jax.random.fold_in(jax.random.fold_in(splits[12], part), 71), part)
    values = noise(part_splits[2], (SEQUENCE_TOKENS, KEY_VALUE_HEADS * HEAD_DIMENSION), 1.0, 6.0, ((0, 4), (1, 2)))
    residual = noise(part_splits[3], (SEQUENCE_TOKENS, D), 1.0, 6.0, ((0, 4),))
    out_weight = noise(splits[4], (QUERY_HEAD_COUNT * HEAD_DIMENSION, D), (QUERY_HEAD_COUNT * HEAD_DIMENSION) ** -0.5, 0.09375, ((0, 4),))
    norm_gain = jnp.clip(1.0 + 0.18 * jax.random.normal(splits[5], (D,), jnp.float32), 0.1, 1.9)
    expert_ids_keys = jax.random.split(jax.random.fold_in(part_splits[6], 1), SEQUENCE_TOKENS // BLK)
    expert_ids_turns = jax.random.permutation(jax.random.fold_in(part_splits[6], 3), SEQUENCE_TOKENS // BLK)
    expert_ids = jax.vmap(lambda own, number: shared_out(jax.random.fold_in(part_splits[6], 2), own, number, BLK, E, 2, MOSTB, 2))(expert_ids_keys, expert_ids_turns).reshape((SEQUENCE_TOKENS, 2))
    gate_codes = set_ends(jax.random.randint(part_splits[7], (SEQUENCE_TOKENS, 2), 1, 256), jax.random.fold_in(part_splits[7], 1), 1, 255).astype(jnp.int32)
    doc_lengths = uneven(part_splits[8], DOCS, SEQUENCE_TOKENS, SEQUENCE_TOKENS // 2, 2).astype(jnp.int32)
    w_gate = noise(splits[9], (TPP, D, E * FF // TPP), D ** -0.5, 0.125, ((0, 4), (2, 4)))
    w_up = noise(splits[10], (TPP, D, E * FF // TPP), D ** -0.5, 0.125, ((0, 4), (2, 4)))
    w_down = noise(splits[11], (TPP, E * FF // TPP, D), FF ** -0.5, 0.0625, ((0, 4), (1, 4)))
    return dict(query=query, keys=keys, values=values, residual=residual, out_weight=out_weight, norm_gain=norm_gain, expert_ids=expert_ids, gate_codes=gate_codes, doc_lengths=doc_lengths, w_gate=w_gate, w_up=w_up, w_down=w_down)


def doc_index(positions, doc_lengths):
    doc_ends = jnp.cumsum(doc_lengths).astype(jnp.int32)
    return lax.optimization_barrier(jnp.sum((positions[:, None] >= doc_ends[None, :]).astype(jnp.int32), axis=1))

def reference(query, keys, values, residual, out_weight, norm_gain, expert_ids, gate_codes, doc_lengths, w_gate, w_up, w_down):
    positions = jnp.arange(SEQUENCE_TOKENS, dtype=jnp.int32)
    doc = doc_index(positions, doc_lengths)
    allowed = (positions[None, :] <= positions[:, None]) & (doc[None, :] == doc[:, None])
    group_width = QUERY_HEAD_COUNT // KEY_VALUE_HEADS
    scale = HEAD_DIMENSION ** (-0.5)

    def one_head(head):
        head = head.astype(jnp.int32)
        kv_head = (head // group_width).astype(jnp.int32)
        query_head = lax.dynamic_slice_in_dim(query, head * HEAD_DIMENSION, HEAD_DIMENSION, 1)
        key_head = lax.dynamic_slice_in_dim(keys, kv_head * HEAD_DIMENSION, HEAD_DIMENSION, 1)
        value_head = lax.dynamic_slice_in_dim(values, kv_head * HEAD_DIMENSION, HEAD_DIMENSION, 1)
        scores = jnp.dot(query_head, key_head.T, preferred_element_type=jnp.float32) * scale
        scores = jnp.where(allowed, scores, -1e+30)
        row_max = lax.optimization_barrier(jnp.max(scores, axis=1, keepdims=True))
        weights = jnp.where(allowed, jnp.exp(scores - row_max), 0.0)
        totals = lax.optimization_barrier(jnp.sum(weights, axis=1, keepdims=True))
        summed = jnp.dot(weights.astype(jnp.bfloat16), value_head, preferred_element_type=jnp.float32)
        return (summed / totals).astype(jnp.bfloat16)
    heads_out = lax.map(one_head, jnp.arange(QUERY_HEAD_COUNT, dtype=jnp.int32))
    attended = heads_out.transpose(1, 0, 2).reshape(SEQUENCE_TOKENS, QUERY_HEAD_COUNT * HEAD_DIMENSION)
    stream = residual.astype(jnp.float32) + jnp.dot(attended, out_weight, preferred_element_type=jnp.float32)
    meansq = lax.optimization_barrier(jnp.mean(stream * stream, axis=1, keepdims=True))
    normed = (stream * lax.rsqrt(meansq + 1e-05) * norm_gain).astype(jnp.bfloat16)
    codes = gate_codes.astype(jnp.float32)
    share = codes / lax.optimization_barrier(jnp.sum(codes, axis=1, keepdims=True))
    block_width = FF // TPP
    capacity = SEQUENCE_TOKENS // BLK * MOSTB

    def add_expert(expert, total):
        expert = jnp.asarray(expert).astype(jnp.int32)
        hits = expert_ids == expert
        member = lax.optimization_barrier(jnp.sum(hits.astype(jnp.int32), axis=1))
        coef = lax.optimization_barrier(jnp.sum(jnp.where(hits, share, 0.0), axis=1))
        order = jnp.argsort(1 - member, stable=True)[:capacity].astype(jnp.int32)
        rows = normed[order]
        gate_matrix = lax.dynamic_slice_in_dim(w_gate, expert * block_width, block_width, 2).transpose(1, 0, 2).reshape(D, FF)
        up_matrix = lax.dynamic_slice_in_dim(w_up, expert * block_width, block_width, 2).transpose(1, 0, 2).reshape(D, FF)
        down_matrix = lax.dynamic_slice_in_dim(w_down, expert * block_width, block_width, 1).reshape(FF, D)
        gate = jnp.dot(rows, gate_matrix, preferred_element_type=jnp.float32)
        up = jnp.dot(rows, up_matrix, preferred_element_type=jnp.float32)
        hidden = (jax.nn.silu(gate) * up).astype(jnp.bfloat16)
        expert_out = jnp.dot(hidden, down_matrix, preferred_element_type=jnp.float32)
        return total.at[order].add(coef[order][:, None] * expert_out)
    mixture = lax.fori_loop(0, E, add_expert, jnp.zeros((SEQUENCE_TOKENS, D), jnp.float32))
    return (stream + mixture).astype(jnp.bfloat16)
```

```python
import functools

import jax
import jax.numpy as jnp
from jax import lax
from jax.experimental import pallas as pl
from jax.experimental.pallas import tpu as pltpu
from jax.sharding import PartitionSpec as P

QUERY_HEAD_COUNT = 32
KEY_VALUE_HEADS = 8
HEAD_DIMENSION = 128
E = 8
MOSTB = 32
LANES = 128

neg_fill = -1e30
norm_eps = 1e-05

VMEM = pl.BlockSpec(memory_space=pltpu.VMEM)
SMEM = pl.BlockSpec(memory_space=pltpu.SMEM)
ANY = pl.BlockSpec(memory_space=pl.ANY)


def dot(a, b):
    return jnp.dot(a, b, preferred_element_type=jnp.float32)


def xor_swap(x, axis, k):
    n = lax.axis_size(axis)
    return lax.ppermute(x, axis, [(i, i ^ k) for i in range(n)])


def attention_kernel(back, kv_heads, group, lengths_ref, sec_ref, q_ref, *refs):
    kv_refs = refs[: back + 1]
    weight_hbm, out_ref, weight_ref, attended_ref, sem = refs[back + 1 :]
    copy = pltpu.make_async_copy(weight_hbm, weight_ref, sem)
    copy.start()
    block = q_ref.shape[0]
    head = HEAD_DIMENSION
    span = (back + 1) * block
    sec = sec_ref[0]
    rows = sec * block + lax.broadcasted_iota(jnp.int32, (block, span), 0)
    cols = (sec - back) * block + lax.broadcasted_iota(jnp.int32, (block, span), 1)
    first = jnp.zeros((block, span), jnp.int32)
    end = jnp.int32(0)
    for d in range(lengths_ref.shape[0]):
        end = end + lengths_ref[d]
        first = jnp.where(rows >= end, end, first)
    allowed = (cols <= rows) & (cols >= first)
    allowed = jnp.concatenate([allowed.astype(jnp.float32)] * group, axis=0) > 0.5
    for g in range(kv_heads):
        q = jnp.concatenate(
            [q_ref[:, (g * group + t) * head : (g * group + t + 1) * head] for t in range(group)],
            axis=0,
        )
        k = jnp.concatenate([r[:, g * head : (g + 1) * head] for r in kv_refs], axis=0)
        v = jnp.concatenate(
            [r[:, (kv_heads + g) * head : (kv_heads + g + 1) * head] for r in kv_refs], axis=0
        )
        scores = lax.dot_general(
            q, k, (((1,), (1,)), ((), ())), preferred_element_type=jnp.float32
        ) * (head**-0.5)
        scores = jnp.where(allowed, scores, neg_fill)
        top = jnp.max(scores, axis=1, keepdims=True)
        weights = jnp.where(allowed, jnp.exp(scores - top), 0.0)
        total = jnp.sum(weights, axis=1, keepdims=True)
        summed = dot(weights.astype(jnp.bfloat16), v) / total
        for t in range(group):
            attended_ref[:, (g * group + t) * head : (g * group + t + 1) * head] = summed[
                t * block : (t + 1) * block
            ].astype(jnp.bfloat16)
    copy.wait()
    out_ref[...] = dot(attended_ref[...], weight_ref[...]).astype(jnp.bfloat16)


def norm_kernel(n_parts, residual_ref, gain_ref, info_ref, *refs):
    parts = refs[:n_parts]
    stream_ref, normed_ref = refs[n_parts:]
    width = residual_ref.shape[1]
    stream = residual_ref[...].astype(jnp.float32)
    mixed = parts[0][...].astype(jnp.float32)
    for p in parts[1:]:
        mixed = mixed + p[...].astype(jnp.float32)
    stream = stream + mixed
    stream_ref[...] = stream
    meansq = jnp.mean(stream * stream, axis=1, keepdims=True)
    normed_ref[:, :width] = (stream * lax.rsqrt(meansq + norm_eps) * gain_ref[...]).astype(
        jnp.bfloat16
    )
    normed_ref[:, width:] = info_ref[...]


def experts_kernel(experts, capacity, tile, expert_ref, *refs):
    n_in = len(refs) - 10
    rows_in = refs[:n_in]
    gate_hbm, up_hbm, down_hbm, out_ref = refs[n_in : n_in + 4]
    rows_ref, gate_ref, up_ref, down_ref, gate_sem, down_sem = refs[n_in + 4 :]
    width = gate_hbm.shape[0]
    hidden_all = gate_hbm.shape[1]
    per_expert = hidden_all // experts
    steps = hidden_all // tile
    copies = []
    for s in range(steps):
        cut = pl.ds(s * tile, tile)
        trio = (
            pltpu.make_async_copy(gate_hbm.at[:, cut], gate_ref.at[s], gate_sem.at[s, 0]),
            pltpu.make_async_copy(up_hbm.at[:, cut], up_ref.at[s], gate_sem.at[s, 1]),
            pltpu.make_async_copy(down_hbm.at[cut, :], down_ref.at[s], down_sem.at[s]),
        )
        for c in trio:
            c.start()
        copies.append(trio)
    start = 0
    for r in rows_in:
        rows_ref[start : start + r.shape[0], :] = r[...]
        start += r.shape[0]
    count = start
    at0 = lax.broadcasted_iota(jnp.int32, (count, count), 0)
    at1 = lax.broadcasted_iota(jnp.int32, (count, count), 1)
    eye = (at0 == at1).astype(jnp.bfloat16)
    before = (at0 < at1).astype(jnp.bfloat16)
    info = lax.dot_general(
        rows_ref[:, width:], eye, (((0,), (0,)), ((), ())), preferred_element_type=jnp.float32
    )
    id0, id1, code0, code1 = (info[i : i + 1, :] for i in range(4))
    slot_of = lax.broadcasted_iota(jnp.int32, (capacity, count), 0).astype(jnp.float32)
    picks, shares, packed = [], [], []
    for x in range(experts):
        e = (expert_ref[0] + x).astype(jnp.float32)
        hit0 = jnp.where(id0 == e, 1.0, 0.0)
        hit1 = jnp.where(id1 == e, 1.0, 0.0)
        member = hit0 + hit1
        share = (hit0 * code0 + hit1 * code1) / (code0 + code1)
        slot = dot(jnp.broadcast_to(member, (8, count)).astype(jnp.bfloat16), before)[:1]
        slot = jnp.where(member > 0.5, slot, -1.0)
        pick = slot == slot_of
        shares.append(jnp.sum(jnp.where(pick, share, 0.0), axis=1, keepdims=True))
        pick = jnp.where(pick, 1.0, 0.0).astype(jnp.bfloat16)
        picks.append(pick)
        packed.append(dot(pick, rows_ref[:, :width]).astype(jnp.bfloat16))
    total = None
    for x in range(experts):
        acc = None
        for s in range(x * steps // experts, (x + 1) * steps // experts):
            gate_copy, up_copy, down_copy = copies[s]
            gate_copy.wait()
            gate = dot(packed[x], gate_ref[s])
            up_copy.wait()
            up = dot(packed[x], up_ref[s])
            hidden = (gate / (1.0 + jnp.exp(-gate)) * up).astype(jnp.bfloat16)
            down_copy.wait()
            part = dot(hidden, down_ref[s])
            acc = part if acc is None else acc + part
        weighted = (acc * shares[x]).astype(jnp.bfloat16)
        spread = lax.dot_general(
            picks[x], weighted, (((0,), (0,)), ((), ())), preferred_element_type=jnp.float32
        )
        total = spread if total is None else total + spread
    out_ref[...] = total.astype(jnp.bfloat16)


def per_device(
    query,
    keys,
    values,
    residual,
    out_weight,
    norm_gain,
    expert_ids,
    gate_codes,
    doc_lengths,
    w_gate,
    w_up,
    w_down,
):
    block, width = residual.shape
    head = HEAD_DIMENSION
    group_width = QUERY_HEAD_COUNT // KEY_VALUE_HEADS
    q_heads = query.shape[1] // head
    sec_count, tp_count, pp_count = (lax.axis_size(a) for a in ("sec", "tp", "pp"))
    sec_index = lax.axis_index("sec")
    pp_index = lax.axis_index("pp")
    ranks = tp_count * pp_count
    rank = lax.axis_index("tp") * pp_count + pp_index
    own_rows = block // ranks

    kv_heads = max(1, q_heads // group_width)
    group = q_heads // kv_heads
    kv_start = pp_index * q_heads // group_width * head
    kv = jnp.concatenate(
        [lax.dynamic_slice_in_dim(a, kv_start, kv_heads * head, 1) for a in (keys, values)], axis=1
    )
    back = -(-(sec_count * block // 2 - 1) // block)
    pieces = [
        lax.ppermute(kv, "sec", [(i, i + k) for i in range(sec_count - k)])
        for k in range(back, 0, -1)
    ] + [kv]
    vmem = 40 * 2**20
    partial = pl.pallas_call(
        functools.partial(attention_kernel, back, kv_heads, group),
        out_shape=jax.ShapeDtypeStruct((block, width), jnp.bfloat16),
        in_specs=[SMEM, SMEM, VMEM] + [VMEM] * (back + 1) + [ANY],
        out_specs=VMEM,
        scratch_shapes=[
            pltpu.VMEM(out_weight.shape, jnp.bfloat16),
            pltpu.VMEM(query.shape, jnp.bfloat16),
            pltpu.SemaphoreType.DMA,
        ],
        compiler_params=pltpu.CompilerParams(vmem_limit_bytes=vmem),
        name="attention",
    )(doc_lengths, sec_index.reshape(1), query, *pieces, out_weight)

    def rows_of(x, r):
        return lax.dynamic_slice_in_dim(x, r * own_rows, own_rows, 0)

    parts = [rows_of(partial, rank)] + [
        xor_swap(rows_of(partial, rank ^ k), ("tp", "pp"), k) for k in range(1, ranks)
    ]
    info = jnp.concatenate([expert_ids, gate_codes], axis=1).astype(jnp.bfloat16)
    info = jnp.pad(rows_of(info, rank), ((0, 0), (0, LANES - info.shape[1])))
    stream, normed = pl.pallas_call(
        functools.partial(norm_kernel, ranks),
        out_shape=(
            jax.ShapeDtypeStruct((own_rows, width), jnp.float32),
            jax.ShapeDtypeStruct((own_rows, width + LANES), jnp.bfloat16),
        ),
        in_specs=[VMEM] * (3 + ranks),
        out_specs=(VMEM, VMEM),
        compiler_params=pltpu.CompilerParams(vmem_limit_bytes=vmem),
        name="norm",
    )(rows_of(residual, rank), norm_gain.reshape(1, width), info, *parts)

    rows = jnp.concatenate(
        [normed] + [xor_swap(normed, "sec", k) for k in range(1, sec_count)], axis=0
    )
    rows = jnp.concatenate([rows] + [xor_swap(rows, "tp", k) for k in range(1, tp_count)], axis=0)
    rows = [rows] + [xor_swap(rows, "pp", k) for k in range(1, pp_count)]

    experts = max(1, E // sec_count)
    halves = max(1, sec_count // E)
    count = sec_count * block
    capacity = sec_count * MOSTB
    hidden_all = w_gate.shape[2]
    tile = min(512, hidden_all // experts)
    steps = hidden_all // tile
    first_expert = (sec_index * experts if halves == 1 else sec_index // halves).reshape(1)
    out = pl.pallas_call(
        functools.partial(experts_kernel, experts, capacity, tile),
        out_shape=jax.ShapeDtypeStruct((count, width), jnp.bfloat16),
        in_specs=[SMEM] + [VMEM] * len(rows) + [ANY] * 3,
        out_specs=VMEM,
        scratch_shapes=[
            pltpu.VMEM((count, width + LANES), jnp.bfloat16),
            pltpu.VMEM((steps, width, tile), jnp.bfloat16),
            pltpu.VMEM((steps, width, tile), jnp.bfloat16),
            pltpu.VMEM((steps, tile, width), jnp.bfloat16),
            pltpu.SemaphoreType.DMA((steps, 2)),
            pltpu.SemaphoreType.DMA((steps,)),
        ],
        compiler_params=pltpu.CompilerParams(vmem_limit_bytes=60 * 2**20),
        name="experts",
    )(first_expert, *rows, w_gate[0], w_up[0], w_down[0])

    def sum_swapped(x, axis):
        n = lax.axis_size(axis)
        x = x.reshape((n, -1) + x.shape[1:])
        total = x[0].astype(jnp.float32)
        for k in range(1, n):
            total = total + xor_swap(x[k], axis, k).astype(jnp.float32)
        return total

    out = sum_swapped(out, "pp").astype(jnp.bfloat16)
    out = sum_swapped(out, "tp").astype(jnp.bfloat16)
    return (stream + sum_swapped(out, "sec")).astype(jnp.bfloat16)


def solution(mesh):
    in_specs = (
        P(("groups", "sec"), ("tp", "pp")),
        P(("groups", "sec"), "tp"),
        P(("groups", "sec"), "tp"),
        P(("groups", "sec"), None),
        P(("tp", "pp"), None),
        P(),
        P(("groups", "sec"), None),
        P(("groups", "sec"), None),
        P("groups"),
        P(("tp", "pp"), None, "sec"),
        P(("tp", "pp"), None, "sec"),
        P(("tp", "pp"), "sec", None),
    )
    out_specs = P(("groups", "sec", "tp", "pp"), None)
    return jax.shard_map(
        per_device, mesh=mesh, in_specs=in_specs, out_specs=out_specs, check_vma=False
    )
```

```python
import functools

import jax
import jax.numpy as jnp
from jax import lax
from jax.experimental import pallas as pl
from jax.experimental.pallas import tpu as pltpu
from jax.sharding import PartitionSpec as P

QUERY_HEAD_COUNT = 32
KEY_VALUE_HEADS = 8
HEAD_DIMENSION = 128
E = 8
MOSTB = 32
LANES = 128

neg_fill = -1e30
norm_eps = 1e-05

VMEM = pl.BlockSpec(memory_space=pltpu.VMEM)
SMEM = pl.BlockSpec(memory_space=pltpu.SMEM)
HBM = pl.BlockSpec(memory_space=pltpu.HBM)
ANY = pl.BlockSpec(memory_space=pl.ANY)
MIB = 2**20


def dot(a, b):
    return jnp.dot(a, b, preferred_element_type=jnp.float32)


def xor_swap(x, axis, k):
    n = lax.axis_size(axis)
    return lax.ppermute(x, axis, [(i, i ^ k) for i in range(n)])


def call(kernel, out_shape, args, scratch=(), vmem=8, name=None, cost_us=1.0):
    args = [
        (s, pltpu.with_memory_space_constraint(a, pltpu.HBM) if s is HBM else a) for s, a in args
    ]
    single = not isinstance(out_shape, (tuple, list))
    return pl.pallas_call(
        kernel,
        out_shape=out_shape,
        in_specs=[s for s, _ in args],
        out_specs=VMEM if single else [VMEM] * len(out_shape),
        scratch_shapes=list(scratch),
        compiler_params=pltpu.CompilerParams(vmem_limit_bytes=vmem * MIB),
        cost_estimate=pl.CostEstimate(
            flops=0, bytes_accessed=int(cost_us * 3.4e6), transcendentals=0
        ),
        name=name,
    )(*[a for _, a in args])


def sds(shape, dtype):
    return jax.ShapeDtypeStruct(shape, dtype)


def position():
    rank = lax.axis_index("tp") * lax.axis_size("pp") + lax.axis_index("pp")
    return lax.axis_index("sec"), rank


def columns(source, targets, first=0):
    per = targets[0].shape[1] if targets else 0
    return [(source.at[:, pl.ds((first + i) * per, per)], t) for i, t in enumerate(targets)]


def prepare_kernel(
    back, tp_count, pp_count, lengths_hbm, ids_hbm, codes_hbm, query_hbm, weight_hbm, residual_hbm,
    gain_hbm, *refs
):
    gate_hbm, query_ref, weight_ref, gain_ref, mask_ref, order_ref, residual_ref, info_ref = refs[
        :8
    ]
    gate_refs = refs[8:-5]
    lengths, ids, codes, residual_all, sem = refs[-5:]
    pairs = [
        (lengths_hbm, lengths),
        (ids_hbm, ids),
        (codes_hbm, codes),
        (residual_hbm, residual_all),
        (query_hbm, query_ref),
        (gain_hbm, gain_ref),
        (weight_hbm, weight_ref),
    ] + columns(gate_hbm, gate_refs)
    copies = [pltpu.make_async_copy(a, b, sem.at[i]) for i, (a, b) in enumerate(pairs)]
    for c in copies:
        c.start()
    sec, rank = position()
    block = query_ref.shape[0]
    own_rows = residual_ref.shape[0]
    at = lax.broadcasted_iota(jnp.int32, (block, block), 0)
    to = lax.broadcasted_iota(jnp.int32, (block, block), 1)
    chunk = lax.div(at, own_rows)
    flip = lax.rem(chunk, tp_count) * pp_count + lax.div(chunk, tp_count)
    source = (rank ^ flip) * own_rows + lax.rem(at, own_rows)
    order_ref[...] = jnp.where(to == source, 1.0, 0.0).astype(jnp.bfloat16)
    own = lax.broadcasted_iota(jnp.int32, (own_rows, block), 0) + rank * own_rows
    own = jnp.where(own == lax.broadcasted_iota(jnp.int32, (own_rows, block), 1), 1.0, 0.0)
    own = own.astype(jnp.bfloat16)
    for c in copies[:4]:
        c.wait()
    span = (back + 1) * block
    rows = sec * block + lax.broadcasted_iota(jnp.int32, (block, span), 0)
    cols = (sec - back) * block + lax.broadcasted_iota(jnp.int32, (block, span), 1)
    first = jnp.zeros((block, span), jnp.int32)
    end = jnp.int32(0)
    for d in range(lengths.shape[0]):
        end = end + lengths[d]
        first = jnp.where(rows >= end, end, first)
    mask_ref[...] = jnp.where((cols <= rows) & (cols >= first), 1.0, 0.0)
    residual_ref[...] = dot(own, residual_all[...])
    info = jnp.concatenate(
        [ids[...], codes[...], jnp.zeros((LANES - 4, block), jnp.int32)], axis=0
    ).astype(jnp.float32)
    info_ref[...] = lax.dot_general(
        own, info.astype(jnp.bfloat16), (((1,), (1,)), ((), ())), preferred_element_type=jnp.float32
    ).astype(jnp.bfloat16)
    for c in copies[4:]:
        c.wait()


def load_kernel(n_after, source, *refs):
    *targets, token_ref, sem = refs[n_after:]
    copies = [
        pltpu.make_async_copy(a, b, sem.at[i])
        for i, (a, b) in enumerate(columns(source, targets))
    ]
    for c in copies:
        c.start()
    token_ref[...] = jnp.zeros_like(token_ref)
    for c in copies:
        c.wait()


def load(array, parts, wanted, after, name):
    rows, cols = array.shape
    out = call(
        functools.partial(load_kernel, len(after)),
        [sds((rows, cols // parts), array.dtype)] * wanted + [sds((8, LANES), jnp.float32)],
        [(HBM, array)] + [(ANY, a) for a in after],
        scratch=[pltpu.SemaphoreType.DMA((wanted,))],
        vmem=1,
        name=name,
        cost_us=array.size * wanted / parts * 2 / 3.4e6,
    )
    return out[:-1], out[-1]


def attention_kernel(back, kv_heads, group, q_ref, mask_ref, order_ref, *refs):
    kv_refs = refs[: back + 1]
    weight_ref, keep_ref, send_ref, attended_ref = refs[back + 1 :]
    block = q_ref.shape[0]
    head = HEAD_DIMENSION
    allowed = jnp.concatenate([mask_ref[...]] * group, axis=0) > 0.5
    for g in range(kv_heads):
        q = jnp.concatenate(
            [q_ref[:, (g * group + t) * head : (g * group + t + 1) * head] for t in range(group)],
            axis=0,
        )
        k = jnp.concatenate([r[:, g * head : (g + 1) * head] for r in kv_refs], axis=0)
        v = jnp.concatenate(
            [r[:, (kv_heads + g) * head : (kv_heads + g + 1) * head] for r in kv_refs], axis=0
        )
        scores = lax.dot_general(
            q, k, (((1,), (1,)), ((), ())), preferred_element_type=jnp.float32
        ) * (head**-0.5)
        scores = jnp.where(allowed, scores, neg_fill)
        top = jnp.max(scores, axis=1, keepdims=True)
        weights = jnp.where(allowed, jnp.exp(scores - top), 0.0)
        total = jnp.sum(weights, axis=1, keepdims=True)
        summed = dot(weights.astype(jnp.bfloat16), v) / total
        for t in range(group):
            attended_ref[:, (g * group + t) * head : (g * group + t + 1) * head] = summed[
                t * block : (t + 1) * block
            ].astype(jnp.bfloat16)
    attended = dot(order_ref[...], attended_ref[...]).astype(jnp.bfloat16)
    mixed = dot(attended, weight_ref[...])
    kept = keep_ref.shape[0]
    keep_ref[...] = mixed[:kept]
    send_ref[...] = mixed[kept:].astype(jnp.bfloat16)


def add_kernel(keep_rows, n_in, *refs):
    total = refs[0][...].astype(jnp.float32)
    for r in refs[1:n_in]:
        total = total + r[...].astype(jnp.float32)
    start = 0
    for r in refs[n_in:]:
        r[...] = total[start : start + r.shape[0]].astype(r.dtype)
        start += r.shape[0]


def add(arrays, keep, send, name):
    width = arrays[0].shape[1]
    out = [sds((r, width), jnp.float32) for r in keep]
    out += [sds((r, width), jnp.bfloat16) for r in send]
    out = call(
        functools.partial(add_kernel, sum(keep), len(arrays)),
        out,
        [(VMEM, a) for a in arrays],
        name=name,
        cost_us=0.2,
    )
    return out[: len(keep)], out[len(keep) :]


def norm_kernel(n_parts, residual_ref, gain_ref, info_ref, *refs):
    parts = refs[:n_parts]
    stream_ref, normed_ref = refs[-2:]
    width = residual_ref.shape[1]
    mixed = parts[0][...].astype(jnp.float32)
    for p in parts[1:]:
        mixed = mixed + p[...].astype(jnp.float32)
    stream = residual_ref[...] + mixed
    stream_ref[...] = stream
    meansq = jnp.mean(stream * stream, axis=1, keepdims=True)
    normed_ref[:, :width] = (stream * lax.rsqrt(meansq + norm_eps) * gain_ref[...]).astype(
        jnp.bfloat16
    )
    normed_ref[:, width:] = info_ref[...]


def experts_kernel(experts, capacity, tile, halves, n_rows, n_gate, n_up, *refs):
    rows_in = refs[:n_rows]
    gate_refs = list(refs[n_rows : n_rows + n_gate])
    up_refs = list(refs[n_rows + n_gate : n_rows + n_gate + n_up])
    refs = refs[n_rows + n_gate + n_up :]
    up_hbm, down_hbm, keep_ref, send_ref, rows_ref, pick_ref, packed_ref, hidden_ref = refs[:8]
    up_late = list(refs[8 : 8 + experts - n_up])
    down_ref, up_sem, down_sem = refs[8 + experts - n_up :]
    per_expert, width = down_hbm.shape[0] // experts, down_hbm.shape[1]
    up_copies = [
        pltpu.make_async_copy(a, b, up_sem.at[i])
        for i, (a, b) in enumerate(columns(up_hbm, up_late, n_up))
    ]
    up_refs += up_late
    down_copies = [
        pltpu.make_async_copy(
            down_hbm.at[pl.ds(x * per_expert, per_expert)], down_ref, down_sem.at[x]
        )
        for x in range(experts)
    ]
    for c in down_copies[:1] + up_copies:
        c.start()
    count = 0
    for r in rows_in:
        rows_ref[count : count + r.shape[0], :] = r[...]
        count += r.shape[0]
    at0 = lax.broadcasted_iota(jnp.int32, (count, count), 0)
    at1 = lax.broadcasted_iota(jnp.int32, (count, count), 1)
    eye = jnp.where(at0 == at1, 1.0, 0.0).astype(jnp.bfloat16)
    before = jnp.where(at0 < at1, 1.0, 0.0).astype(jnp.bfloat16)
    info = lax.dot_general(
        rows_ref[:, width:], eye, (((0,), (0,)), ((), ())), preferred_element_type=jnp.float32
    )
    id0, id1, code0, code1 = (info[i : i + 1, :] for i in range(4))
    slot_of = lax.broadcasted_iota(jnp.int32, (capacity, count), 0).astype(jnp.float32)
    first = lax.axis_index("sec") * experts if halves == 1 else lax.axis_index("sec") // halves
    picks, shares = [], []
    for x in range(experts):
        e = (first + x).astype(jnp.float32)
        hit0 = jnp.where(id0 == e, 1.0, 0.0)
        hit1 = jnp.where(id1 == e, 1.0, 0.0)
        member = hit0 + hit1
        share = (hit0 * code0 + hit1 * code1) / (code0 + code1)
        slot = dot(jnp.broadcast_to(member, (8, count)).astype(jnp.bfloat16), before)[:1]
        slot = jnp.where(member > 0.5, slot, -1.0)
        pick = slot == slot_of
        shares.append(jnp.sum(jnp.where(pick, share, 0.0), axis=1, keepdims=True))
        picks.append(jnp.where(pick, 1.0, 0.0).astype(jnp.bfloat16))
    pick_ref[...] = jnp.concatenate(picks, axis=0)
    column = min(512, width)

    def pack(c, _):
        cut = pl.ds(pl.multiple_of(c * column, column), column)
        packed_ref[:, cut] = dot(pick_ref[...], rows_ref[:, cut]).astype(jnp.bfloat16)
        return 0

    lax.fori_loop(0, width // column, pack, 0)
    for x in range(experts):
        mine = slice(x * capacity, (x + 1) * capacity)
        if x >= n_up:
            up_copies[x - n_up].wait()
        gate_ref, up_ref = gate_refs[x], up_refs[x]

        def inner(s, _):
            cut = pl.ds(pl.multiple_of(s * tile, tile), tile)
            gate = dot(packed_ref[mine, :], gate_ref[:, cut])
            up = dot(packed_ref[mine, :], up_ref[:, cut])
            hidden_ref[mine, cut] = (gate / (1.0 + jnp.exp(-gate)) * up).astype(jnp.bfloat16)
            return 0

        lax.fori_loop(0, per_expert // tile, inner, 0)
        down_copies[x].wait()

        def outer(c, _):
            cut = pl.ds(pl.multiple_of(c * column, column), column)
            out = dot(hidden_ref[mine, :], down_ref[:, cut])
            packed_ref[mine, cut] = (out * shares[x]).astype(jnp.bfloat16)
            return 0

        lax.fori_loop(0, width // column, outer, 0)
        if x + 1 < experts:
            down_copies[x + 1].start()
    kept = keep_ref.shape[0]

    def spread(c, _):
        cut = pl.ds(pl.multiple_of(c * column, column), column)
        out = lax.dot_general(
            pick_ref[...], packed_ref[:, cut], (((0,), (0,)), ((), ())),
            preferred_element_type=jnp.float32,
        )
        keep_ref[:, cut] = out[:kept]
        send_ref[:, cut] = out[kept:].astype(jnp.bfloat16)
        return 0

    lax.fori_loop(0, width // column, spread, 0)


def per_device(
    query,
    keys,
    values,
    residual,
    out_weight,
    norm_gain,
    expert_ids,
    gate_codes,
    doc_lengths,
    w_gate,
    w_up,
    w_down,
):
    block, width = residual.shape
    head = HEAD_DIMENSION
    group_width = QUERY_HEAD_COUNT // KEY_VALUE_HEADS
    q_heads = query.shape[1] // head
    sec_count, tp_count, pp_count = (lax.axis_size(a) for a in ("sec", "tp", "pp"))
    own_rows = block // (tp_count * pp_count)
    bf16, f32 = jnp.bfloat16, jnp.float32

    kv_heads = max(1, q_heads // group_width)
    group = q_heads // kv_heads
    kv_start = lax.axis_index("pp") * q_heads // group_width * head
    kv = jnp.concatenate(
        [lax.dynamic_slice_in_dim(a, kv_start, kv_heads * head, 1) for a in (keys, values)], axis=1
    )
    back = -(-(sec_count * block // 2 - 1) // block)
    pieces = [
        lax.ppermute(kv, "sec", [(i, i + k) for i in range(sec_count - k)])
        for k in range(back, 0, -1)
    ] + [kv]

    experts = max(1, E // sec_count)
    per_expert = w_gate.shape[2] // experts
    span = (back + 1) * block
    query_v, weight_v, gain_v, mask, order, residual_own, info, *gate_v = call(
        functools.partial(prepare_kernel, back, tp_count, pp_count),
        [
            sds(query.shape, bf16),
            sds(out_weight.shape, bf16),
            sds((1, width), f32),
            sds((block, span), f32),
            sds((block, block), bf16),
            sds((own_rows, width), f32),
            sds((own_rows, LANES), bf16),
        ]
        + [sds((width, per_expert), bf16)] * experts,
        [
            (HBM, a)
            for a in (
                doc_lengths, expert_ids.T, gate_codes.T, query, out_weight, residual,
                norm_gain.reshape(1, width), w_gate[0],
            )
        ],
        scratch=[
            pltpu.SMEM(doc_lengths.shape, jnp.int32),
            pltpu.VMEM((2, block), jnp.int32),
            pltpu.VMEM((2, block), jnp.int32),
            pltpu.VMEM(residual.shape, bf16),
            pltpu.SemaphoreType.DMA((7 + experts,)),
        ],
        vmem=6,
        name="prepare",
        cost_us=6.0,
    )
    half = block // pp_count
    keep, send = call(
        functools.partial(attention_kernel, back, kv_heads, group),
        [sds((half, width), f32), sds((block - half, width), bf16)],
        [(VMEM, a) for a in (query_v, mask, order, *pieces, weight_v)],
        scratch=[pltpu.VMEM(query.shape, bf16)],
        name="attention",
        cost_us=2.4,
    )

    (own,), sends = add(
        [keep] + [xor_swap(send, "pp", 1)], [own_rows], [own_rows] * (tp_count - 1), "sum_cores"
    )
    got = [xor_swap(sends[k - 1], "tp", k) for k in range(1, tp_count)]
    up_v, token = load(w_up[0], experts, 1, [own], "load_up")
    stream, normed = call(
        functools.partial(norm_kernel, tp_count),
        [sds((own_rows, width), f32), sds((own_rows, width + LANES), bf16)],
        [(VMEM, a) for a in (residual_own, gain_v, info, own, *got)] + [(ANY, token)],
        name="norm",
        cost_us=0.2,
    )

    groups = min(4, sec_count)
    near = [normed] + [xor_swap(normed, "sec", k) for k in range(1, sec_count)]
    per_group = sec_count // groups
    near = [
        jnp.concatenate(near[g * per_group : (g + 1) * per_group], axis=0)
        if per_group > 1
        else near[g]
        for g in range(groups)
    ]
    rows = [[r] + [xor_swap(r, "tp", k) for k in range(1, tp_count)] for r in near]
    rows = [rows[g][k] for k in range(tp_count) for g in range(groups)]
    rows = rows + [xor_swap(r, "pp", k) for k in range(1, pp_count) for r in rows]

    halves = max(1, sec_count // E)
    count = sec_count * block
    capacity = sec_count * MOSTB
    down = w_down[0]
    tile = min(512, down.shape[0] // experts)
    kept = count // pp_count
    keep, send = call(
        functools.partial(experts_kernel, experts, capacity, tile, halves, len(rows), experts, 1),
        [sds((kept, width), f32), sds((count - kept, width), bf16)],
        [(VMEM, a) for a in (*rows, *gate_v, *up_v)] + [(HBM, w_up[0]), (HBM, down)],
        scratch=[
            pltpu.VMEM((count, width + LANES), bf16),
            pltpu.VMEM((experts * capacity, count), bf16),
            pltpu.VMEM((experts * capacity, width), bf16),
            pltpu.VMEM((experts * capacity, down.shape[0] // experts), bf16),
            *[pltpu.VMEM((width, per_expert), bf16)] * (experts - 1),
            pltpu.VMEM((per_expert, width), bf16),
            pltpu.SemaphoreType.DMA((experts,)),
            pltpu.SemaphoreType.DMA((experts,)),
        ],
        vmem=20,
        name="experts",
        cost_us=12.0,
    )

    piece = kept // (tp_count * groups)
    own, sends = add(
        [keep, xor_swap(send, "pp", 1)], [piece] * groups, [piece] * (groups * (tp_count - 1)), "sum_cores2"
    )
    final = [stream]
    for g in list(range(1, groups)) + [0]:
        got = [xor_swap(sends[(k - 1) * groups + g], "tp", k) for k in range(1, tp_count)]
        if g == 0 and per_group == 1:
            final += [own[0]] + got
            continue
        kept_rows = own_rows if g == 0 else 0
        mine, out = add(
            [own[g]] + got,
            [own_rows] if g == 0 else [],
            [own_rows] * (per_group - (g == 0)),
            "sum_x%d" % g,
        )
        final += list(mine)
        for j, o in enumerate(out):
            final.append(xor_swap(o, "sec", g * per_group + j + (g == 0)))
    return call(
        functools.partial(add_kernel, 0, len(final)),
        [sds((own_rows, width), bf16)],
        [(VMEM, a) for a in final],
        name="total",
        cost_us=0.2,
    )[0]


def solution(mesh):
    in_specs = (
        P(("groups", "sec"), ("tp", "pp")),
        P(("groups", "sec"), "tp"),
        P(("groups", "sec"), "tp"),
        P(("groups", "sec"), None),
        P(("tp", "pp"), None),
        P(),
        P(("groups", "sec"), None),
        P(("groups", "sec"), None),
        P("groups"),
        P(("tp", "pp"), None, "sec"),
        P(("tp", "pp"), None, "sec"),
        P(("tp", "pp"), "sec", None),
    )
    out_specs = P(("groups", "sec", "tp", "pp"), None)
    return jax.shard_map(
        per_device, mesh=mesh, in_specs=in_specs, out_specs=out_specs, check_vma=False
    )
```

```python
import functools

import jax
import jax.numpy as jnp
from jax import lax
from jax.experimental import pallas as pl
from jax.experimental.pallas import tpu as pltpu
from jax.sharding import PartitionSpec as P

QUERY_HEAD_COUNT = 32
KEY_VALUE_HEADS = 8
HEAD_DIMENSION = 128
E = 8
MOSTB = 32
LANES = 128

neg_fill = -1e30
norm_eps = 1e-05

VMEM = pl.BlockSpec(memory_space=pltpu.VMEM)
SMEM = pl.BlockSpec(memory_space=pltpu.SMEM)
HBM = pl.BlockSpec(memory_space=pltpu.HBM)
ANY = pl.BlockSpec(memory_space=pl.ANY)
MIB = 2**20


def dot(a, b):
    return jnp.dot(a, b, preferred_element_type=jnp.float32)


def xor_swap(x, axis, k):
    n = lax.axis_size(axis)
    return lax.ppermute(x, axis, [(i, i ^ k) for i in range(n)])


def call(kernel, out_shape, args, scratch=(), vmem=8, name=None, cost_us=1.0):
    args = [
        (s, pltpu.with_memory_space_constraint(a, pltpu.HBM) if s is HBM else a) for s, a in args
    ]
    single = not isinstance(out_shape, (tuple, list))
    return pl.pallas_call(
        kernel,
        out_shape=out_shape,
        in_specs=[s for s, _ in args],
        out_specs=VMEM if single else [VMEM] * len(out_shape),
        scratch_shapes=list(scratch),
        compiler_params=pltpu.CompilerParams(vmem_limit_bytes=vmem * MIB),
        cost_estimate=pl.CostEstimate(
            flops=0, bytes_accessed=int(cost_us * 3.4e6), transcendentals=0
        ),
        name=name,
    )(*[a for _, a in args])


def sds(shape, dtype):
    return jax.ShapeDtypeStruct(shape, dtype)


def position():
    rank = lax.axis_index("tp") * lax.axis_size("pp") + lax.axis_index("pp")
    return lax.axis_index("sec"), rank


def columns(source, targets, first=0):
    per = targets[0].shape[1] if targets else 0
    return [(source.at[:, pl.ds((first + i) * per, per)], t) for i, t in enumerate(targets)]


def prepare_kernel(
    back, tp_count, pp_count, lengths_hbm, ids_hbm, codes_hbm, query_hbm, weight_hbm, residual_hbm,
    gain_hbm, *refs
):
    query_ref, weight_ref, gain_ref, mask_ref, order_ref, residual_ref, info_ref = refs[:7]
    lengths, ids, codes, residual_all, sem = refs[7:]
    pairs = [
        (lengths_hbm, lengths),
        (ids_hbm, ids),
        (codes_hbm, codes),
        (residual_hbm, residual_all),
        (query_hbm, query_ref),
        (gain_hbm, gain_ref),
        (weight_hbm, weight_ref),
    ]
    copies = [pltpu.make_async_copy(a, b, sem.at[i]) for i, (a, b) in enumerate(pairs)]
    for c in copies:
        c.start()
    sec, rank = position()
    block = query_ref.shape[0]
    own_rows = residual_ref.shape[0]
    at = lax.broadcasted_iota(jnp.int32, (block, block), 0)
    to = lax.broadcasted_iota(jnp.int32, (block, block), 1)
    chunk = lax.div(at, own_rows)
    flip = lax.rem(chunk, tp_count) * pp_count + lax.div(chunk, tp_count)
    source = (rank ^ flip) * own_rows + lax.rem(at, own_rows)
    order_ref[...] = jnp.where(to == source, 1.0, 0.0).astype(jnp.bfloat16)
    own = lax.broadcasted_iota(jnp.int32, (own_rows, block), 0) + rank * own_rows
    own = jnp.where(own == lax.broadcasted_iota(jnp.int32, (own_rows, block), 1), 1.0, 0.0)
    own = own.astype(jnp.bfloat16)
    for c in copies[:4]:
        c.wait()
    span = (back + 1) * block
    rows = sec * block + lax.broadcasted_iota(jnp.int32, (block, span), 0)
    cols = (sec - back) * block + lax.broadcasted_iota(jnp.int32, (block, span), 1)
    first = jnp.zeros((block, span), jnp.int32)
    end = jnp.int32(0)
    for d in range(lengths.shape[0]):
        end = end + lengths[d]
        first = jnp.where(rows >= end, end, first)
    mask_ref[...] = jnp.where((cols <= rows) & (cols >= first), 1.0, 0.0)
    residual_ref[...] = dot(own, residual_all[...])
    info = jnp.concatenate(
        [ids[...], codes[...], jnp.zeros((LANES - 4, block), jnp.int32)], axis=0
    ).astype(jnp.float32)
    info_ref[...] = lax.dot_general(
        own, info.astype(jnp.bfloat16), (((1,), (1,)), ((), ())), preferred_element_type=jnp.float32
    ).astype(jnp.bfloat16)
    for c in copies[4:]:
        c.wait()


def load_kernel(first, n_after, source, *refs):
    target, sem = refs[n_after:]
    copy = pltpu.make_async_copy(
        source.at[:, pl.ds(first, target.shape[1])], target, sem
    )
    copy.start()
    copy.wait()


def load(array, first, columns, after, name):
    rows = array.shape[0]
    return call(
        functools.partial(load_kernel, first, len(after)),
        sds((rows, columns), array.dtype),
        [(HBM, array)] + [(ANY, a) for a in after],
        scratch=[pltpu.SemaphoreType.DMA],
        vmem=1,
        name=name,
        cost_us=rows * columns * 2 / 3.4e6,
    )


def join_kernel(n, n_after, *refs):
    start = 0
    for r in refs[:n]:
        refs[n + n_after][start : start + r.shape[0], :] = r[...]
        start += r.shape[0]


def join(arrays, after, name):
    rows = sum(a.shape[0] for a in arrays)
    return call(
        functools.partial(join_kernel, len(arrays), len(after)),
        sds((rows, arrays[0].shape[1]), arrays[0].dtype),
        [(VMEM, a) for a in arrays] + [(ANY, a) for a in after],
        name=name,
        cost_us=0.1,
    )


def attention_kernel(back, kv_heads, group, q_ref, mask_ref, order_ref, *refs):
    kv_refs = refs[: back + 1]
    weight_ref, keep_ref, send_ref, attended_ref = refs[back + 1 :]
    block = q_ref.shape[0]
    head = HEAD_DIMENSION
    allowed = jnp.concatenate([mask_ref[...]] * group, axis=0) > 0.5
    for g in range(kv_heads):
        q = jnp.concatenate(
            [q_ref[:, (g * group + t) * head : (g * group + t + 1) * head] for t in range(group)],
            axis=0,
        )
        k = jnp.concatenate([r[:, g * head : (g + 1) * head] for r in kv_refs], axis=0)
        v = jnp.concatenate(
            [r[:, (kv_heads + g) * head : (kv_heads + g + 1) * head] for r in kv_refs], axis=0
        )
        scores = lax.dot_general(
            q, k, (((1,), (1,)), ((), ())), preferred_element_type=jnp.float32
        ) * (head**-0.5)
        scores = jnp.where(allowed, scores, neg_fill)
        top = jnp.max(scores, axis=1, keepdims=True)
        weights = jnp.where(allowed, jnp.exp(scores - top), 0.0)
        total = jnp.sum(weights, axis=1, keepdims=True)
        summed = dot(weights.astype(jnp.bfloat16), v) / total
        for t in range(group):
            attended_ref[:, (g * group + t) * head : (g * group + t + 1) * head] = summed[
                t * block : (t + 1) * block
            ].astype(jnp.bfloat16)
    attended = dot(order_ref[...], attended_ref[...]).astype(jnp.bfloat16)
    mixed = dot(attended, weight_ref[...])
    kept = keep_ref.shape[0]
    keep_ref[...] = mixed[:kept]
    send_ref[...] = mixed[kept:].astype(jnp.bfloat16)


def add_kernel(keep_rows, n_in, *refs):
    total = refs[0][...].astype(jnp.float32)
    for r in refs[1:n_in]:
        total = total + r[...].astype(jnp.float32)
    start = 0
    for r in refs[n_in:]:
        r[...] = total[start : start + r.shape[0]].astype(r.dtype)
        start += r.shape[0]


def add(arrays, keep, send, name):
    width = arrays[0].shape[1]
    out = [sds((r, width), jnp.float32) for r in keep]
    out += [sds((r, width), jnp.bfloat16) for r in send]
    out = call(
        functools.partial(add_kernel, sum(keep), len(arrays)),
        out,
        [(VMEM, a) for a in arrays],
        name=name,
        cost_us=0.2,
    )
    return out[: len(keep)], out[len(keep) :]


def norm_kernel(n_parts, residual_ref, gain_ref, info_ref, *refs):
    parts = refs[:n_parts]
    stream_ref, normed_ref = refs[-2:]
    width = residual_ref.shape[1]
    mixed = parts[0][...].astype(jnp.float32)
    for p in parts[1:]:
        mixed = mixed + p[...].astype(jnp.float32)
    stream = residual_ref[...] + mixed
    stream_ref[...] = stream
    meansq = jnp.mean(stream * stream, axis=1, keepdims=True)
    normed_ref[:, :width] = (stream * lax.rsqrt(meansq + norm_eps) * gain_ref[...]).astype(
        jnp.bfloat16
    )
    normed_ref[:, width:] = info_ref[...]


def experts_kernel(experts, capacity, tile, halves, n_rows, n_gate, n_up, *refs):
    rows_in = refs[:n_rows]
    gate_refs = list(refs[n_rows : n_rows + n_gate])
    up_refs = list(refs[n_rows + n_gate : n_rows + n_gate + n_up])
    refs = refs[n_rows + n_gate + n_up :]
    up_hbm, down_hbm, keep_ref, send_ref, rows_ref, pick_ref, packed_ref, hidden_ref = refs[:8]
    up_late = list(refs[8 : 8 + experts - n_up])
    down_ref, up_sem, down_sem = refs[8 + experts - n_up :]
    per_expert, width = down_hbm.shape[0] // experts, down_hbm.shape[1]
    up_copies = [
        pltpu.make_async_copy(a, b, up_sem.at[i])
        for i, (a, b) in enumerate(columns(up_hbm, up_late, n_up))
    ]
    up_refs += up_late
    down_copies = [
        pltpu.make_async_copy(
            down_hbm.at[pl.ds(x * per_expert, per_expert)], down_ref, down_sem.at[x]
        )
        for x in range(experts)
    ]
    for c in down_copies[:1] + up_copies:
        c.start()
    count = 0
    for r in rows_in:
        rows_ref[count : count + r.shape[0], :] = r[...]
        count += r.shape[0]
    at0 = lax.broadcasted_iota(jnp.int32, (count, count), 0)
    at1 = lax.broadcasted_iota(jnp.int32, (count, count), 1)
    eye = jnp.where(at0 == at1, 1.0, 0.0).astype(jnp.bfloat16)
    before = jnp.where(at0 < at1, 1.0, 0.0).astype(jnp.bfloat16)
    info = lax.dot_general(
        rows_ref[:, width:], eye, (((0,), (0,)), ((), ())), preferred_element_type=jnp.float32
    )
    id0, id1, code0, code1 = (info[i : i + 1, :] for i in range(4))
    slot_of = lax.broadcasted_iota(jnp.int32, (capacity, count), 0).astype(jnp.float32)
    first = lax.axis_index("sec") * experts if halves == 1 else lax.axis_index("sec") // halves
    picks, shares = [], []
    for x in range(experts):
        e = (first + x).astype(jnp.float32)
        hit0 = jnp.where(id0 == e, 1.0, 0.0)
        hit1 = jnp.where(id1 == e, 1.0, 0.0)
        member = hit0 + hit1
        share = (hit0 * code0 + hit1 * code1) / (code0 + code1)
        slot = dot(jnp.broadcast_to(member, (8, count)).astype(jnp.bfloat16), before)[:1]
        slot = jnp.where(member > 0.5, slot, -1.0)
        pick = slot == slot_of
        shares.append(jnp.sum(jnp.where(pick, share, 0.0), axis=1, keepdims=True))
        picks.append(jnp.where(pick, 1.0, 0.0).astype(jnp.bfloat16))
    pick_ref[...] = jnp.concatenate(picks, axis=0)
    column = min(512, width)

    def pack(c, _):
        cut = pl.ds(pl.multiple_of(c * column, column), column)
        packed_ref[:, cut] = dot(pick_ref[...], rows_ref[:, cut]).astype(jnp.bfloat16)
        return 0

    lax.fori_loop(0, width // column, pack, 0)
    for x in range(experts):
        mine = slice(x * capacity, (x + 1) * capacity)
        if x >= n_up:
            up_copies[x - n_up].wait()
        gate_ref, up_ref = gate_refs[x], up_refs[x]

        def inner(s, _):
            cut = pl.ds(pl.multiple_of(s * tile, tile), tile)
            gate = dot(packed_ref[mine, :], gate_ref[:, cut])
            up = dot(packed_ref[mine, :], up_ref[:, cut])
            hidden_ref[mine, cut] = (gate / (1.0 + jnp.exp(-gate)) * up).astype(jnp.bfloat16)
            return 0

        lax.fori_loop(0, per_expert // tile, inner, 0)
        down_copies[x].wait()

        def outer(c, _):
            cut = pl.ds(pl.multiple_of(c * column, column), column)
            out = dot(hidden_ref[mine, :], down_ref[:, cut])
            packed_ref[mine, cut] = (out * shares[x]).astype(jnp.bfloat16)
            return 0

        lax.fori_loop(0, width // column, outer, 0)
        if x + 1 < experts:
            down_copies[x + 1].start()
    kept = keep_ref.shape[0]

    def spread(c, _):
        cut = pl.ds(pl.multiple_of(c * column, column), column)
        out = lax.dot_general(
            pick_ref[...], packed_ref[:, cut], (((0,), (0,)), ((), ())),
            preferred_element_type=jnp.float32,
        )
        keep_ref[:, cut] = out[:kept]
        send_ref[:, cut] = out[kept:].astype(jnp.bfloat16)
        return 0

    lax.fori_loop(0, width // column, spread, 0)


def per_device(
    query,
    keys,
    values,
    residual,
    out_weight,
    norm_gain,
    expert_ids,
    gate_codes,
    doc_lengths,
    w_gate,
    w_up,
    w_down,
):
    block, width = residual.shape
    head = HEAD_DIMENSION
    group_width = QUERY_HEAD_COUNT // KEY_VALUE_HEADS
    q_heads = query.shape[1] // head
    sec_count, tp_count, pp_count = (lax.axis_size(a) for a in ("sec", "tp", "pp"))
    own_rows = block // (tp_count * pp_count)
    bf16, f32 = jnp.bfloat16, jnp.float32

    kv_heads = max(1, q_heads // group_width)
    group = q_heads // kv_heads
    kv_start = lax.axis_index("pp") * q_heads // group_width * head
    kv = jnp.concatenate(
        [lax.dynamic_slice_in_dim(a, kv_start, kv_heads * head, 1) for a in (keys, values)], axis=1
    )
    back = -(-(sec_count * block // 2 - 1) // block)
    pieces = [
        lax.ppermute(kv, "sec", [(i, i + k) for i in range(sec_count - k)])
        for k in range(back, 0, -1)
    ] + [kv]

    experts = max(1, E // sec_count)
    per_expert = w_gate.shape[2] // experts
    span = (back + 1) * block
    query_v, weight_v, gain_v, mask, order, residual_own, info = call(
        functools.partial(prepare_kernel, back, tp_count, pp_count),
        [
            sds(query.shape, bf16),
            sds(out_weight.shape, bf16),
            sds((1, width), f32),
            sds((block, span), f32),
            sds((block, block), bf16),
            sds((own_rows, width), f32),
            sds((own_rows, LANES), bf16),
        ],
        [
            (HBM, a)
            for a in (
                doc_lengths, expert_ids.T, gate_codes.T, query, out_weight, residual,
                norm_gain.reshape(1, width),
            )
        ],
        scratch=[
            pltpu.SMEM(doc_lengths.shape, jnp.int32),
            pltpu.VMEM((2, block), jnp.int32),
            pltpu.VMEM((2, block), jnp.int32),
            pltpu.VMEM(residual.shape, bf16),
            pltpu.SemaphoreType.DMA((7,)),
        ],
        vmem=6,
        name="prepare",
        cost_us=2.0,
    )
    half = block // pp_count
    keep, send = call(
        functools.partial(attention_kernel, back, kv_heads, group),
        [sds((half, width), f32), sds((block - half, width), bf16)],
        [(VMEM, a) for a in (query_v, mask, order, *pieces, weight_v)],
        scratch=[pltpu.VMEM(query.shape, bf16)],
        name="attention",
        cost_us=2.4,
    )

    (own,), sends = add(
        [keep] + [xor_swap(send, "pp", 1)], [own_rows], [own_rows] * (tp_count - 1), "sum_cores"
    )
    got = [xor_swap(sends[k - 1], "tp", k) for k in range(1, tp_count)]
    stream, normed = call(
        functools.partial(norm_kernel, tp_count),
        [sds((own_rows, width), f32), sds((own_rows, width + LANES), bf16)],
        [(VMEM, a) for a in (residual_own, gain_v, info, own, *got)],
        name="norm",
        cost_us=0.2,
    )

    near = {k: xor_swap(normed, "sec", k) for k in range(sec_count - 1, 0, -1)}
    near[0] = normed
    split = max(1, sec_count // 2)
    groups = [g for g in ([0], list(range(1, split)), list(range(split, sec_count))) if g]
    gate_v = [load(w_gate[0], 0, per_expert, [normed], "load_gate")]
    up_v = []
    last_load = gate_v[0]
    rows = []
    for i, g in enumerate(groups):
        piece = near[0] if i == 0 else join([near[k] for k in g], [last_load], "join_z")
        rows.append([piece] + [xor_swap(piece, "tp", k) for k in range(1, tp_count)])
        if i == 1 or (i == 0 and len(groups) == 1):
            last_load = load(w_up[0], 0, per_expert, [piece, last_load], "load_up")
            up_v.append(last_load)
        if i == len(groups) - 1:
            for x in range(1, experts):
                last_load = load(
                    w_gate[0], x * per_expert, per_expert, [piece, last_load], "load_gate"
                )
                gate_v.append(last_load)
    rows = [[rows[g][k] for g in range(len(groups))] for k in range(tp_count)]
    early = join(
        rows[0] + [r for k in range(1, tp_count) for r in rows[k][:-1]], [], "join_early"
    )
    late = join([rows[k][-1] for k in range(1, tp_count)], [last_load], "join_late")
    early = [early] + [xor_swap(early, "pp", k) for k in range(1, pp_count)]
    late = [late] + [xor_swap(late, "pp", k) for k in range(1, pp_count)]
    rows = [r for pair in zip(early, late) for r in pair]

    halves = max(1, sec_count // E)
    count = sec_count * block
    capacity = sec_count * MOSTB
    down = w_down[0]
    tile = min(512, down.shape[0] // experts)
    kept = count // pp_count
    keep, send = call(
        functools.partial(experts_kernel, experts, capacity, tile, halves, len(rows), experts, 1),
        [sds((kept, width), f32), sds((count - kept, width), bf16)],
        [(VMEM, a) for a in (*rows, *gate_v, *up_v)] + [(HBM, w_up[0]), (HBM, down)],
        scratch=[
            pltpu.VMEM((count, width + LANES), bf16),
            pltpu.VMEM((experts * capacity, count), bf16),
            pltpu.VMEM((experts * capacity, width), bf16),
            pltpu.VMEM((experts * capacity, down.shape[0] // experts), bf16),
            *[pltpu.VMEM((width, per_expert), bf16)] * (experts - 1),
            pltpu.VMEM((per_expert, width), bf16),
            pltpu.SemaphoreType.DMA((experts,)),
            pltpu.SemaphoreType.DMA((experts,)),
        ],
        vmem=20,
        name="experts",
        cost_us=12.0,
    )

    sizes = [len(g) * own_rows for g in groups]
    last = len(groups) - 1
    outs = add(
        [keep, xor_swap(send, "pp", 1)],
        sizes,
        [z for k in range(1, tp_count) for z in sizes[:-1]] + sizes[-1:] * (tp_count - 1),
        "sum_cores2",
    )
    mine, sends = outs
    theirs = [
        [sends[(k - 1) * last + g] for k in range(1, tp_count)] for g in range(last)
    ] + [sends[(tp_count - 1) * last :]]
    final = [stream]
    for g in range(last, -1, -1):
        got = [xor_swap(theirs[g][k - 1], "tp", k) for k in range(1, tp_count)]
        if g == 0:
            final += [mine[0]] + got
            continue
        _, out = add([mine[g]] + got, [], [own_rows] * len(groups[g]), "sum_x%d" % g)
        final += [xor_swap(o, "sec", k) for k, o in zip(groups[g], out)]
    return call(
        functools.partial(add_kernel, 0, len(final)),
        [sds((own_rows, width), bf16)],
        [(VMEM, a) for a in final],
        name="total",
        cost_us=0.2,
    )[0]


def solution(mesh):
    in_specs = (
        P(("groups", "sec"), ("tp", "pp")),
        P(("groups", "sec"), "tp"),
        P(("groups", "sec"), "tp"),
        P(("groups", "sec"), None),
        P(("tp", "pp"), None),
        P(),
        P(("groups", "sec"), None),
        P(("groups", "sec"), None),
        P("groups"),
        P(("tp", "pp"), None, "sec"),
        P(("tp", "pp"), None, "sec"),
        P(("tp", "pp"), "sec", None),
    )
    out_specs = P(("groups", "sec", "tp", "pp"), None)
    return jax.shard_map(
        per_device, mesh=mesh, in_specs=in_specs, out_specs=out_specs, check_vma=False
    )
```

```python
import functools

import jax
import jax.numpy as jnp
from jax import lax
from jax.experimental import pallas as pl
from jax.experimental.pallas import tpu as pltpu
from jax.sharding import PartitionSpec as P

QUERY_HEAD_COUNT = 32
KEY_VALUE_HEADS = 8
HEAD_DIMENSION = 128
E = 8
MOSTB = 32
LANES = 128

neg_fill = -1e30
norm_eps = 1e-05

VMEM = pl.BlockSpec(memory_space=pltpu.VMEM)
SMEM = pl.BlockSpec(memory_space=pltpu.SMEM)
HBM = pl.BlockSpec(memory_space=pltpu.HBM)
ANY = pl.BlockSpec(memory_space=pl.ANY)
MIB = 2**20


def dot(a, b):
    return jnp.dot(a, b, preferred_element_type=jnp.float32)


def xor_swap(x, axis, k):
    n = lax.axis_size(axis)
    return lax.ppermute(x, axis, [(i, i ^ k) for i in range(n)])


def call(kernel, out_shape, args, scratch=(), vmem=8, name=None, cost_us=1.0):
    args = [
        (s, pltpu.with_memory_space_constraint(a, pltpu.HBM) if s is HBM else a) for s, a in args
    ]
    single = not isinstance(out_shape, (tuple, list))
    return pl.pallas_call(
        kernel,
        out_shape=out_shape,
        in_specs=[s for s, _ in args],
        out_specs=VMEM if single else [VMEM] * len(out_shape),
        scratch_shapes=list(scratch),
        compiler_params=pltpu.CompilerParams(vmem_limit_bytes=vmem * MIB),
        cost_estimate=pl.CostEstimate(
            flops=0, bytes_accessed=int(cost_us * 3.4e6), transcendentals=0
        ),
        name=name,
    )(*[a for _, a in args])


def sds(shape, dtype):
    return jax.ShapeDtypeStruct(shape, dtype)


def position():
    rank = lax.axis_index("tp") * lax.axis_size("pp") + lax.axis_index("pp")
    return lax.axis_index("sec"), rank


def columns(source, targets, first=0):
    per = targets[0].shape[1] if targets else 0
    return [(source.at[:, pl.ds((first + i) * per, per)], t) for i, t in enumerate(targets)]


def prepare_kernel(
    back, tp_count, pp_count, lengths_hbm, ids_hbm, codes_hbm, query_hbm, weight_hbm, residual_hbm,
    gain_hbm, *refs
):
    gate_hbm, query_ref, weight_ref, gain_ref, mask_ref, order_ref, residual_ref, info_ref = refs[
        :8
    ]
    gate_refs = refs[8:-5]
    lengths, ids, codes, residual_all, sem = refs[-5:]
    pairs = [
        (lengths_hbm, lengths),
        (ids_hbm, ids),
        (codes_hbm, codes),
        (residual_hbm, residual_all),
        (query_hbm, query_ref),
        (gain_hbm, gain_ref),
        (weight_hbm, weight_ref),
    ] + columns(gate_hbm, gate_refs)
    copies = [pltpu.make_async_copy(a, b, sem.at[i]) for i, (a, b) in enumerate(pairs)]
    for c in copies:
        c.start()
    sec, rank = position()
    block = query_ref.shape[0]
    own_rows = residual_ref.shape[0]
    at = lax.broadcasted_iota(jnp.int32, (block, block), 0)
    to = lax.broadcasted_iota(jnp.int32, (block, block), 1)
    chunk = lax.div(at, own_rows)
    flip = lax.rem(chunk, tp_count) * pp_count + lax.div(chunk, tp_count)
    source = (rank ^ flip) * own_rows + lax.rem(at, own_rows)
    order_ref[...] = jnp.where(to == source, 1.0, 0.0).astype(jnp.bfloat16)
    own = lax.broadcasted_iota(jnp.int32, (own_rows, block), 0) + rank * own_rows
    own = jnp.where(own == lax.broadcasted_iota(jnp.int32, (own_rows, block), 1), 1.0, 0.0)
    own = own.astype(jnp.bfloat16)
    for c in copies[:4]:
        c.wait()
    span = (back + 1) * block
    rows = sec * block + lax.broadcasted_iota(jnp.int32, (block, span), 0)
    cols = (sec - back) * block + lax.broadcasted_iota(jnp.int32, (block, span), 1)
    first = jnp.zeros((block, span), jnp.int32)
    end = jnp.int32(0)
    for d in range(lengths.shape[0]):
        end = end + lengths[d]
        first = jnp.where(rows >= end, end, first)
    mask_ref[...] = jnp.where((cols <= rows) & (cols >= first), 1.0, 0.0)
    residual_ref[...] = dot(own, residual_all[...])
    info = jnp.concatenate(
        [ids[...], codes[...], jnp.zeros((LANES - 4, block), jnp.int32)], axis=0
    ).astype(jnp.float32)
    info_ref[...] = lax.dot_general(
        own, info.astype(jnp.bfloat16), (((1,), (1,)), ((), ())), preferred_element_type=jnp.float32
    ).astype(jnp.bfloat16)
    for c in copies[4:]:
        c.wait()


def load_kernel(n_after, source, *refs):
    *targets, token_ref, sem = refs[n_after:]
    copies = [
        pltpu.make_async_copy(a, b, sem.at[i])
        for i, (a, b) in enumerate(columns(source, targets))
    ]
    for c in copies:
        c.start()
    token_ref[...] = jnp.zeros_like(token_ref)
    for c in copies:
        c.wait()


def load(array, parts, wanted, after, name):
    rows, cols = array.shape
    out = call(
        functools.partial(load_kernel, len(after)),
        [sds((rows, cols // parts), array.dtype)] * wanted + [sds((8, LANES), jnp.float32)],
        [(HBM, array)] + [(ANY, a) for a in after],
        scratch=[pltpu.SemaphoreType.DMA((wanted,))],
        vmem=1,
        name=name,
        cost_us=array.size * wanted / parts * 2 / 3.4e6,
    )
    return out[:-1], out[-1]


def attention_kernel(back, kv_heads, group, q_ref, mask_ref, order_ref, *refs):
    kv_refs = refs[: back + 1]
    weight_ref, keep_ref, send_ref, attended_ref = refs[back + 1 :]
    block = q_ref.shape[0]
    head = HEAD_DIMENSION
    allowed = jnp.concatenate([mask_ref[...]] * group, axis=0) > 0.5
    for g in range(kv_heads):
        q = jnp.concatenate(
            [q_ref[:, (g * group + t) * head : (g * group + t + 1) * head] for t in range(group)],
            axis=0,
        )
        k = jnp.concatenate([r[:, g * head : (g + 1) * head] for r in kv_refs], axis=0)
        v = jnp.concatenate(
            [r[:, (kv_heads + g) * head : (kv_heads + g + 1) * head] for r in kv_refs], axis=0
        )
        scores = lax.dot_general(
            q, k, (((1,), (1,)), ((), ())), preferred_element_type=jnp.float32
        ) * (head**-0.5)
        scores = jnp.where(allowed, scores, neg_fill)
        top = jnp.max(scores, axis=1, keepdims=True)
        weights = jnp.where(allowed, jnp.exp(scores - top), 0.0)
        total = jnp.sum(weights, axis=1, keepdims=True)
        summed = dot(weights.astype(jnp.bfloat16), v) / total
        for t in range(group):
            attended_ref[:, (g * group + t) * head : (g * group + t + 1) * head] = summed[
                t * block : (t + 1) * block
            ].astype(jnp.bfloat16)
    attended = dot(order_ref[...], attended_ref[...]).astype(jnp.bfloat16)
    mixed = dot(attended, weight_ref[...])
    kept = keep_ref.shape[0]
    keep_ref[...] = mixed[:kept]
    send_ref[...] = mixed[kept:].astype(jnp.bfloat16)


def add_kernel(keep_rows, n_in, *refs):
    total = refs[0][...].astype(jnp.float32)
    for r in refs[1:n_in]:
        total = total + r[...].astype(jnp.float32)
    start = 0
    for r in refs[n_in:]:
        r[...] = total[start : start + r.shape[0]].astype(r.dtype)
        start += r.shape[0]


def add(arrays, keep, send, name):
    width = arrays[0].shape[1]
    out = [sds((r, width), jnp.float32) for r in keep]
    out += [sds((r, width), jnp.bfloat16) for r in send]
    out = call(
        functools.partial(add_kernel, sum(keep), len(arrays)),
        out,
        [(VMEM, a) for a in arrays],
        name=name,
        cost_us=0.2,
    )
    return out[: len(keep)], out[len(keep) :]


def norm_kernel(n_parts, residual_ref, gain_ref, info_ref, *refs):
    parts = refs[:n_parts]
    stream_ref, normed_ref = refs[-2:]
    width = residual_ref.shape[1]
    mixed = parts[0][...].astype(jnp.float32)
    for p in parts[1:]:
        mixed = mixed + p[...].astype(jnp.float32)
    stream = residual_ref[...] + mixed
    stream_ref[...] = stream
    meansq = jnp.mean(stream * stream, axis=1, keepdims=True)
    normed_ref[:, :width] = (stream * lax.rsqrt(meansq + norm_eps) * gain_ref[...]).astype(
        jnp.bfloat16
    )
    normed_ref[:, width:] = info_ref[...]


def experts_kernel(experts, capacity, tile, halves, n_rows, *refs):
    rows_in = refs[:n_rows]
    gate_first, up_first, gate_hbm, up_hbm, down_hbm, keep_ref, send_ref = refs[
        n_rows : n_rows + 7
    ]
    rows_ref, pick_ref, packed_ref, hidden_ref, gate_ref, up_ref, down_ref, sem = refs[n_rows + 7 :]
    per_expert, width = down_hbm.shape[0] // experts, down_hbm.shape[1]
    steps = per_expert // tile
    column = min(512, width)
    gates, ups, downs = [], [], []
    for x in range(experts):
        for s in range(steps if x else 0):
            cut = pl.ds(x * per_expert + s * tile, tile)
            at = (x - 1) * steps + s
            gates.append(pltpu.make_async_copy(gate_hbm.at[:, cut], gate_ref.at[at], sem.at[0, at]))
            ups.append(pltpu.make_async_copy(up_hbm.at[:, cut], up_ref.at[at], sem.at[1, at]))
        for c in range(width // column):
            source = down_hbm.at[pl.ds(x * per_expert, per_expert), pl.ds(c * column, column)]
            at = x * (width // column) + c
            downs.append(pltpu.make_async_copy(source, down_ref.at[c], sem.at[2, at]))
    first_downs = downs[: width // column]
    for c in first_downs + [c for pair in zip(gates, ups) for c in pair]:
        c.start()
    count = 0
    for r in rows_in:
        rows_ref[count : count + r.shape[0], :] = r[...]
        count += r.shape[0]
    at0 = lax.broadcasted_iota(jnp.int32, (count, count), 0)
    at1 = lax.broadcasted_iota(jnp.int32, (count, count), 1)
    eye = jnp.where(at0 == at1, 1.0, 0.0).astype(jnp.bfloat16)
    before = jnp.where(at0 < at1, 1.0, 0.0).astype(jnp.bfloat16)
    info = lax.dot_general(
        rows_ref[:, width:], eye, (((0,), (0,)), ((), ())), preferred_element_type=jnp.float32
    )
    id0, id1, code0, code1 = (info[i : i + 1, :] for i in range(4))
    slot_of = lax.broadcasted_iota(jnp.int32, (capacity, count), 0).astype(jnp.float32)
    first = lax.axis_index("sec") * experts if halves == 1 else lax.axis_index("sec") // halves
    picks, shares = [], []
    for x in range(experts):
        e = (first + x).astype(jnp.float32)
        hit0 = jnp.where(id0 == e, 1.0, 0.0)
        hit1 = jnp.where(id1 == e, 1.0, 0.0)
        member = hit0 + hit1
        share = (hit0 * code0 + hit1 * code1) / (code0 + code1)
        slot = dot(jnp.broadcast_to(member, (8, count)).astype(jnp.bfloat16), before)[:1]
        slot = jnp.where(member > 0.5, slot, -1.0)
        pick = slot == slot_of
        shares.append(jnp.sum(jnp.where(pick, share, 0.0), axis=1, keepdims=True))
        picks.append(jnp.where(pick, 1.0, 0.0).astype(jnp.bfloat16))
    pick_ref[...] = jnp.concatenate(picks, axis=0)
    for c in range(0, width, column):
        packed_ref[:, c : c + column] = dot(pick_ref[...], rows_ref[:, c : c + column]).astype(
            jnp.bfloat16
        )
    for x in range(experts):
        mine = slice(x * capacity, (x + 1) * capacity)
        for s in range(steps):
            cut = slice(s * tile, (s + 1) * tile)
            at = (x - 1) * steps + s
            if x:
                gates[at].wait()
                ups[at].wait()
            gate = dot(packed_ref[mine, :], gate_ref[at] if x else gate_first[:, cut])
            up = dot(packed_ref[mine, :], up_ref[at] if x else up_first[:, cut])
            half = 0.5 * gate
            hidden_ref[mine, cut] = ((half + half * jnp.tanh(half)) * up).astype(jnp.bfloat16)
        for c in range(width // column):
            cut = slice(c * column, (c + 1) * column)
            downs[x * (width // column) + c].wait()
            out = dot(hidden_ref[mine, :], down_ref[c])
            packed_ref[mine, cut] = (out * shares[x]).astype(jnp.bfloat16)
            if x + 1 < experts:
                downs[(x + 1) * (width // column) + c].start()
    kept = keep_ref.shape[0]
    for c in range(0, width, column):
        out = lax.dot_general(
            pick_ref[...], packed_ref[:, c : c + column], (((0,), (0,)), ((), ())),
            preferred_element_type=jnp.float32,
        )
        keep_ref[:, c : c + column] = out[:kept]
        send_ref[:, c : c + column] = out[kept:].astype(jnp.bfloat16)


def per_device(
    query,
    keys,
    values,
    residual,
    out_weight,
    norm_gain,
    expert_ids,
    gate_codes,
    doc_lengths,
    w_gate,
    w_up,
    w_down,
):
    block, width = residual.shape
    head = HEAD_DIMENSION
    group_width = QUERY_HEAD_COUNT // KEY_VALUE_HEADS
    q_heads = query.shape[1] // head
    sec_count, tp_count, pp_count = (lax.axis_size(a) for a in ("sec", "tp", "pp"))
    own_rows = block // (tp_count * pp_count)
    bf16, f32 = jnp.bfloat16, jnp.float32

    kv_heads = max(1, q_heads // group_width)
    group = q_heads // kv_heads
    kv_start = lax.axis_index("pp") * q_heads // group_width * head
    kv = jnp.concatenate(
        [lax.dynamic_slice_in_dim(a, kv_start, kv_heads * head, 1) for a in (keys, values)], axis=1
    )
    back = -(-(sec_count * block // 2 - 1) // block)
    pieces = [
        lax.ppermute(kv, "sec", [(i, i + k) for i in range(sec_count - k)])
        for k in range(back, 0, -1)
    ] + [kv]

    experts = max(1, E // sec_count)
    per_expert = w_gate.shape[2] // experts
    span = (back + 1) * block
    query_v, weight_v, gain_v, mask, order, residual_own, info, *gate_v = call(
        functools.partial(prepare_kernel, back, tp_count, pp_count),
        [
            sds(query.shape, bf16),
            sds(out_weight.shape, bf16),
            sds((1, width), f32),
            sds((block, span), f32),
            sds((block, block), bf16),
            sds((own_rows, width), f32),
            sds((own_rows, LANES), bf16),
        ]
        + [sds((width, per_expert), bf16)],
        [
            (HBM, a)
            for a in (
                doc_lengths, expert_ids.T, gate_codes.T, query, out_weight, residual,
                norm_gain.reshape(1, width), w_gate[0],
            )
        ],
        scratch=[
            pltpu.SMEM(doc_lengths.shape, jnp.int32),
            pltpu.VMEM((2, block), jnp.int32),
            pltpu.VMEM((2, block), jnp.int32),
            pltpu.VMEM(residual.shape, bf16),
            pltpu.SemaphoreType.DMA((8,)),
        ],
        vmem=6,
        name="prepare",
        cost_us=4.0,
    )
    half = block // pp_count
    keep, send = call(
        functools.partial(attention_kernel, back, kv_heads, group),
        [sds((half, width), f32), sds((block - half, width), bf16)],
        [(VMEM, a) for a in (query_v, mask, order, *pieces, weight_v)],
        scratch=[pltpu.VMEM(query.shape, bf16)],
        name="attention",
        cost_us=2.4,
    )

    (own,), sends = add(
        [keep] + [xor_swap(send, "pp", 1)], [own_rows], [own_rows] * (tp_count - 1), "sum_cores"
    )
    got = [xor_swap(sends[k - 1], "tp", k) for k in range(1, tp_count)]
    up_v, token = load(w_up[0], experts, 1, [own], "load_up")
    stream, normed = call(
        functools.partial(norm_kernel, tp_count),
        [sds((own_rows, width), f32), sds((own_rows, width + LANES), bf16)],
        [(VMEM, a) for a in (residual_own, gain_v, info, own, *got)] + [(ANY, token)],
        name="norm",
        cost_us=0.2,
    )

    groups = min(4, sec_count)
    near = [normed] + [xor_swap(normed, "sec", k) for k in range(1, sec_count)]
    per_group = sec_count // groups
    near = [
        jnp.concatenate(near[g * per_group : (g + 1) * per_group], axis=0)
        if per_group > 1
        else near[g]
        for g in range(groups)
    ]
    rows = [[r] + [xor_swap(r, "tp", k) for k in range(1, tp_count)] for r in near]
    rows = [rows[g][k] for k in range(tp_count) for g in range(groups)]
    rows = rows + [xor_swap(r, "pp", k) for k in range(1, pp_count) for r in rows]

    halves = max(1, sec_count // E)
    count = sec_count * block
    capacity = sec_count * MOSTB
    down = w_down[0]
    tile = min(512, down.shape[0] // experts)
    late = max(1, (experts - 1) * (per_expert // tile))
    column = min(512, width)
    kept = count // pp_count
    keep, send = call(
        functools.partial(experts_kernel, experts, capacity, tile, halves, len(rows)),
        [sds((kept, width), f32), sds((count - kept, width), bf16)],
        [(VMEM, a) for a in (*rows, *gate_v, *up_v)] + [(HBM, a) for a in (w_gate[0], w_up[0], down)],
        scratch=[
            pltpu.VMEM((count, width + LANES), bf16),
            pltpu.VMEM((experts * capacity, count), bf16),
            pltpu.VMEM((experts * capacity, width), bf16),
            pltpu.VMEM((experts * capacity, down.shape[0] // experts), bf16),
            pltpu.VMEM((late, width, tile), bf16),
            pltpu.VMEM((late, width, tile), bf16),
            pltpu.VMEM((width // column, per_expert, column), bf16),
            pltpu.SemaphoreType.DMA((3, max(late, experts * (width // column)))),
        ],
        vmem=30,
        name="experts",
        cost_us=12.0,
    )

    piece = kept // (tp_count * groups)
    own, sends = add(
        [keep, xor_swap(send, "pp", 1)], [piece] * groups, [piece] * (groups * (tp_count - 1)), "sum_cores2"
    )
    final = [stream]
    for g in list(range(1, groups)) + [0]:
        got = [xor_swap(sends[(k - 1) * groups + g], "tp", k) for k in range(1, tp_count)]
        if g == 0 and per_group == 1:
            final += [own[0]] + got
            continue
        kept_rows = own_rows if g == 0 else 0
        mine, out = add(
            [own[g]] + got,
            [own_rows] if g == 0 else [],
            [own_rows] * (per_group - (g == 0)),
            "sum_x%d" % g,
        )
        final += list(mine)
        for j, o in enumerate(out):
            final.append(xor_swap(o, "sec", g * per_group + j + (g == 0)))
    return call(
        functools.partial(add_kernel, 0, len(final)),
        [sds((own_rows, width), bf16)],
        [(VMEM, a) for a in final],
        name="total",
        cost_us=0.2,
    )[0]


def solution(mesh):
    in_specs = (
        P(("groups", "sec"), ("tp", "pp")),
        P(("groups", "sec"), "tp"),
        P(("groups", "sec"), "tp"),
        P(("groups", "sec"), None),
        P(("tp", "pp"), None),
        P(),
        P(("groups", "sec"), None),
        P(("groups", "sec"), None),
        P("groups"),
        P(("tp", "pp"), None, "sec"),
        P(("tp", "pp"), None, "sec"),
        P(("tp", "pp"), "sec", None),
    )
    out_specs = P(("groups", "sec", "tp", "pp"), None)
    return jax.shard_map(
        per_device, mesh=mesh, in_specs=in_specs, out_specs=out_specs, check_vma=False
    )
```

```python
import functools

import jax
import jax.numpy as jnp
from jax import lax
from jax.experimental import pallas as pl
from jax.experimental.pallas import tpu as pltpu
from jax.sharding import PartitionSpec as P

QUERY_HEAD_COUNT = 32
KEY_VALUE_HEADS = 8
HEAD_DIMENSION = 128
E = 8
MOSTB = 32
LANES = 128

neg_fill = -1e30
norm_eps = 1e-05

VMEM = pl.BlockSpec(memory_space=pltpu.VMEM)
SMEM = pl.BlockSpec(memory_space=pltpu.SMEM)
HBM = pl.BlockSpec(memory_space=pltpu.HBM)
ANY = pl.BlockSpec(memory_space=pl.ANY)
MIB = 2**20


def dot(a, b):
    return jnp.dot(a, b, preferred_element_type=jnp.float32)


def xor_swap(x, axis, k):
    n = lax.axis_size(axis)
    return lax.ppermute(x, axis, [(i, i ^ k) for i in range(n)])


def call(kernel, out_shape, args, scratch=(), vmem=8, name=None, cost_us=1.0):
    args = [
        (s, pltpu.with_memory_space_constraint(a, pltpu.HBM) if s is HBM else a) for s, a in args
    ]
    single = not isinstance(out_shape, (tuple, list))
    return pl.pallas_call(
        kernel,
        out_shape=out_shape,
        in_specs=[s for s, _ in args],
        out_specs=VMEM if single else [VMEM] * len(out_shape),
        scratch_shapes=list(scratch),
        compiler_params=pltpu.CompilerParams(vmem_limit_bytes=vmem * MIB),
        cost_estimate=pl.CostEstimate(
            flops=0, bytes_accessed=int(cost_us * 3.4e6), transcendentals=0
        ),
        name=name,
    )(*[a for _, a in args])


def sds(shape, dtype):
    return jax.ShapeDtypeStruct(shape, dtype)


def position():
    rank = lax.axis_index("tp") * lax.axis_size("pp") + lax.axis_index("pp")
    return lax.axis_index("sec"), rank


def columns(source, targets, first=0):
    per = targets[0].shape[1] if targets else 0
    return [(source.at[:, pl.ds((first + i) * per, per)], t) for i, t in enumerate(targets)]


def prepare_kernel(
    back, tp_count, pp_count, lengths_hbm, ids_hbm, codes_hbm, query_hbm, weight_hbm, residual_hbm,
    gain_hbm, *refs
):
    gate_hbm, query_ref, weight_ref, gain_ref, mask_ref, order_ref, residual_ref, info_ref = refs[
        :8
    ]
    gate_refs = refs[8:-5]
    lengths, ids, codes, residual_all, sem = refs[-5:]
    pairs = [
        (lengths_hbm, lengths),
        (ids_hbm, ids),
        (codes_hbm, codes),
        (residual_hbm, residual_all),
        (query_hbm, query_ref),
        (gain_hbm, gain_ref),
        (weight_hbm, weight_ref),
    ] + columns(gate_hbm, gate_refs)
    copies = [pltpu.make_async_copy(a, b, sem.at[i]) for i, (a, b) in enumerate(pairs)]
    for c in copies:
        c.start()
    sec, rank = position()
    block = query_ref.shape[0]
    own_rows = residual_ref.shape[0]
    at = lax.broadcasted_iota(jnp.int32, (block, block), 0)
    to = lax.broadcasted_iota(jnp.int32, (block, block), 1)
    chunk = lax.div(at, own_rows)
    flip = lax.rem(chunk, tp_count) * pp_count + lax.div(chunk, tp_count)
    source = (rank ^ flip) * own_rows + lax.rem(at, own_rows)
    order_ref[...] = jnp.where(to == source, 1.0, 0.0).astype(jnp.bfloat16)
    own = lax.broadcasted_iota(jnp.int32, (own_rows, block), 0) + rank * own_rows
    own = jnp.where(own == lax.broadcasted_iota(jnp.int32, (own_rows, block), 1), 1.0, 0.0)
    own = own.astype(jnp.bfloat16)
    for c in copies[:4]:
        c.wait()
    span = (back + 1) * block
    rows = sec * block + lax.broadcasted_iota(jnp.int32, (block, span), 0)
    cols = (sec - back) * block + lax.broadcasted_iota(jnp.int32, (block, span), 1)
    first = jnp.zeros((block, span), jnp.int32)
    end = jnp.int32(0)
    for d in range(lengths.shape[0]):
        end = end + lengths[d]
        first = jnp.where(rows >= end, end, first)
    mask_ref[...] = jnp.where((cols <= rows) & (cols >= first), 1.0, 0.0)
    residual_ref[...] = dot(own, residual_all[...])
    info = jnp.concatenate(
        [ids[...], codes[...], jnp.zeros((LANES - 4, block), jnp.int32)], axis=0
    ).astype(jnp.float32)
    info_ref[...] = lax.dot_general(
        own, info.astype(jnp.bfloat16), (((1,), (1,)), ((), ())), preferred_element_type=jnp.float32
    ).astype(jnp.bfloat16)
    for c in copies[4:]:
        c.wait()


def load_kernel(n_after, source, *refs):
    *targets, token_ref, sem = refs[n_after:]
    copies = [
        pltpu.make_async_copy(a, b, sem.at[i])
        for i, (a, b) in enumerate(columns(source, targets))
    ]
    for c in copies:
        c.start()
    token_ref[...] = jnp.zeros_like(token_ref)
    for c in copies:
        c.wait()


def load(array, parts, wanted, after, name):
    rows, cols = array.shape
    out = call(
        functools.partial(load_kernel, len(after)),
        [sds((rows, cols // parts), array.dtype)] * wanted + [sds((8, LANES), jnp.float32)],
        [(HBM, array)] + [(ANY, a) for a in after],
        scratch=[pltpu.SemaphoreType.DMA((wanted,))],
        vmem=1,
        name=name,
        cost_us=array.size * wanted / parts * 2 / 3.4e6,
    )
    return out[:-1], out[-1]


def attention_kernel(back, kv_heads, group, q_ref, mask_ref, order_ref, *refs):
    kv_refs = refs[: back + 1]
    weight_ref, keep_ref, send_ref, attended_ref = refs[back + 1 :]
    block = q_ref.shape[0]
    head = HEAD_DIMENSION
    allowed = jnp.concatenate([mask_ref[...]] * group, axis=0) > 0.5
    for g in range(kv_heads):
        q = jnp.concatenate(
            [q_ref[:, (g * group + t) * head : (g * group + t + 1) * head] for t in range(group)],
            axis=0,
        )
        k = jnp.concatenate([r[:, g * head : (g + 1) * head] for r in kv_refs], axis=0)
        v = jnp.concatenate(
            [r[:, (kv_heads + g) * head : (kv_heads + g + 1) * head] for r in kv_refs], axis=0
        )
        scores = lax.dot_general(
            q, k, (((1,), (1,)), ((), ())), preferred_element_type=jnp.float32
        ) * (head**-0.5)
        scores = jnp.where(allowed, scores, neg_fill)
        top = jnp.max(scores, axis=1, keepdims=True)
        weights = jnp.where(allowed, jnp.exp(scores - top), 0.0)
        total = jnp.sum(weights, axis=1, keepdims=True)
        summed = dot(weights.astype(jnp.bfloat16), v) / total
        for t in range(group):
            attended_ref[:, (g * group + t) * head : (g * group + t + 1) * head] = summed[
                t * block : (t + 1) * block
            ].astype(jnp.bfloat16)
    attended = dot(order_ref[...], attended_ref[...]).astype(jnp.bfloat16)
    mixed = dot(attended, weight_ref[...])
    kept = keep_ref.shape[0]
    keep_ref[...] = mixed[:kept]
    send_ref[...] = mixed[kept:].astype(jnp.bfloat16)


def add_kernel(keep_rows, n_in, *refs):
    total = refs[0][...].astype(jnp.float32)
    for r in refs[1:n_in]:
        total = total + r[...].astype(jnp.float32)
    start = 0
    for r in refs[n_in:]:
        r[...] = total[start : start + r.shape[0]].astype(r.dtype)
        start += r.shape[0]


def add(arrays, keep, send, name):
    width = arrays[0].shape[1]
    out = [sds((r, width), jnp.float32) for r in keep]
    out += [sds((r, width), jnp.bfloat16) for r in send]
    out = call(
        functools.partial(add_kernel, sum(keep), len(arrays)),
        out,
        [(VMEM, a) for a in arrays],
        name=name,
        cost_us=0.2,
    )
    return out[: len(keep)], out[len(keep) :]


def norm_kernel(n_parts, residual_ref, gain_ref, info_ref, *refs):
    parts = refs[:n_parts]
    stream_ref, normed_ref = refs[-2:]
    width = residual_ref.shape[1]
    mixed = parts[0][...].astype(jnp.float32)
    for p in parts[1:]:
        mixed = mixed + p[...].astype(jnp.float32)
    stream = residual_ref[...] + mixed
    stream_ref[...] = stream
    meansq = jnp.mean(stream * stream, axis=1, keepdims=True)
    normed_ref[:, :width] = (stream * lax.rsqrt(meansq + norm_eps) * gain_ref[...]).astype(
        jnp.bfloat16
    )
    normed_ref[:, width:] = info_ref[...]


def experts_kernel(experts, capacity, tile, halves, n_rows, n_gate, n_up, *refs):
    rows_in = refs[:n_rows]
    gate_refs = list(refs[n_rows : n_rows + n_gate])
    up_refs = list(refs[n_rows + n_gate : n_rows + n_gate + n_up])
    refs = refs[n_rows + n_gate + n_up :]
    up_hbm, down_hbm, keep_ref, send_ref, rows_ref, pick_ref, packed_ref, hidden_ref = refs[:8]
    up_late = list(refs[8 : 8 + experts - n_up])
    down_ref, up_sem, down_sem = refs[8 + experts - n_up :]
    per_expert, width = down_hbm.shape[0] // experts, down_hbm.shape[1]
    up_copies = [
        pltpu.make_async_copy(a, b, up_sem.at[i])
        for i, (a, b) in enumerate(columns(up_hbm, up_late, n_up))
    ]
    up_refs += up_late
    down_copies = [
        pltpu.make_async_copy(
            down_hbm.at[pl.ds(x * per_expert, per_expert)], down_ref, down_sem.at[x]
        )
        for x in range(experts)
    ]
    for c in down_copies[:1] + up_copies:
        c.start()
    count = 0
    for r in rows_in:
        rows_ref[count : count + r.shape[0], :] = r[...]
        count += r.shape[0]
    at0 = lax.broadcasted_iota(jnp.int32, (count, count), 0)
    at1 = lax.broadcasted_iota(jnp.int32, (count, count), 1)
    eye = jnp.where(at0 == at1, 1.0, 0.0).astype(jnp.bfloat16)
    before = jnp.where(at0 < at1, 1.0, 0.0).astype(jnp.bfloat16)
    info = lax.dot_general(
        rows_ref[:, width:], eye, (((0,), (0,)), ((), ())), preferred_element_type=jnp.float32
    )
    id0, id1, code0, code1 = (info[i : i + 1, :] for i in range(4))
    slot_of = lax.broadcasted_iota(jnp.int32, (capacity, count), 0).astype(jnp.float32)
    first = lax.axis_index("sec") * experts if halves == 1 else lax.axis_index("sec") // halves
    picks, shares = [], []
    for x in range(experts):
        e = (first + x).astype(jnp.float32)
        hit0 = jnp.where(id0 == e, 1.0, 0.0)
        hit1 = jnp.where(id1 == e, 1.0, 0.0)
        member = hit0 + hit1
        share = (hit0 * code0 + hit1 * code1) / (code0 + code1)
        slot = dot(jnp.broadcast_to(member, (8, count)).astype(jnp.bfloat16), before)[:1]
        slot = jnp.where(member > 0.5, slot, -1.0)
        pick = slot == slot_of
        shares.append(jnp.sum(jnp.where(pick, share, 0.0), axis=1, keepdims=True))
        picks.append(jnp.where(pick, 1.0, 0.0).astype(jnp.bfloat16))
    pick_ref[...] = jnp.concatenate(picks, axis=0)
    column = min(512, width)

    for c in range(0, width, column):
        packed_ref[:, c : c + column] = dot(pick_ref[...], rows_ref[:, c : c + column]).astype(
            jnp.bfloat16
        )
    for x in range(experts):
        mine = slice(x * capacity, (x + 1) * capacity)
        if x >= n_up:
            up_copies[x - n_up].wait()
        gate_ref, up_ref = gate_refs[x], up_refs[x]

        for s in range(0, per_expert, tile):
            cut = slice(s, s + tile)
            gate = dot(packed_ref[mine, :], gate_ref[:, cut])
            up = dot(packed_ref[mine, :], up_ref[:, cut])
            half = 0.5 * gate
            hidden_ref[mine, cut] = ((half + half * jnp.tanh(half)) * up).astype(jnp.bfloat16)
        down_copies[x].wait()

        for c in range(0, width, column):
            out = dot(hidden_ref[mine, :], down_ref[:, c : c + column])
            packed_ref[mine, c : c + column] = (out * shares[x]).astype(jnp.bfloat16)
        if x + 1 < experts:
            down_copies[x + 1].start()
    kept = keep_ref.shape[0]

    for c in range(0, width, column):
        out = lax.dot_general(
            pick_ref[...], packed_ref[:, c : c + column], (((0,), (0,)), ((), ())),
            preferred_element_type=jnp.float32,
        )
        keep_ref[:, c : c + column] = out[:kept]
        send_ref[:, c : c + column] = out[kept:].astype(jnp.bfloat16)


def per_device(
    query,
    keys,
    values,
    residual,
    out_weight,
    norm_gain,
    expert_ids,
    gate_codes,
    doc_lengths,
    w_gate,
    w_up,
    w_down,
):
    block, width = residual.shape
    head = HEAD_DIMENSION
    group_width = QUERY_HEAD_COUNT // KEY_VALUE_HEADS
    q_heads = query.shape[1] // head
    sec_count, tp_count, pp_count = (lax.axis_size(a) for a in ("sec", "tp", "pp"))
    own_rows = block // (tp_count * pp_count)
    bf16, f32 = jnp.bfloat16, jnp.float32

    kv_heads = max(1, q_heads // group_width)
    group = q_heads // kv_heads
    kv_start = lax.axis_index("pp") * q_heads // group_width * head
    kv = jnp.concatenate(
        [lax.dynamic_slice_in_dim(a, kv_start, kv_heads * head, 1) for a in (keys, values)], axis=1
    )
    back = -(-(sec_count * block // 2 - 1) // block)
    pieces = [
        lax.ppermute(kv, "sec", [(i, i + k) for i in range(sec_count - k)])
        for k in range(back, 0, -1)
    ] + [kv]

    experts = max(1, E // sec_count)
    per_expert = w_gate.shape[2] // experts
    span = (back + 1) * block
    query_v, weight_v, gain_v, mask, order, residual_own, info, *gate_v = call(
        functools.partial(prepare_kernel, back, tp_count, pp_count),
        [
            sds(query.shape, bf16),
            sds(out_weight.shape, bf16),
            sds((1, width), f32),
            sds((block, span), f32),
            sds((block, block), bf16),
            sds((own_rows, width), f32),
            sds((own_rows, LANES), bf16),
        ]
        + [sds((width, per_expert), bf16)] * experts,
        [
            (HBM, a)
            for a in (
                doc_lengths, expert_ids.T, gate_codes.T, query, out_weight, residual,
                norm_gain.reshape(1, width), w_gate[0],
            )
        ],
        scratch=[
            pltpu.SMEM(doc_lengths.shape, jnp.int32),
            pltpu.VMEM((2, block), jnp.int32),
            pltpu.VMEM((2, block), jnp.int32),
            pltpu.VMEM(residual.shape, bf16),
            pltpu.SemaphoreType.DMA((7 + experts,)),
        ],
        vmem=6,
        name="prepare",
        cost_us=6.0,
    )
    half = block // pp_count
    keep, send = call(
        functools.partial(attention_kernel, back, kv_heads, group),
        [sds((half, width), f32), sds((block - half, width), bf16)],
        [(VMEM, a) for a in (query_v, mask, order, *pieces, weight_v)],
        scratch=[pltpu.VMEM(query.shape, bf16)],
        name="attention",
        cost_us=2.4,
    )

    (own,), sends = add(
        [keep] + [xor_swap(send, "pp", 1)], [own_rows], [own_rows] * (tp_count - 1), "sum_cores"
    )
    got = [xor_swap(sends[k - 1], "tp", k) for k in range(1, tp_count)]
    up_v, token = load(w_up[0], experts, 1, [own], "load_up")
    stream, normed = call(
        functools.partial(norm_kernel, tp_count),
        [sds((own_rows, width), f32), sds((own_rows, width + LANES), bf16)],
        [(VMEM, a) for a in (residual_own, gain_v, info, own, *got)] + [(ANY, token)],
        name="norm",
        cost_us=0.2,
    )

    groups = min(4, sec_count)
    near = [normed] + [xor_swap(normed, "sec", k) for k in range(1, sec_count)]
    per_group = sec_count // groups
    near = [
        jnp.concatenate(near[g * per_group : (g + 1) * per_group], axis=0)
        if per_group > 1
        else near[g]
        for g in range(groups)
    ]
    rows = [[r] + [xor_swap(r, "tp", k) for k in range(1, tp_count)] for r in near]
    rows = [rows[g][k] for k in range(tp_count) for g in range(groups)]
    rows = rows + [xor_swap(r, "pp", k) for k in range(1, pp_count) for r in rows]

    halves = max(1, sec_count // E)
    count = sec_count * block
    capacity = sec_count * MOSTB
    down = w_down[0]
    tile = min(512, down.shape[0] // experts)
    kept = count // pp_count
    keep, send = call(
        functools.partial(experts_kernel, experts, capacity, tile, halves, len(rows), experts, 1),
        [sds((kept, width), f32), sds((count - kept, width), bf16)],
        [(VMEM, a) for a in (*rows, *gate_v, *up_v)] + [(HBM, w_up[0]), (HBM, down)],
        scratch=[
            pltpu.VMEM((count, width + LANES), bf16),
            pltpu.VMEM((experts * capacity, count), bf16),
            pltpu.VMEM((experts * capacity, width), bf16),
            pltpu.VMEM((experts * capacity, down.shape[0] // experts), bf16),
            *[pltpu.VMEM((width, per_expert), bf16)] * (experts - 1),
            pltpu.VMEM((per_expert, width), bf16),
            pltpu.SemaphoreType.DMA((experts,)),
            pltpu.SemaphoreType.DMA((experts,)),
        ],
        vmem=24,
        name="experts",
        cost_us=12.0,
    )

    piece = kept // (tp_count * groups)
    own, sends = add(
        [keep, xor_swap(send, "pp", 1)], [piece] * groups, [piece] * (groups * (tp_count - 1)), "sum_cores2"
    )
    final = [stream]
    for g in list(range(1, groups)) + [0]:
        got = [xor_swap(sends[(k - 1) * groups + g], "tp", k) for k in range(1, tp_count)]
        if g == 0 and per_group == 1:
            final += [own[0]] + got
            continue
        kept_rows = own_rows if g == 0 else 0
        mine, out = add(
            [own[g]] + got,
            [own_rows] if g == 0 else [],
            [own_rows] * (per_group - (g == 0)),
            "sum_x%d" % g,
        )
        final += list(mine)
        for j, o in enumerate(out):
            final.append(xor_swap(o, "sec", g * per_group + j + (g == 0)))
    return call(
        functools.partial(add_kernel, 0, len(final)),
        [sds((own_rows, width), bf16)],
        [(VMEM, a) for a in final],
        name="total",
        cost_us=0.2,
    )[0]


def solution(mesh):
    in_specs = (
        P(("groups", "sec"), ("tp", "pp")),
        P(("groups", "sec"), "tp"),
        P(("groups", "sec"), "tp"),
        P(("groups", "sec"), None),
        P(("tp", "pp"), None),
        P(),
        P(("groups", "sec"), None),
        P(("groups", "sec"), None),
        P("groups"),
        P(("tp", "pp"), None, "sec"),
        P(("tp", "pp"), None, "sec"),
        P(("tp", "pp"), "sec", None),
    )
    out_specs = P(("groups", "sec", "tp", "pp"), None)
    return jax.shard_map(
        per_device, mesh=mesh, in_specs=in_specs, out_specs=out_specs, check_vma=False
    )
```

```python
import functools

import jax
import jax.numpy as jnp
from jax import lax
from jax.experimental import pallas as pl
from jax.experimental.pallas import tpu as pltpu
from jax.sharding import PartitionSpec as P

QUERY_HEAD_COUNT = 32
KEY_VALUE_HEADS = 8
HEAD_DIMENSION = 128
E = 8
MOSTB = 32
LANES = 128

neg_fill = -1e30
norm_eps = 1e-05

VMEM = pl.BlockSpec(memory_space=pltpu.VMEM)
SMEM = pl.BlockSpec(memory_space=pltpu.SMEM)
HBM = pl.BlockSpec(memory_space=pltpu.HBM)
ANY = pl.BlockSpec(memory_space=pl.ANY)
MIB = 2**20


def dot(a, b):
    return jnp.dot(a, b, preferred_element_type=jnp.float32)


def xor_swap(x, axis, k):
    n = lax.axis_size(axis)
    return lax.ppermute(x, axis, [(i, i ^ k) for i in range(n)])


def call(kernel, out_shape, args, scratch=(), vmem=8, name=None, cost_us=1.0):
    args = [
        (s, pltpu.with_memory_space_constraint(a, pltpu.HBM) if s is HBM else a) for s, a in args
    ]
    single = not isinstance(out_shape, (tuple, list))
    return pl.pallas_call(
        kernel,
        out_shape=out_shape,
        in_specs=[s for s, _ in args],
        out_specs=VMEM if single else [VMEM] * len(out_shape),
        scratch_shapes=list(scratch),
        compiler_params=pltpu.CompilerParams(vmem_limit_bytes=vmem * MIB),
        cost_estimate=pl.CostEstimate(
            flops=0, bytes_accessed=int(cost_us * 3.4e6), transcendentals=0
        ),
        name=name,
    )(*[a for _, a in args])


def sds(shape, dtype):
    return jax.ShapeDtypeStruct(shape, dtype)


def position():
    rank = lax.axis_index("tp") * lax.axis_size("pp") + lax.axis_index("pp")
    return lax.axis_index("sec"), rank


def columns(source, targets, first=0):
    per = targets[0].shape[1] if targets else 0
    return [(source.at[:, pl.ds((first + i) * per, per)], t) for i, t in enumerate(targets)]


def prepare_kernel(
    back, tp_count, pp_count, lengths_hbm, ids_hbm, codes_hbm, query_hbm, weight_hbm, residual_hbm,
    gain_hbm, *refs
):
    gate_hbm, query_ref, weight_ref, gain_ref, mask_ref, order_ref, residual_ref, info_ref = refs[
        :8
    ]
    gate_refs = refs[8:-5]
    lengths, ids, codes, residual_all, sem = refs[-5:]
    pairs = [
        (lengths_hbm, lengths),
        (ids_hbm, ids),
        (codes_hbm, codes),
        (residual_hbm, residual_all),
        (query_hbm, query_ref),
        (gain_hbm, gain_ref),
        (weight_hbm, weight_ref),
    ] + columns(gate_hbm, gate_refs)
    copies = [pltpu.make_async_copy(a, b, sem.at[i]) for i, (a, b) in enumerate(pairs)]
    for c in copies:
        c.start()
    sec, rank = position()
    block = query_ref.shape[0]
    own_rows = residual_ref.shape[0]
    at = lax.broadcasted_iota(jnp.int32, (block, block), 0)
    to = lax.broadcasted_iota(jnp.int32, (block, block), 1)
    chunk = lax.div(at, own_rows)
    flip = lax.rem(chunk, tp_count) * pp_count + lax.div(chunk, tp_count)
    source = (rank ^ flip) * own_rows + lax.rem(at, own_rows)
    order_ref[...] = jnp.where(to == source, 1.0, 0.0).astype(jnp.bfloat16)
    own = lax.broadcasted_iota(jnp.int32, (own_rows, block), 0) + rank * own_rows
    own = jnp.where(own == lax.broadcasted_iota(jnp.int32, (own_rows, block), 1), 1.0, 0.0)
    own = own.astype(jnp.bfloat16)
    for c in copies[:4]:
        c.wait()
    span = (back + 1) * block
    rows = sec * block + lax.broadcasted_iota(jnp.int32, (block, span), 0)
    cols = (sec - back) * block + lax.broadcasted_iota(jnp.int32, (block, span), 1)
    first = jnp.zeros((block, span), jnp.int32)
    end = jnp.int32(0)
    for d in range(lengths.shape[0]):
        end = end + lengths[d]
        first = jnp.where(rows >= end, end, first)
    mask_ref[...] = jnp.where((cols <= rows) & (cols >= first), 1.0, 0.0)
    residual_ref[...] = dot(own, residual_all[...])
    info = jnp.concatenate(
        [ids[...], codes[...], jnp.zeros((LANES - 4, block), jnp.int32)], axis=0
    ).astype(jnp.float32)
    info_ref[...] = lax.dot_general(
        own, info.astype(jnp.bfloat16), (((1,), (1,)), ((), ())), preferred_element_type=jnp.float32
    ).astype(jnp.bfloat16)
    for c in copies[4:]:
        c.wait()


def load_kernel(first, n_after, source, *refs):
    target, token_ref, sem = refs[n_after:]
    copy = pltpu.make_async_copy(source.at[:, pl.ds(first, target.shape[1])], target, sem)
    copy.start()
    token_ref[...] = jnp.zeros_like(token_ref)
    copy.wait()


def load(array, first, columns, after, name):
    rows = array.shape[0]
    return call(
        functools.partial(load_kernel, first, len(after)),
        [sds((rows, columns), array.dtype), sds((8, LANES), jnp.float32)],
        [(HBM, array)] + [(ANY, a) for a in after],
        scratch=[pltpu.SemaphoreType.DMA],
        vmem=1,
        name=name,
        cost_us=rows * columns * 2 / 3.4e6,
    )


def attention_kernel(back, kv_heads, group, q_ref, mask_ref, order_ref, *refs):
    kv_refs = refs[: back + 1]
    weight_ref, up_hbm, keep_ref, send_ref, up_ref, attended_ref, sem = refs[back + 1 :]
    copy = pltpu.make_async_copy(up_hbm.at[:, pl.ds(0, up_ref.shape[1])], up_ref, sem)
    copy.start()
    block = q_ref.shape[0]
    head = HEAD_DIMENSION
    allowed = jnp.concatenate([mask_ref[...]] * group, axis=0) > 0.5
    for g in range(kv_heads):
        q = jnp.concatenate(
            [q_ref[:, (g * group + t) * head : (g * group + t + 1) * head] for t in range(group)],
            axis=0,
        )
        k = jnp.concatenate([r[:, g * head : (g + 1) * head] for r in kv_refs], axis=0)
        v = jnp.concatenate(
            [r[:, (kv_heads + g) * head : (kv_heads + g + 1) * head] for r in kv_refs], axis=0
        )
        scores = lax.dot_general(
            q, k, (((1,), (1,)), ((), ())), preferred_element_type=jnp.float32
        ) * (head**-0.5)
        scores = jnp.where(allowed, scores, neg_fill)
        top = jnp.max(scores, axis=1, keepdims=True)
        weights = jnp.where(allowed, jnp.exp(scores - top), 0.0)
        total = jnp.sum(weights, axis=1, keepdims=True)
        summed = dot(weights.astype(jnp.bfloat16), v) / total
        for t in range(group):
            attended_ref[:, (g * group + t) * head : (g * group + t + 1) * head] = summed[
                t * block : (t + 1) * block
            ].astype(jnp.bfloat16)
    attended = dot(order_ref[...], attended_ref[...]).astype(jnp.bfloat16)
    mixed = dot(attended, weight_ref[...])
    kept = keep_ref.shape[0]
    keep_ref[...] = mixed[:kept]
    send_ref[...] = mixed[kept:].astype(jnp.bfloat16)
    copy.wait()


def add_kernel(keep_rows, n_in, *refs):
    total = refs[0][...].astype(jnp.float32)
    for r in refs[1:n_in]:
        total = total + r[...].astype(jnp.float32)
    start = 0
    for r in refs[n_in:]:
        r[...] = total[start : start + r.shape[0]].astype(r.dtype)
        start += r.shape[0]


def add(arrays, keep, send, name):
    width = arrays[0].shape[1]
    out = [sds((r, width), jnp.float32) for r in keep]
    out += [sds((r, width), jnp.bfloat16) for r in send]
    out = call(
        functools.partial(add_kernel, sum(keep), len(arrays)),
        out,
        [(VMEM, a) for a in arrays],
        name=name,
        cost_us=0.2,
    )
    return out[: len(keep)], out[len(keep) :]


def norm_kernel(n_parts, residual_ref, gain_ref, info_ref, *refs):
    parts = refs[:n_parts]
    stream_ref, normed_ref = refs[-2:]
    width = residual_ref.shape[1]
    mixed = parts[0][...].astype(jnp.float32)
    for p in parts[1:]:
        mixed = mixed + p[...].astype(jnp.float32)
    stream = residual_ref[...] + mixed
    stream_ref[...] = stream
    meansq = jnp.mean(stream * stream, axis=1, keepdims=True)
    normed_ref[:, :width] = (stream * lax.rsqrt(meansq + norm_eps) * gain_ref[...]).astype(
        jnp.bfloat16
    )
    normed_ref[:, width:] = info_ref[...]


def experts_kernel(experts, capacity, tile, halves, n_rows, *refs):
    rows_in = refs[:n_rows]
    gate_first, up_early, up_late, gate_hbm, up_hbm, down_hbm, keep_ref, send_ref = refs[
        n_rows : n_rows + 8
    ]
    rows_ref, pick_ref, packed_ref, hidden_ref, half_ref, gate_ref, up_ref, down_ref, sem = refs[
        n_rows + 8 :
    ]
    per_expert, width = down_hbm.shape[0] // experts, down_hbm.shape[1]
    early = up_early.shape[1]
    column = min(512, width)
    gates, ups, downs = [], [], []
    for x in range(experts):
        cut = pl.ds(x * per_expert, per_expert)
        downs.append(pltpu.make_async_copy(down_hbm.at[cut], down_ref, sem.at[0, x]))
        if x:
            gates.append(pltpu.make_async_copy(gate_hbm.at[:, cut], gate_ref.at[x - 1], sem.at[1, x]))
            ups.append(pltpu.make_async_copy(up_hbm.at[:, cut], up_ref.at[x - 1], sem.at[2, x]))
    for c in downs[:1] + [c for pair in zip(gates, ups) for c in pair]:
        c.start()
    count = 0
    for r in rows_in:
        rows_ref[count : count + r.shape[0], :] = r[...]
        count += r.shape[0]
    at0 = lax.broadcasted_iota(jnp.int32, (count, count), 0)
    at1 = lax.broadcasted_iota(jnp.int32, (count, count), 1)
    eye = jnp.where(at0 == at1, 1.0, 0.0).astype(jnp.bfloat16)
    before = jnp.where(at0 < at1, 1.0, 0.0).astype(jnp.bfloat16)
    info = lax.dot_general(
        rows_ref[:, width:], eye, (((0,), (0,)), ((), ())), preferred_element_type=jnp.float32
    )
    id0, id1, code0, code1 = (info[i : i + 1, :] for i in range(4))
    slot_of = lax.broadcasted_iota(jnp.int32, (capacity, count), 0).astype(jnp.float32)
    first = lax.axis_index("sec") * experts if halves == 1 else lax.axis_index("sec") // halves
    picks, shares = [], []
    for x in range(experts):
        e = (first + x).astype(jnp.float32)
        hit0 = jnp.where(id0 == e, 1.0, 0.0)
        hit1 = jnp.where(id1 == e, 1.0, 0.0)
        member = hit0 + hit1
        share = (hit0 * code0 + hit1 * code1) / (code0 + code1)
        slot = dot(jnp.broadcast_to(member, (8, count)).astype(jnp.bfloat16), before)[:1]
        slot = jnp.where(member > 0.5, slot, -1.0)
        pick = slot == slot_of
        shares.append(jnp.sum(jnp.where(pick, share, 0.0), axis=1, keepdims=True))
        picks.append(jnp.where(pick, 1.0, 0.0).astype(jnp.bfloat16))
    pick_ref[...] = jnp.concatenate(picks, axis=0)
    column = min(512, width)

    for c in range(0, width, column):
        packed_ref[:, c : c + column] = dot(pick_ref[...], rows_ref[:, c : c + column]).astype(
            jnp.bfloat16
        )
    for x in range(experts):
        mine = slice(x * capacity, (x + 1) * capacity)
        if x:
            gates[x - 1].wait()
        for s in range(0, per_expert, tile):
            cut = slice(s, s + tile)
            gate = dot(packed_ref[mine, :], gate_ref[x - 1, :, cut] if x else gate_first[:, cut])
            half = 0.5 * gate
            half_ref[:, cut] = half + half * jnp.tanh(half)
        if x:
            ups[x - 1].wait()
        for s in range(0, per_expert, tile):
            cut = slice(s, s + tile)
            if x:
                weight = up_ref[x - 1, :, cut]
            elif s < early:
                weight = up_early[:, cut]
            else:
                weight = up_late[:, s - early : s - early + tile]
            up = dot(packed_ref[mine, :], weight)
            hidden_ref[mine, cut] = (half_ref[:, cut] * up).astype(jnp.bfloat16)
        downs[x].wait()
        for c in range(0, width, column):
            out = dot(hidden_ref[mine, :], down_ref[:, c : c + column])
            packed_ref[mine, c : c + column] = (out * shares[x]).astype(jnp.bfloat16)
        if x + 1 < experts:
            downs[x + 1].start()
    kept = keep_ref.shape[0]

    for c in range(0, width, column):
        out = lax.dot_general(
            pick_ref[...], packed_ref[:, c : c + column], (((0,), (0,)), ((), ())),
            preferred_element_type=jnp.float32,
        )
        keep_ref[:, c : c + column] = out[:kept]
        send_ref[:, c : c + column] = out[kept:].astype(jnp.bfloat16)


def per_device(
    query,
    keys,
    values,
    residual,
    out_weight,
    norm_gain,
    expert_ids,
    gate_codes,
    doc_lengths,
    w_gate,
    w_up,
    w_down,
):
    block, width = residual.shape
    head = HEAD_DIMENSION
    group_width = QUERY_HEAD_COUNT // KEY_VALUE_HEADS
    q_heads = query.shape[1] // head
    sec_count, tp_count, pp_count = (lax.axis_size(a) for a in ("sec", "tp", "pp"))
    own_rows = block // (tp_count * pp_count)
    bf16, f32 = jnp.bfloat16, jnp.float32

    kv_heads = max(1, q_heads // group_width)
    group = q_heads // kv_heads
    kv_start = lax.axis_index("pp") * q_heads // group_width * head
    kv = jnp.concatenate(
        [lax.dynamic_slice_in_dim(a, kv_start, kv_heads * head, 1) for a in (keys, values)], axis=1
    )
    back = -(-(sec_count * block // 2 - 1) // block)
    pieces = [
        lax.ppermute(kv, "sec", [(i, i + k) for i in range(sec_count - k)])
        for k in range(back, 0, -1)
    ] + [kv]

    experts = max(1, E // sec_count)
    per_expert = w_gate.shape[2] // experts
    span = (back + 1) * block
    query_v, weight_v, gain_v, mask, order, residual_own, info, *gate_v = call(
        functools.partial(prepare_kernel, back, tp_count, pp_count),
        [
            sds(query.shape, bf16),
            sds(out_weight.shape, bf16),
            sds((1, width), f32),
            sds((block, span), f32),
            sds((block, block), bf16),
            sds((own_rows, width), f32),
            sds((own_rows, LANES), bf16),
        ]
        + [sds((width, per_expert), bf16)],
        [
            (HBM, a)
            for a in (
                doc_lengths, expert_ids.T, gate_codes.T, query, out_weight, residual,
                norm_gain.reshape(1, width), w_gate[0],
            )
        ],
        scratch=[
            pltpu.SMEM(doc_lengths.shape, jnp.int32),
            pltpu.VMEM((2, block), jnp.int32),
            pltpu.VMEM((2, block), jnp.int32),
            pltpu.VMEM(residual.shape, bf16),
            pltpu.SemaphoreType.DMA((8,)),
        ],
        vmem=6,
        name="prepare",
        cost_us=4.0,
    )
    half = block // pp_count
    early = max(LANES, per_expert // 2)
    keep, send, up_early = call(
        functools.partial(attention_kernel, back, kv_heads, group),
        [sds((half, width), f32), sds((block - half, width), bf16), sds((width, early), bf16)],
        [(VMEM, a) for a in (query_v, mask, order, *pieces, weight_v)] + [(HBM, w_up[0])],
        scratch=[pltpu.VMEM(query.shape, bf16), pltpu.SemaphoreType.DMA],
        name="attention",
        cost_us=2.4,
    )

    (own,), sends = add(
        [keep] + [xor_swap(send, "pp", 1)], [own_rows], [own_rows] * (tp_count - 1), "sum_cores"
    )
    got = [xor_swap(sends[k - 1], "tp", k) for k in range(1, tp_count)]
    up_late, token = load(w_up[0], early, per_expert - early, [own], "load_up")
    stream, normed = call(
        functools.partial(norm_kernel, tp_count),
        [sds((own_rows, width), f32), sds((own_rows, width + LANES), bf16)],
        [(VMEM, a) for a in (residual_own, gain_v, info, own, *got)] + [(ANY, token)],
        name="norm",
        cost_us=0.2,
    )

    groups = min(4, sec_count)
    near = [normed] + [xor_swap(normed, "sec", k) for k in range(1, sec_count)]
    per_group = sec_count // groups
    near = [
        jnp.concatenate(near[g * per_group : (g + 1) * per_group], axis=0)
        if per_group > 1
        else near[g]
        for g in range(groups)
    ]
    rows = [[r] + [xor_swap(r, "tp", k) for k in range(1, tp_count)] for r in near]
    rows = [rows[g][k] for k in range(tp_count) for g in range(groups)]
    rows = rows + [xor_swap(r, "pp", k) for k in range(1, pp_count) for r in rows]

    halves = max(1, sec_count // E)
    count = sec_count * block
    capacity = sec_count * MOSTB
    down = w_down[0]
    tile = min(512, early, per_expert - early)
    kept = count // pp_count
    keep, send = call(
        functools.partial(experts_kernel, experts, capacity, tile, halves, len(rows)),
        [sds((kept, width), f32), sds((count - kept, width), bf16)],
        [(VMEM, a) for a in (*rows, *gate_v, up_early, up_late)]
        + [(HBM, a) for a in (w_gate[0], w_up[0], down)],
        scratch=[
            pltpu.VMEM((count, width + LANES), bf16),
            pltpu.VMEM((experts * capacity, count), bf16),
            pltpu.VMEM((experts * capacity, width), bf16),
            pltpu.VMEM((experts * capacity, down.shape[0] // experts), bf16),
            pltpu.VMEM((capacity, per_expert), f32),
            pltpu.VMEM((max(1, experts - 1), width, per_expert), bf16),
            pltpu.VMEM((max(1, experts - 1), width, per_expert), bf16),
            pltpu.VMEM((per_expert, width), bf16),
            pltpu.SemaphoreType.DMA((3, experts)),
        ],
        vmem=33,
        name="experts",
        cost_us=12.0,
    )

    piece = kept // (tp_count * groups)
    own, sends = add(
        [keep, xor_swap(send, "pp", 1)], [piece] * groups, [piece] * (groups * (tp_count - 1)), "sum_cores2"
    )
    final = [stream]
    for g in list(range(1, groups)) + [0]:
        got = [xor_swap(sends[(k - 1) * groups + g], "tp", k) for k in range(1, tp_count)]
        if g == 0 and per_group == 1:
            final += [own[0]] + got
            continue
        kept_rows = own_rows if g == 0 else 0
        mine, out = add(
            [own[g]] + got,
            [own_rows] if g == 0 else [],
            [own_rows] * (per_group - (g == 0)),
            "sum_x%d" % g,
        )
        final += list(mine)
        for j, o in enumerate(out):
            final.append(xor_swap(o, "sec", g * per_group + j + (g == 0)))
    return call(
        functools.partial(add_kernel, 0, len(final)),
        [sds((own_rows, width), bf16)],
        [(VMEM, a) for a in final],
        name="total",
        cost_us=0.2,
    )[0]


def solution(mesh):
    in_specs = (
        P(("groups", "sec"), ("tp", "pp")),
        P(("groups", "sec"), "tp"),
        P(("groups", "sec"), "tp"),
        P(("groups", "sec"), None),
        P(("tp", "pp"), None),
        P(),
        P(("groups", "sec"), None),
        P(("groups", "sec"), None),
        P("groups"),
        P(("tp", "pp"), None, "sec"),
        P(("tp", "pp"), None, "sec"),
        P(("tp", "pp"), "sec", None),
    )
    out_specs = P(("groups", "sec", "tp", "pp"), None)
    return jax.shard_map(
        per_device, mesh=mesh, in_specs=in_specs, out_specs=out_specs, check_vma=False
    )
```

```python
import functools

import jax
import jax.numpy as jnp
from jax import lax
from jax.experimental import pallas as pl
from jax.experimental.pallas import tpu as pltpu
from jax.sharding import PartitionSpec as P

QUERY_HEAD_COUNT = 32
KEY_VALUE_HEADS = 8
HEAD_DIMENSION = 128
E = 8
MOSTB = 32
LANES = 128

neg_fill = -1e30
norm_eps = 1e-05

VMEM = pl.BlockSpec(memory_space=pltpu.VMEM)
SMEM = pl.BlockSpec(memory_space=pltpu.SMEM)
HBM = pl.BlockSpec(memory_space=pltpu.HBM)
ANY = pl.BlockSpec(memory_space=pl.ANY)
MIB = 2**20


def dot(a, b):
    return jnp.dot(a, b, preferred_element_type=jnp.float32)


def xor_swap(x, axis, k):
    n = lax.axis_size(axis)
    return lax.ppermute(x, axis, [(i, i ^ k) for i in range(n)])


def call(kernel, out_shape, args, scratch=(), vmem=8, name=None, cost_us=1.0):
    args = [
        (s, pltpu.with_memory_space_constraint(a, pltpu.HBM) if s is HBM else a) for s, a in args
    ]
    single = not isinstance(out_shape, (tuple, list))
    return pl.pallas_call(
        kernel,
        out_shape=out_shape,
        in_specs=[s for s, _ in args],
        out_specs=VMEM if single else [VMEM] * len(out_shape),
        scratch_shapes=list(scratch),
        compiler_params=pltpu.CompilerParams(vmem_limit_bytes=vmem * MIB),
        cost_estimate=pl.CostEstimate(
            flops=0, bytes_accessed=int(cost_us * 3.4e6), transcendentals=0
        ),
        name=name,
    )(*[a for _, a in args])


def sds(shape, dtype):
    return jax.ShapeDtypeStruct(shape, dtype)


def position():
    rank = lax.axis_index("tp") * lax.axis_size("pp") + lax.axis_index("pp")
    return lax.axis_index("sec"), rank


def columns(source, targets, first=0):
    per = targets[0].shape[1] if targets else 0
    return [(source.at[:, pl.ds((first + i) * per, per)], t) for i, t in enumerate(targets)]


def prepare_kernel(
    back, tp_count, pp_count, lengths_hbm, ids_hbm, codes_hbm, query_hbm, weight_hbm, residual_hbm,
    gain_hbm, *refs
):
    gate_hbm, query_ref, weight_ref, gain_ref, mask_ref, order_ref, residual_ref, info_ref = refs[
        :8
    ]
    gate_refs = refs[8:-5]
    lengths, ids, codes, residual_all, sem = refs[-5:]
    pairs = [
        (lengths_hbm, lengths),
        (ids_hbm, ids),
        (codes_hbm, codes),
        (residual_hbm, residual_all),
        (query_hbm, query_ref),
        (gain_hbm, gain_ref),
        (weight_hbm, weight_ref),
    ] + columns(gate_hbm, gate_refs)
    copies = [pltpu.make_async_copy(a, b, sem.at[i]) for i, (a, b) in enumerate(pairs)]
    for c in copies:
        c.start()
    sec, rank = position()
    block = query_ref.shape[0]
    own_rows = residual_ref.shape[0]
    at = lax.broadcasted_iota(jnp.int32, (block, block), 0)
    to = lax.broadcasted_iota(jnp.int32, (block, block), 1)
    chunk = lax.div(at, own_rows)
    flip = lax.rem(chunk, tp_count) * pp_count + lax.div(chunk, tp_count)
    source = (rank ^ flip) * own_rows + lax.rem(at, own_rows)
    order_ref[...] = jnp.where(to == source, 1.0, 0.0).astype(jnp.bfloat16)
    own = lax.broadcasted_iota(jnp.int32, (own_rows, block), 0) + rank * own_rows
    own = jnp.where(own == lax.broadcasted_iota(jnp.int32, (own_rows, block), 1), 1.0, 0.0)
    own = own.astype(jnp.bfloat16)
    for c in copies[:4]:
        c.wait()
    span = (back + 1) * block
    rows = sec * block + lax.broadcasted_iota(jnp.int32, (block, span), 0)
    cols = (sec - back) * block + lax.broadcasted_iota(jnp.int32, (block, span), 1)
    first = jnp.zeros((block, span), jnp.int32)
    end = jnp.int32(0)
    for d in range(lengths.shape[0]):
        end = end + lengths[d]
        first = jnp.where(rows >= end, end, first)
    mask_ref[...] = jnp.where((cols <= rows) & (cols >= first), 1.0, 0.0)
    residual_ref[...] = dot(own, residual_all[...])
    info = jnp.concatenate(
        [ids[...], codes[...], jnp.zeros((LANES - 4, block), jnp.int32)], axis=0
    ).astype(jnp.float32)
    info_ref[...] = lax.dot_general(
        own, info.astype(jnp.bfloat16), (((1,), (1,)), ((), ())), preferred_element_type=jnp.float32
    ).astype(jnp.bfloat16)
    for c in copies[4:]:
        c.wait()


def load_kernel(n_after, source, *refs):
    *targets, token_ref, sem = refs[n_after:]
    copies = [
        pltpu.make_async_copy(a, b, sem.at[i])
        for i, (a, b) in enumerate(columns(source, targets))
    ]
    for c in copies:
        c.start()
    token_ref[...] = jnp.zeros_like(token_ref)
    for c in copies:
        c.wait()


def load(array, parts, wanted, after, name):
    rows, cols = array.shape
    out = call(
        functools.partial(load_kernel, len(after)),
        [sds((rows, cols // parts), array.dtype)] * wanted + [sds((8, LANES), jnp.float32)],
        [(HBM, array)] + [(ANY, a) for a in after],
        scratch=[pltpu.SemaphoreType.DMA((wanted,))],
        vmem=1,
        name=name,
        cost_us=array.size * wanted / parts * 2 / 3.4e6,
    )
    return out[:-1], out[-1]


def attention_kernel(back, kv_heads, group, q_ref, mask_ref, order_ref, *refs):
    kv_refs = refs[: back + 1]
    weight_ref, keep_ref, send_ref, attended_ref = refs[back + 1 :]
    block = q_ref.shape[0]
    head = HEAD_DIMENSION
    allowed = jnp.concatenate([mask_ref[...]] * group, axis=0) > 0.5
    for g in range(kv_heads):
        q = jnp.concatenate(
            [q_ref[:, (g * group + t) * head : (g * group + t + 1) * head] for t in range(group)],
            axis=0,
        )
        k = jnp.concatenate([r[:, g * head : (g + 1) * head] for r in kv_refs], axis=0)
        v = jnp.concatenate(
            [r[:, (kv_heads + g) * head : (kv_heads + g + 1) * head] for r in kv_refs], axis=0
        )
        scores = lax.dot_general(
            q, k, (((1,), (1,)), ((), ())), preferred_element_type=jnp.float32
        ) * (head**-0.5)
        scores = jnp.where(allowed, scores, neg_fill)
        top = jnp.max(scores, axis=1, keepdims=True)
        weights = jnp.where(allowed, jnp.exp(scores - top), 0.0)
        total = jnp.sum(weights, axis=1, keepdims=True)
        summed = dot(weights.astype(jnp.bfloat16), v) / total
        for t in range(group):
            attended_ref[:, (g * group + t) * head : (g * group + t + 1) * head] = summed[
                t * block : (t + 1) * block
            ].astype(jnp.bfloat16)
    attended = dot(order_ref[...], attended_ref[...]).astype(jnp.bfloat16)
    mixed = dot(attended, weight_ref[...])
    kept = keep_ref.shape[0]
    keep_ref[...] = mixed[:kept]
    send_ref[...] = mixed[kept:].astype(jnp.bfloat16)


def add_kernel(keep_rows, n_in, *refs):
    total = refs[0][...].astype(jnp.float32)
    for r in refs[1:n_in]:
        total = total + r[...].astype(jnp.float32)
    start = 0
    for r in refs[n_in:]:
        r[...] = total[start : start + r.shape[0]].astype(r.dtype)
        start += r.shape[0]


def add(arrays, keep, send, name):
    width = arrays[0].shape[1]
    out = [sds((r, width), jnp.float32) for r in keep]
    out += [sds((r, width), jnp.bfloat16) for r in send]
    out = call(
        functools.partial(add_kernel, sum(keep), len(arrays)),
        out,
        [(VMEM, a) for a in arrays],
        name=name,
        cost_us=0.2,
    )
    return out[: len(keep)], out[len(keep) :]


def norm_kernel(n_parts, residual_ref, gain_ref, info_ref, *refs):
    parts = refs[:n_parts]
    stream_ref, normed_ref = refs[-2:]
    width = residual_ref.shape[1]
    mixed = parts[0][...].astype(jnp.float32)
    for p in parts[1:]:
        mixed = mixed + p[...].astype(jnp.float32)
    stream = residual_ref[...] + mixed
    stream_ref[...] = stream
    meansq = jnp.mean(stream * stream, axis=1, keepdims=True)
    normed_ref[:, :width] = (stream * lax.rsqrt(meansq + norm_eps) * gain_ref[...]).astype(
        jnp.bfloat16
    )
    normed_ref[:, width:] = info_ref[...]


def experts_kernel(experts, tile, halves, n_rows, n_gate, n_up, *refs):
    rows_in = refs[:n_rows]
    gate_refs = list(refs[n_rows : n_rows + n_gate])
    up_refs = list(refs[n_rows + n_gate : n_rows + n_gate + n_up])
    refs = refs[n_rows + n_gate + n_up :]
    up_hbm, down_hbm, keep_ref, send_ref, rows_ref, sum_ref, hidden_ref = refs[:7]
    up_late = list(refs[7 : 7 + experts - n_up])
    down_ref, up_sem, down_sem = refs[7 + experts - n_up :]
    per_expert, width = down_hbm.shape[0] // experts, down_hbm.shape[1]
    up_copies = [
        pltpu.make_async_copy(a, b, up_sem.at[i])
        for i, (a, b) in enumerate(columns(up_hbm, up_late, n_up))
    ]
    up_refs += up_late
    down_copies = [
        pltpu.make_async_copy(
            down_hbm.at[pl.ds(x * per_expert, per_expert)], down_ref, down_sem.at[x]
        )
        for x in range(experts)
    ]
    for c in down_copies[:1] + up_copies:
        c.start()
    count = 0
    for r in rows_in:
        rows_ref[count : count + r.shape[0], :] = r[...]
        count += r.shape[0]
    info = rows_ref[:, width:].astype(jnp.float32)
    id0, id1, code0, code1 = (info[:, i : i + 1] for i in range(4))
    first = lax.axis_index("sec") * experts if halves == 1 else lax.axis_index("sec") // halves
    kept = keep_ref.shape[0]
    column = min(512, width)
    for x in range(experts):
        e = (first + x).astype(jnp.float32)
        named = jnp.where(id0 == e, code0, 0.0) + jnp.where(id1 == e, code1, 0.0)
        share = 0.5 * named / (code0 + code1)
        if x >= n_up:
            up_copies[x - n_up].wait()
        gate_ref, up_ref = gate_refs[x], up_refs[x]
        for s in range(0, per_expert, tile):
            cut = slice(s, s + tile)
            gate = dot(rows_ref[:, :width], gate_ref[:, cut])
            up = dot(rows_ref[:, :width], up_ref[:, cut]) * share
            hidden_ref[:, cut] = ((gate + gate * jnp.tanh(0.5 * gate)) * up).astype(jnp.bfloat16)
        down_copies[x].wait()
        for c in range(0, width, column):
            cut = slice(c, c + column)
            out = dot(hidden_ref[...], down_ref[:, cut])
            if x:
                out = out + sum_ref[:, cut]
            if x + 1 < experts:
                sum_ref[:, cut] = out
            else:
                keep_ref[:, cut] = out[:kept]
                send_ref[:, cut] = out[kept:].astype(jnp.bfloat16)
        if x + 1 < experts:
            down_copies[x + 1].start()


def per_device(
    query,
    keys,
    values,
    residual,
    out_weight,
    norm_gain,
    expert_ids,
    gate_codes,
    doc_lengths,
    w_gate,
    w_up,
    w_down,
):
    block, width = residual.shape
    head = HEAD_DIMENSION
    group_width = QUERY_HEAD_COUNT // KEY_VALUE_HEADS
    q_heads = query.shape[1] // head
    sec_count, tp_count, pp_count = (lax.axis_size(a) for a in ("sec", "tp", "pp"))
    own_rows = block // (tp_count * pp_count)
    bf16, f32 = jnp.bfloat16, jnp.float32

    kv_heads = max(1, q_heads // group_width)
    group = q_heads // kv_heads
    kv_start = lax.axis_index("pp") * q_heads // group_width * head
    kv = jnp.concatenate(
        [lax.dynamic_slice_in_dim(a, kv_start, kv_heads * head, 1) for a in (keys, values)], axis=1
    )
    back = -(-(sec_count * block // 2 - 1) // block)
    pieces = [
        lax.ppermute(kv, "sec", [(i, i + k) for i in range(sec_count - k)])
        for k in range(back, 0, -1)
    ] + [kv]

    experts = max(1, E // sec_count)
    per_expert = w_gate.shape[2] // experts
    span = (back + 1) * block
    query_v, weight_v, gain_v, mask, order, residual_own, info, *gate_v = call(
        functools.partial(prepare_kernel, back, tp_count, pp_count),
        [
            sds(query.shape, bf16),
            sds(out_weight.shape, bf16),
            sds((1, width), f32),
            sds((block, span), f32),
            sds((block, block), bf16),
            sds((own_rows, width), f32),
            sds((own_rows, LANES), bf16),
        ]
        + [sds((width, per_expert), bf16)] * experts,
        [
            (HBM, a)
            for a in (
                doc_lengths, expert_ids.T, gate_codes.T, query, out_weight, residual,
                norm_gain.reshape(1, width), w_gate[0],
            )
        ],
        scratch=[
            pltpu.SMEM(doc_lengths.shape, jnp.int32),
            pltpu.VMEM((2, block), jnp.int32),
            pltpu.VMEM((2, block), jnp.int32),
            pltpu.VMEM(residual.shape, bf16),
            pltpu.SemaphoreType.DMA((7 + experts,)),
        ],
        vmem=6,
        name="prepare",
        cost_us=6.0,
    )
    half = block // pp_count
    keep, send = call(
        functools.partial(attention_kernel, back, kv_heads, group),
        [sds((half, width), f32), sds((block - half, width), bf16)],
        [(VMEM, a) for a in (query_v, mask, order, *pieces, weight_v)],
        scratch=[pltpu.VMEM(query.shape, bf16)],
        name="attention",
        cost_us=2.4,
    )

    (own,), sends = add(
        [keep] + [xor_swap(send, "pp", 1)], [own_rows], [own_rows] * (tp_count - 1), "sum_cores"
    )
    got = [xor_swap(sends[k - 1], "tp", k) for k in range(1, tp_count)]
    up_v, token = load(w_up[0], experts, 1, [own], "load_up")
    stream, normed = call(
        functools.partial(norm_kernel, tp_count),
        [sds((own_rows, width), f32), sds((own_rows, width + LANES), bf16)],
        [(VMEM, a) for a in (residual_own, gain_v, info, own, *got)] + [(ANY, token)],
        name="norm",
        cost_us=0.2,
    )

    groups = min(4, sec_count)
    near = [normed] + [xor_swap(normed, "sec", k) for k in range(1, sec_count)]
    per_group = sec_count // groups
    near = [
        jnp.concatenate(near[g * per_group : (g + 1) * per_group], axis=0)
        if per_group > 1
        else near[g]
        for g in range(groups)
    ]
    rows = [[r] + [xor_swap(r, "tp", k) for k in range(1, tp_count)] for r in near]
    rows = [rows[g][k] for k in range(tp_count) for g in range(groups)]
    rows = rows + [xor_swap(r, "pp", k) for k in range(1, pp_count) for r in rows]

    halves = max(1, sec_count // E)
    count = sec_count * block
    down = w_down[0]
    tile = min(512, down.shape[0] // experts)
    kept = count // pp_count
    keep, send = call(
        functools.partial(experts_kernel, experts, tile, halves, len(rows), experts, 1),
        [sds((kept, width), f32), sds((count - kept, width), bf16)],
        [(VMEM, a) for a in (*rows, *gate_v, *up_v)] + [(HBM, w_up[0]), (HBM, down)],
        scratch=[
            pltpu.VMEM((count, width + LANES), bf16),
            pltpu.VMEM((count, width), f32),
            pltpu.VMEM((count, per_expert), bf16),
            *[pltpu.VMEM((width, per_expert), bf16)] * (experts - 1),
            pltpu.VMEM((per_expert, width), bf16),
            pltpu.SemaphoreType.DMA((experts,)),
            pltpu.SemaphoreType.DMA((experts,)),
        ],
        vmem=24,
        name="experts",
        cost_us=12.0,
    )

    piece = kept // (tp_count * groups)
    own, sends = add(
        [keep, xor_swap(send, "pp", 1)], [piece] * groups, [piece] * (groups * (tp_count - 1)), "sum_cores2"
    )
    final = [stream]
    for g in list(range(1, groups)) + [0]:
        got = [xor_swap(sends[(k - 1) * groups + g], "tp", k) for k in range(1, tp_count)]
        if g == 0 and per_group == 1:
            final += [own[0]] + got
            continue
        kept_rows = own_rows if g == 0 else 0
        mine, out = add(
            [own[g]] + got,
            [own_rows] if g == 0 else [],
            [own_rows] * (per_group - (g == 0)),
            "sum_x%d" % g,
        )
        final += list(mine)
        for j, o in enumerate(out):
            final.append(xor_swap(o, "sec", g * per_group + j + (g == 0)))
    return call(
        functools.partial(add_kernel, 0, len(final)),
        [sds((own_rows, width), bf16)],
        [(VMEM, a) for a in final],
        name="total",
        cost_us=0.2,
    )[0]


def solution(mesh):
    in_specs = (
        P(("groups", "sec"), ("tp", "pp")),
        P(("groups", "sec"), "tp"),
        P(("groups", "sec"), "tp"),
        P(("groups", "sec"), None),
        P(("tp", "pp"), None),
        P(),
        P(("groups", "sec"), None),
        P(("groups", "sec"), None),
        P("groups"),
        P(("tp", "pp"), None, "sec"),
        P(("tp", "pp"), None, "sec"),
        P(("tp", "pp"), "sec", None),
    )
    out_specs = P(("groups", "sec", "tp", "pp"), None)
    return jax.shard_map(
        per_device, mesh=mesh, in_specs=in_specs, out_specs=out_specs, check_vma=False
    )
```

```python
import functools

import jax
import jax.numpy as jnp
from jax import lax
from jax.experimental import pallas as pl
from jax.experimental.pallas import tpu as pltpu
from jax.sharding import PartitionSpec as P

QUERY_HEAD_COUNT = 32
KEY_VALUE_HEADS = 8
HEAD_DIMENSION = 128
E = 8
MOSTB = 32
LANES = 128

neg_fill = -1e30
norm_eps = 1e-05

VMEM = pl.BlockSpec(memory_space=pltpu.VMEM)
SMEM = pl.BlockSpec(memory_space=pltpu.SMEM)
HBM = pl.BlockSpec(memory_space=pltpu.HBM)
ANY = pl.BlockSpec(memory_space=pl.ANY)
MIB = 2**20


def dot(a, b):
    return jnp.dot(a, b, preferred_element_type=jnp.float32)


def xor_swap(x, axis, k):
    n = lax.axis_size(axis)
    return lax.ppermute(x, axis, [(i, i ^ k) for i in range(n)])


def call(kernel, out_shape, args, scratch=(), vmem=8, name=None, cost_us=1.0):
    args = [
        (s, pltpu.with_memory_space_constraint(a, pltpu.HBM) if s is HBM else a) for s, a in args
    ]
    single = not isinstance(out_shape, (tuple, list))
    return pl.pallas_call(
        kernel,
        out_shape=out_shape,
        in_specs=[s for s, _ in args],
        out_specs=VMEM if single else [VMEM] * len(out_shape),
        scratch_shapes=list(scratch),
        compiler_params=pltpu.CompilerParams(vmem_limit_bytes=vmem * MIB),
        cost_estimate=pl.CostEstimate(
            flops=0, bytes_accessed=int(cost_us * 3.4e6), transcendentals=0
        ),
        name=name,
    )(*[a for _, a in args])


def sds(shape, dtype):
    return jax.ShapeDtypeStruct(shape, dtype)


def position():
    rank = lax.axis_index("tp") * lax.axis_size("pp") + lax.axis_index("pp")
    return lax.axis_index("sec"), rank


def columns(source, targets, first=0):
    per = targets[0].shape[1] if targets else 0
    return [(source.at[:, pl.ds((first + i) * per, per)], t) for i, t in enumerate(targets)]


def prepare_kernel(
    back, tp_count, pp_count, lengths_hbm, ids_hbm, codes_hbm, query_hbm, weight_hbm, residual_hbm,
    gain_hbm, *refs
):
    gate_hbm, query_ref, weight_ref, gain_ref, mask_ref, order_ref, residual_ref, info_ref = refs[
        :8
    ]
    gate_refs = refs[8:-5]
    lengths, ids, codes, residual_all, sem = refs[-5:]
    pairs = [
        (lengths_hbm, lengths),
        (ids_hbm, ids),
        (codes_hbm, codes),
        (residual_hbm, residual_all),
        (query_hbm, query_ref),
        (gain_hbm, gain_ref),
        (weight_hbm, weight_ref),
    ] + columns(gate_hbm, gate_refs)
    copies = [pltpu.make_async_copy(a, b, sem.at[i]) for i, (a, b) in enumerate(pairs)]
    for c in copies:
        c.start()
    sec, rank = position()
    block = query_ref.shape[0]
    own_rows = residual_ref.shape[0]
    at = lax.broadcasted_iota(jnp.int32, (block, block), 0)
    to = lax.broadcasted_iota(jnp.int32, (block, block), 1)
    chunk = lax.div(at, own_rows)
    flip = lax.rem(chunk, tp_count) * pp_count + lax.div(chunk, tp_count)
    source = (rank ^ flip) * own_rows + lax.rem(at, own_rows)
    order_ref[...] = jnp.where(to == source, 1.0, 0.0).astype(jnp.bfloat16)
    own = lax.broadcasted_iota(jnp.int32, (own_rows, block), 0) + rank * own_rows
    own = jnp.where(own == lax.broadcasted_iota(jnp.int32, (own_rows, block), 1), 1.0, 0.0)
    own = own.astype(jnp.bfloat16)
    for c in copies[:4]:
        c.wait()
    span = (back + 1) * block
    rows = sec * block + lax.broadcasted_iota(jnp.int32, (block, span), 0)
    cols = (sec - back) * block + lax.broadcasted_iota(jnp.int32, (block, span), 1)
    first = jnp.zeros((block, span), jnp.int32)
    end = jnp.int32(0)
    for d in range(lengths.shape[0]):
        end = end + lengths[d]
        first = jnp.where(rows >= end, end, first)
    mask_ref[...] = jnp.where((cols <= rows) & (cols >= first), 1.0, 0.0)
    residual_ref[...] = dot(own, residual_all[...])
    info = jnp.concatenate(
        [ids[...], codes[...], jnp.zeros((LANES - 4, block), jnp.int32)], axis=0
    ).astype(jnp.float32)
    info_ref[...] = lax.dot_general(
        own, info.astype(jnp.bfloat16), (((1,), (1,)), ((), ())), preferred_element_type=jnp.float32
    ).astype(jnp.bfloat16)
    for c in copies[4:]:
        c.wait()


def load_kernel(n_after, source, *refs):
    *targets, token_ref, sem = refs[n_after:]
    copies = [
        pltpu.make_async_copy(a, b, sem.at[i])
        for i, (a, b) in enumerate(columns(source, targets))
    ]
    for c in copies:
        c.start()
    token_ref[...] = jnp.zeros_like(token_ref)
    for c in copies:
        c.wait()


def load(array, parts, wanted, after, name):
    rows, cols = array.shape
    out = call(
        functools.partial(load_kernel, len(after)),
        [sds((rows, cols // parts), array.dtype)] * wanted + [sds((8, LANES), jnp.float32)],
        [(HBM, array)] + [(ANY, a) for a in after],
        scratch=[pltpu.SemaphoreType.DMA((wanted,))],
        vmem=1,
        name=name,
        cost_us=array.size * wanted / parts * 2 / 3.4e6,
    )
    return out[:-1], out[-1]


def attention_kernel(back, kv_heads, group, q_ref, mask_ref, order_ref, *refs):
    kv_refs = refs[: back + 1]
    weight_ref, keep_ref, send_ref, attended_ref = refs[back + 1 :]
    block = q_ref.shape[0]
    head = HEAD_DIMENSION
    allowed = jnp.concatenate([mask_ref[...]] * group, axis=0) > 0.5
    for g in range(kv_heads):
        q = jnp.concatenate(
            [q_ref[:, (g * group + t) * head : (g * group + t + 1) * head] for t in range(group)],
            axis=0,
        )
        k = jnp.concatenate([r[:, g * head : (g + 1) * head] for r in kv_refs], axis=0)
        v = jnp.concatenate(
            [r[:, (kv_heads + g) * head : (kv_heads + g + 1) * head] for r in kv_refs], axis=0
        )
        scores = lax.dot_general(
            q, k, (((1,), (1,)), ((), ())), preferred_element_type=jnp.float32
        ) * (head**-0.5)
        scores = jnp.where(allowed, scores, neg_fill)
        top = jnp.max(scores, axis=1, keepdims=True)
        weights = jnp.where(allowed, jnp.exp(scores - top), 0.0)
        total = jnp.sum(weights, axis=1, keepdims=True)
        summed = dot(weights.astype(jnp.bfloat16), v) / total
        for t in range(group):
            attended_ref[:, (g * group + t) * head : (g * group + t + 1) * head] = summed[
                t * block : (t + 1) * block
            ].astype(jnp.bfloat16)
    attended = dot(order_ref[...], attended_ref[...]).astype(jnp.bfloat16)
    mixed = dot(attended, weight_ref[...])
    kept = keep_ref.shape[0]
    keep_ref[...] = mixed[:kept]
    send_ref[...] = mixed[kept:].astype(jnp.bfloat16)


def add_kernel(keep_rows, n_in, *refs):
    total = refs[0][...].astype(jnp.float32)
    for r in refs[1:n_in]:
        total = total + r[...].astype(jnp.float32)
    start = 0
    for r in refs[n_in:]:
        r[...] = total[start : start + r.shape[0]].astype(r.dtype)
        start += r.shape[0]


def add(arrays, keep, send, name):
    width = arrays[0].shape[1]
    out = [sds((r, width), jnp.float32) for r in keep]
    out += [sds((r, width), jnp.bfloat16) for r in send]
    out = call(
        functools.partial(add_kernel, sum(keep), len(arrays)),
        out,
        [(VMEM, a) for a in arrays],
        name=name,
        cost_us=0.2,
    )
    return out[: len(keep)], out[len(keep) :]


def norm_kernel(n_parts, residual_ref, gain_ref, info_ref, *refs):
    parts = refs[:n_parts]
    stream_ref, normed_ref = refs[-2:]
    width = residual_ref.shape[1]
    mixed = parts[0][...].astype(jnp.float32)
    for p in parts[1:]:
        mixed = mixed + p[...].astype(jnp.float32)
    stream = residual_ref[...] + mixed
    stream_ref[...] = stream
    meansq = jnp.mean(stream * stream, axis=1, keepdims=True)
    normed_ref[:, :width] = (stream * lax.rsqrt(meansq + norm_eps) * gain_ref[...]).astype(
        jnp.bfloat16
    )
    normed_ref[:, width:] = info_ref[...]


def experts_kernel(experts, capacity, tile, halves, n_rows, n_gate, n_up, *refs):
    rows_in = refs[:n_rows]
    gate_refs = list(refs[n_rows : n_rows + n_gate])
    up_refs = list(refs[n_rows + n_gate : n_rows + n_gate + n_up])
    refs = refs[n_rows + n_gate + n_up :]
    up_hbm, down_hbm, keep_ref, send_ref, rows_ref, pick_ref, packed_ref, hidden_ref = refs[:8]
    up_late = list(refs[8 : 8 + experts - n_up])
    down_ref, up_sem, down_sem = refs[8 + experts - n_up :]
    per_expert, width = down_hbm.shape[0] // experts, down_hbm.shape[1]
    up_copies = [
        pltpu.make_async_copy(a, b, up_sem.at[i])
        for i, (a, b) in enumerate(columns(up_hbm, up_late, n_up))
    ]
    up_refs += up_late
    down_copies = [
        pltpu.make_async_copy(
            down_hbm.at[pl.ds(x * per_expert, per_expert)], down_ref, down_sem.at[x]
        )
        for x in range(experts)
    ]
    for c in down_copies[:1] + up_copies:
        c.start()
    count = 0
    for r in rows_in:
        rows_ref[count : count + r.shape[0], :] = r[...]
        count += r.shape[0]
    at0 = lax.broadcasted_iota(jnp.int32, (count, count), 0)
    at1 = lax.broadcasted_iota(jnp.int32, (count, count), 1)
    eye = jnp.where(at0 == at1, 1.0, 0.0).astype(jnp.bfloat16)
    before = jnp.where(at0 < at1, 1.0, 0.0).astype(jnp.bfloat16)
    info = lax.dot_general(
        rows_ref[:, width:], eye, (((0,), (0,)), ((), ())), preferred_element_type=jnp.float32
    )
    id0, id1, code0, code1 = (info[i : i + 1, :] for i in range(4))
    slot_of = lax.broadcasted_iota(jnp.int32, (capacity, count), 0).astype(jnp.float32)
    first = lax.axis_index("sec") * experts if halves == 1 else lax.axis_index("sec") // halves
    picks, shares = [], []
    for x in range(experts):
        e = (first + x).astype(jnp.float32)
        hit0 = jnp.where(id0 == e, 1.0, 0.0)
        hit1 = jnp.where(id1 == e, 1.0, 0.0)
        member = hit0 + hit1
        share = (hit0 * code0 + hit1 * code1) / (code0 + code1)
        slot = dot(jnp.broadcast_to(member, (8, count)).astype(jnp.bfloat16), before)[:1]
        slot = jnp.where(member > 0.5, slot, -1.0)
        pick = slot == slot_of
        shares.append(jnp.sum(jnp.where(pick, share, 0.0), axis=1, keepdims=True))
        picks.append(jnp.where(pick, 1.0, 0.0).astype(jnp.bfloat16))
    pick_ref[...] = jnp.concatenate(picks, axis=0)
    column = min(256, width)

    for c in range(0, width, column):
        packed_ref[:, c : c + column] = dot(pick_ref[...], rows_ref[:, c : c + column]).astype(
            jnp.bfloat16
        )
    for x in range(experts):
        mine = slice(x * capacity, (x + 1) * capacity)
        if x >= n_up:
            up_copies[x - n_up].wait()
        gate_ref, up_ref = gate_refs[x], up_refs[x]

        for s in range(0, per_expert, tile):
            cut = slice(s, s + tile)
            gate = dot(packed_ref[mine, :], gate_ref[:, cut])
            up = dot(packed_ref[mine, :], up_ref[:, cut])
            half = 0.5 * gate
            hidden_ref[mine, cut] = ((half + half * jnp.tanh(half)) * up).astype(jnp.bfloat16)
        down_copies[x].wait()

        for c in range(0, width, column):
            out = dot(hidden_ref[mine, :], down_ref[:, c : c + column])
            packed_ref[mine, c : c + column] = (out * shares[x]).astype(jnp.bfloat16)
        if x + 1 < experts:
            down_copies[x + 1].start()
    kept = keep_ref.shape[0]

    for c in range(0, width, column):
        out = lax.dot_general(
            pick_ref[...], packed_ref[:, c : c + column], (((0,), (0,)), ((), ())),
            preferred_element_type=jnp.float32,
        )
        keep_ref[:, c : c + column] = out[:kept]
        send_ref[:, c : c + column] = out[kept:].astype(jnp.bfloat16)


def per_device(
    query,
    keys,
    values,
    residual,
    out_weight,
    norm_gain,
    expert_ids,
    gate_codes,
    doc_lengths,
    w_gate,
    w_up,
    w_down,
):
    block, width = residual.shape
    head = HEAD_DIMENSION
    group_width = QUERY_HEAD_COUNT // KEY_VALUE_HEADS
    q_heads = query.shape[1] // head
    sec_count, tp_count, pp_count = (lax.axis_size(a) for a in ("sec", "tp", "pp"))
    own_rows = block // (tp_count * pp_count)
    bf16, f32 = jnp.bfloat16, jnp.float32

    kv_heads = max(1, q_heads // group_width)
    group = q_heads // kv_heads
    kv_start = lax.axis_index("pp") * q_heads // group_width * head
    kv = jnp.concatenate(
        [lax.dynamic_slice_in_dim(a, kv_start, kv_heads * head, 1) for a in (keys, values)], axis=1
    )
    back = -(-(sec_count * block // 2 - 1) // block)
    pieces = [
        lax.ppermute(kv, "sec", [(i, i + k) for i in range(sec_count - k)])
        for k in range(back, 0, -1)
    ] + [kv]

    experts = max(1, E // sec_count)
    per_expert = w_gate.shape[2] // experts
    span = (back + 1) * block
    query_v, weight_v, gain_v, mask, order, residual_own, info, *gate_v = call(
        functools.partial(prepare_kernel, back, tp_count, pp_count),
        [
            sds(query.shape, bf16),
            sds(out_weight.shape, bf16),
            sds((1, width), f32),
            sds((block, span), f32),
            sds((block, block), bf16),
            sds((own_rows, width), f32),
            sds((own_rows, LANES), bf16),
        ]
        + [sds((width, per_expert), bf16)] * experts,
        [
            (HBM, a)
            for a in (
                doc_lengths, expert_ids.T, gate_codes.T, query, out_weight, residual,
                norm_gain.reshape(1, width), w_gate[0],
            )
        ],
        scratch=[
            pltpu.SMEM(doc_lengths.shape, jnp.int32),
            pltpu.VMEM((2, block), jnp.int32),
            pltpu.VMEM((2, block), jnp.int32),
            pltpu.VMEM(residual.shape, bf16),
            pltpu.SemaphoreType.DMA((7 + experts,)),
        ],
        vmem=6,
        name="prepare",
        cost_us=6.0,
    )
    half = block // pp_count
    keep, send = call(
        functools.partial(attention_kernel, back, kv_heads, group),
        [sds((half, width), f32), sds((block - half, width), bf16)],
        [(VMEM, a) for a in (query_v, mask, order, *pieces, weight_v)],
        scratch=[pltpu.VMEM(query.shape, bf16)],
        name="attention",
        cost_us=2.4,
    )

    (own,), sends = add(
        [keep] + [xor_swap(send, "pp", 1)], [own_rows], [own_rows] * (tp_count - 1), "sum_cores"
    )
    got = [xor_swap(sends[k - 1], "tp", k) for k in range(1, tp_count)]
    up_v, token = load(w_up[0], experts, 1, [own], "load_up")
    stream, normed = call(
        functools.partial(norm_kernel, tp_count),
        [sds((own_rows, width), f32), sds((own_rows, width + LANES), bf16)],
        [(VMEM, a) for a in (residual_own, gain_v, info, own, *got)] + [(ANY, token)],
        name="norm",
        cost_us=0.2,
    )

    groups = min(4, sec_count)
    near = [normed] + [xor_swap(normed, "sec", k) for k in range(1, sec_count)]
    per_group = sec_count // groups
    near = [
        jnp.concatenate(near[g * per_group : (g + 1) * per_group], axis=0)
        if per_group > 1
        else near[g]
        for g in range(groups)
    ]
    rows = [[r] + [xor_swap(r, "tp", k) for k in range(1, tp_count)] for r in near]
    rows = [rows[g][k] for k in range(tp_count) for g in range(groups)]
    rows = rows + [xor_swap(r, "pp", k) for k in range(1, pp_count) for r in rows]

    halves = max(1, sec_count // E)
    count = sec_count * block
    capacity = sec_count * MOSTB
    down = w_down[0]
    tile = min(256, down.shape[0] // experts)
    kept = count // pp_count
    keep, send = call(
        functools.partial(experts_kernel, experts, capacity, tile, halves, len(rows), experts, 1),
        [sds((kept, width), f32), sds((count - kept, width), bf16)],
        [(VMEM, a) for a in (*rows, *gate_v, *up_v)] + [(HBM, w_up[0]), (HBM, down)],
        scratch=[
            pltpu.VMEM((count, width + LANES), bf16),
            pltpu.VMEM((experts * capacity, count), bf16),
            pltpu.VMEM((experts * capacity, width), bf16),
            pltpu.VMEM((experts * capacity, down.shape[0] // experts), bf16),
            *[pltpu.VMEM((width, per_expert), bf16)] * (experts - 1),
            pltpu.VMEM((per_expert, width), bf16),
            pltpu.SemaphoreType.DMA((experts,)),
            pltpu.SemaphoreType.DMA((experts,)),
        ],
        vmem=24,
        name="experts",
        cost_us=12.0,
    )

    piece = kept // (tp_count * groups)
    own, sends = add(
        [keep, xor_swap(send, "pp", 1)], [piece] * groups, [piece] * (groups * (tp_count - 1)), "sum_cores2"
    )
    final = [stream]
    for g in list(range(1, groups)) + [0]:
        got = [xor_swap(sends[(k - 1) * groups + g], "tp", k) for k in range(1, tp_count)]
        if g == 0 and per_group == 1:
            final += [own[0]] + got
            continue
        kept_rows = own_rows if g == 0 else 0
        mine, out = add(
            [own[g]] + got,
            [own_rows] if g == 0 else [],
            [own_rows] * (per_group - (g == 0)),
            "sum_x%d" % g,
        )
        final += list(mine)
        for j, o in enumerate(out):
            final.append(xor_swap(o, "sec", g * per_group + j + (g == 0)))
    return call(
        functools.partial(add_kernel, 0, len(final)),
        [sds((own_rows, width), bf16)],
        [(VMEM, a) for a in final],
        name="total",
        cost_us=0.2,
    )[0]


def solution(mesh):
    in_specs = (
        P(("groups", "sec"), ("tp", "pp")),
        P(("groups", "sec"), "tp"),
        P(("groups", "sec"), "tp"),
        P(("groups", "sec"), None),
        P(("tp", "pp"), None),
        P(),
        P(("groups", "sec"), None),
        P(("groups", "sec"), None),
        P("groups"),
        P(("tp", "pp"), None, "sec"),
        P(("tp", "pp"), None, "sec"),
        P(("tp", "pp"), "sec", None),
    )
    out_specs = P(("groups", "sec", "tp", "pp"), None)
    return jax.shard_map(
        per_device, mesh=mesh, in_specs=in_specs, out_specs=out_specs, check_vma=False
    )
```

```python
import functools

import jax
import jax.numpy as jnp
from jax import lax
from jax.experimental import pallas as pl
from jax.experimental.pallas import tpu as pltpu
from jax.sharding import PartitionSpec as P

QUERY_HEAD_COUNT = 32
KEY_VALUE_HEADS = 8
HEAD_DIMENSION = 128
E = 8
MOSTB = 32
LANES = 128

neg_fill = -1e30
norm_eps = 1e-05

VMEM = pl.BlockSpec(memory_space=pltpu.VMEM)
SMEM = pl.BlockSpec(memory_space=pltpu.SMEM)
HBM = pl.BlockSpec(memory_space=pltpu.HBM)
ANY = pl.BlockSpec(memory_space=pl.ANY)
MIB = 2**20


def dot(a, b):
    return jnp.dot(a, b, preferred_element_type=jnp.float32)


def xor_swap(x, axis, k):
    n = lax.axis_size(axis)
    return lax.ppermute(x, axis, [(i, i ^ k) for i in range(n)])


def call(kernel, out_shape, args, scratch=(), vmem=8, name=None, cost_us=1.0):
    args = [
        (s, pltpu.with_memory_space_constraint(a, pltpu.HBM) if s is HBM else a) for s, a in args
    ]
    single = not isinstance(out_shape, (tuple, list))
    return pl.pallas_call(
        kernel,
        out_shape=out_shape,
        in_specs=[s for s, _ in args],
        out_specs=VMEM if single else [VMEM] * len(out_shape),
        scratch_shapes=list(scratch),
        compiler_params=pltpu.CompilerParams(vmem_limit_bytes=vmem * MIB),
        cost_estimate=pl.CostEstimate(
            flops=0, bytes_accessed=int(cost_us * 3.4e6), transcendentals=0
        ),
        name=name,
    )(*[a for _, a in args])


def sds(shape, dtype):
    return jax.ShapeDtypeStruct(shape, dtype)


def position():
    rank = lax.axis_index("tp") * lax.axis_size("pp") + lax.axis_index("pp")
    return lax.axis_index("sec"), rank


def columns(source, targets, first=0):
    per = targets[0].shape[1] if targets else 0
    return [(source.at[:, pl.ds((first + i) * per, per)], t) for i, t in enumerate(targets)]


def prepare_kernel(
    back, tp_count, pp_count, lengths_hbm, ids_hbm, codes_hbm, query_hbm, weight_hbm, residual_hbm,
    gain_hbm, *refs
):
    gate_hbm, query_ref, weight_ref, gain_ref, mask_ref, order_ref, residual_ref, info_ref = refs[
        :8
    ]
    gate_refs = refs[8:-5]
    lengths, ids, codes, residual_all, sem = refs[-5:]
    pairs = [
        (lengths_hbm, lengths),
        (ids_hbm, ids),
        (codes_hbm, codes),
        (residual_hbm, residual_all),
        (query_hbm, query_ref),
        (gain_hbm, gain_ref),
        (weight_hbm, weight_ref),
    ] + columns(gate_hbm, gate_refs)
    copies = [pltpu.make_async_copy(a, b, sem.at[i]) for i, (a, b) in enumerate(pairs)]
    for c in copies:
        c.start()
    sec, rank = position()
    block = query_ref.shape[0]
    own_rows = residual_ref.shape[0]
    at = lax.broadcasted_iota(jnp.int32, (block, block), 0)
    to = lax.broadcasted_iota(jnp.int32, (block, block), 1)
    chunk = lax.div(at, own_rows)
    flip = lax.rem(chunk, tp_count) * pp_count + lax.div(chunk, tp_count)
    source = (rank ^ flip) * own_rows + lax.rem(at, own_rows)
    order_ref[...] = jnp.where(to == source, 1.0, 0.0).astype(jnp.bfloat16)
    own = lax.broadcasted_iota(jnp.int32, (own_rows, block), 0) + rank * own_rows
    own = jnp.where(own == lax.broadcasted_iota(jnp.int32, (own_rows, block), 1), 1.0, 0.0)
    own = own.astype(jnp.bfloat16)
    for c in copies[:4]:
        c.wait()
    span = (back + 1) * block
    rows = sec * block + lax.broadcasted_iota(jnp.int32, (block, span), 0)
    cols = (sec - back) * block + lax.broadcasted_iota(jnp.int32, (block, span), 1)
    first = jnp.zeros((block, span), jnp.int32)
    end = jnp.int32(0)
    for d in range(lengths.shape[0]):
        end = end + lengths[d]
        first = jnp.where(rows >= end, end, first)
    mask_ref[...] = jnp.where((cols <= rows) & (cols >= first), 1.0, 0.0)
    residual_ref[...] = dot(own, residual_all[...])
    info = jnp.concatenate(
        [ids[...], codes[...], jnp.zeros((LANES - 4, block), jnp.int32)], axis=0
    ).astype(jnp.float32)
    info_ref[...] = lax.dot_general(
        own, info.astype(jnp.bfloat16), (((1,), (1,)), ((), ())), preferred_element_type=jnp.float32
    ).astype(jnp.bfloat16)
    for c in copies[4:]:
        c.wait()


def load_kernel(n_after, source, *refs):
    *targets, token_ref, sem = refs[n_after:]
    copies = [
        pltpu.make_async_copy(a, b, sem.at[i])
        for i, (a, b) in enumerate(columns(source, targets))
    ]
    for c in copies:
        c.start()
    token_ref[...] = jnp.zeros_like(token_ref)
    for c in copies:
        c.wait()


def load(array, parts, wanted, after, name):
    rows, cols = array.shape
    out = call(
        functools.partial(load_kernel, len(after)),
        [sds((rows, cols // parts), array.dtype)] * wanted + [sds((8, LANES), jnp.float32)],
        [(HBM, array)] + [(ANY, a) for a in after],
        scratch=[pltpu.SemaphoreType.DMA((wanted,))],
        vmem=1,
        name=name,
        cost_us=array.size * wanted / parts * 2 / 3.4e6,
    )
    return out[:-1], out[-1]


def attention_kernel(back, kv_heads, group, q_ref, mask_ref, order_ref, *refs):
    kv_refs = refs[: back + 1]
    weight_ref, keep_ref, send_ref, attended_ref = refs[back + 1 :]
    block = q_ref.shape[0]
    head = HEAD_DIMENSION
    allowed = jnp.concatenate([mask_ref[...]] * group, axis=0) > 0.5
    for g in range(kv_heads):
        q = jnp.concatenate(
            [q_ref[:, (g * group + t) * head : (g * group + t + 1) * head] for t in range(group)],
            axis=0,
        )
        k = jnp.concatenate([r[:, g * head : (g + 1) * head] for r in kv_refs], axis=0)
        v = jnp.concatenate(
            [r[:, (kv_heads + g) * head : (kv_heads + g + 1) * head] for r in kv_refs], axis=0
        )
        scores = lax.dot_general(
            q, k, (((1,), (1,)), ((), ())), preferred_element_type=jnp.float32
        ) * (head**-0.5)
        scores = jnp.where(allowed, scores, neg_fill)
        top = jnp.max(scores, axis=1, keepdims=True)
        weights = jnp.where(allowed, jnp.exp(scores - top), 0.0)
        total = jnp.sum(weights, axis=1, keepdims=True)
        summed = dot(weights.astype(jnp.bfloat16), v) / total
        for t in range(group):
            attended_ref[:, (g * group + t) * head : (g * group + t + 1) * head] = summed[
                t * block : (t + 1) * block
            ].astype(jnp.bfloat16)
    attended = dot(order_ref[...], attended_ref[...]).astype(jnp.bfloat16)
    mixed = dot(attended, weight_ref[...])
    kept = keep_ref.shape[0]
    keep_ref[...] = mixed[:kept]
    send_ref[...] = mixed[kept:].astype(jnp.bfloat16)


def add_kernel(keep_rows, n_in, *refs):
    total = refs[0][...].astype(jnp.float32)
    for r in refs[1:n_in]:
        total = total + r[...].astype(jnp.float32)
    start = 0
    for r in refs[n_in:]:
        r[...] = total[start : start + r.shape[0]].astype(r.dtype)
        start += r.shape[0]


def add(arrays, keep, send, name):
    width = arrays[0].shape[1]
    out = [sds((r, width), jnp.float32) for r in keep]
    out += [sds((r, width), jnp.bfloat16) for r in send]
    out = call(
        functools.partial(add_kernel, sum(keep), len(arrays)),
        out,
        [(VMEM, a) for a in arrays],
        name=name,
        cost_us=0.2,
    )
    return out[: len(keep)], out[len(keep) :]


def norm_kernel(n_parts, residual_ref, gain_ref, info_ref, *refs):
    parts = refs[:n_parts]
    stream_ref, normed_ref = refs[-2:]
    width = residual_ref.shape[1]
    mixed = parts[0][...].astype(jnp.float32)
    for p in parts[1:]:
        mixed = mixed + p[...].astype(jnp.float32)
    stream = residual_ref[...] + mixed
    stream_ref[...] = stream
    meansq = jnp.mean(stream * stream, axis=1, keepdims=True)
    normed_ref[:, :width] = (stream * lax.rsqrt(meansq + norm_eps) * gain_ref[...]).astype(
        jnp.bfloat16
    )
    normed_ref[:, width:] = info_ref[...]


def experts_kernel(experts, capacity, tile, halves, n_rows, n_gate, n_up, *refs):
    rows_in = refs[:n_rows]
    gate_refs = list(refs[n_rows : n_rows + n_gate])
    up_refs = list(refs[n_rows + n_gate : n_rows + n_gate + n_up])
    refs = refs[n_rows + n_gate + n_up :]
    up_hbm, down_hbm, keep_ref, send_ref, rows_ref, pick_ref, share_ref, packed_ref, hidden_ref = refs[:9]
    up_late = list(refs[9 : 9 + experts - n_up])
    down_ref, up_sem, down_sem = refs[9 + experts - n_up :]
    per_expert, width = down_hbm.shape[0] // experts, down_hbm.shape[1]
    up_copies = [
        pltpu.make_async_copy(a, b, up_sem.at[i])
        for i, (a, b) in enumerate(columns(up_hbm, up_late, n_up))
    ]
    up_refs += up_late
    down_copies = [
        pltpu.make_async_copy(
            down_hbm.at[pl.ds(x * per_expert, per_expert)], down_ref, down_sem.at[x]
        )
        for x in range(experts)
    ]
    for c in down_copies[:1] + up_copies:
        c.start()
    count = 0
    for r in rows_in:
        rows_ref[count : count + r.shape[0], :] = r[...]
        count += r.shape[0]
    at0 = lax.broadcasted_iota(jnp.int32, (count, count), 0)
    at1 = lax.broadcasted_iota(jnp.int32, (count, count), 1)
    eye = jnp.where(at0 == at1, 1.0, 0.0).astype(jnp.bfloat16)
    before = jnp.where(at0 < at1, 1.0, 0.0).astype(jnp.bfloat16)
    info = lax.dot_general(
        rows_ref[:, width:], eye, (((0,), (0,)), ((), ())), preferred_element_type=jnp.float32
    )
    id0, id1, code0, code1 = (info[i : i + 1, :] for i in range(4))
    slot_of = lax.broadcasted_iota(jnp.int32, (capacity, count), 0).astype(jnp.float32)
    first = lax.axis_index("sec") * experts if halves == 1 else lax.axis_index("sec") // halves
    picks, shares, taken = [], [], []
    for x in range(experts):
        e = (first + x).astype(jnp.float32)
        hit0 = jnp.where(id0 == e, 1.0, 0.0)
        hit1 = jnp.where(id1 == e, 1.0, 0.0)
        member = hit0 + hit1
        share = (hit0 * code0 + hit1 * code1) / (code0 + code1)
        slot = dot(jnp.broadcast_to(member, (8, count)).astype(jnp.bfloat16), before)[:1]
        slot = jnp.where(member > 0.5, slot, -1.0)
        pick = slot == slot_of
        shares.append(jnp.sum(jnp.where(pick, share, 0.0), axis=1, keepdims=True))
        taken.append(jnp.sum(member).astype(jnp.int32))
        picks.append(jnp.where(pick, 1.0, 0.0).astype(jnp.bfloat16))
    pick_ref[...] = jnp.concatenate(picks, axis=0)
    share_ref[...] = jnp.broadcast_to(jnp.concatenate(shares, axis=0), share_ref.shape)
    column = min(512, width)

    for c in range(0, width, column):
        packed_ref[:, c : c + column] = dot(pick_ref[...], rows_ref[:, c : c + column]).astype(
            jnp.bfloat16
        )
    step = min(capacity, 32)
    sizes = range(step, capacity + 1, step) if capacity <= 4 * step else [capacity]

    def by_size(x, run):
        for size in sizes:
            fits = taken[x] <= size
            if size > sizes[0]:
                fits = fits & (taken[x] > size - step)
            if len(sizes) > 1:
                pl.when(fits)(functools.partial(run, slice(x * capacity, x * capacity + size)))
            else:
                run(slice(x * capacity, x * capacity + size))

    for x in range(experts):
        if x >= n_up:
            up_copies[x - n_up].wait()

        def inner(mine, gate_ref=gate_refs[x], up_ref=up_refs[x]):
            def body(s, _):
                cut = pl.ds(pl.multiple_of(s * tile, tile), tile)
                gate = dot(packed_ref[mine, :], gate_ref[:, cut])
                up = dot(packed_ref[mine, :], up_ref[:, cut])
                half = 0.5 * gate
                hidden_ref[mine, cut] = ((half + half * jnp.tanh(half)) * up).astype(jnp.bfloat16)
                return 0

            lax.fori_loop(0, per_expert // tile, body, 0)

        def outer(mine, x=x):
            def body(c, _):
                cut = pl.ds(pl.multiple_of(c * column, column), column)
                out = dot(hidden_ref[mine, :], down_ref[:, cut])
                packed_ref[mine, cut] = (out * share_ref[mine, :1]).astype(jnp.bfloat16)
                return 0

            lax.fori_loop(0, width // column, body, 0)

        by_size(x, inner)
        down_copies[x].wait()
        by_size(x, outer)
        if x + 1 < experts:
            down_copies[x + 1].start()
    kept = keep_ref.shape[0]

    for c in range(0, width, column):
        out = lax.dot_general(
            pick_ref[...], packed_ref[:, c : c + column], (((0,), (0,)), ((), ())),
            preferred_element_type=jnp.float32,
        )
        keep_ref[:, c : c + column] = out[:kept]
        send_ref[:, c : c + column] = out[kept:].astype(jnp.bfloat16)


def per_device(
    query,
    keys,
    values,
    residual,
    out_weight,
    norm_gain,
    expert_ids,
    gate_codes,
    doc_lengths,
    w_gate,
    w_up,
    w_down,
):
    block, width = residual.shape
    head = HEAD_DIMENSION
    group_width = QUERY_HEAD_COUNT // KEY_VALUE_HEADS
    q_heads = query.shape[1] // head
    sec_count, tp_count, pp_count = (lax.axis_size(a) for a in ("sec", "tp", "pp"))
    own_rows = block // (tp_count * pp_count)
    bf16, f32 = jnp.bfloat16, jnp.float32

    kv_heads = max(1, q_heads // group_width)
    group = q_heads // kv_heads
    kv_start = lax.axis_index("pp") * q_heads // group_width * head
    kv = jnp.concatenate(
        [lax.dynamic_slice_in_dim(a, kv_start, kv_heads * head, 1) for a in (keys, values)], axis=1
    )
    back = -(-(sec_count * block // 2 - 1) // block)
    pieces = [
        lax.ppermute(kv, "sec", [(i, i + k) for i in range(sec_count - k)])
        for k in range(back, 0, -1)
    ] + [kv]

    experts = max(1, E // sec_count)
    per_expert = w_gate.shape[2] // experts
    span = (back + 1) * block
    query_v, weight_v, gain_v, mask, order, residual_own, info, *gate_v = call(
        functools.partial(prepare_kernel, back, tp_count, pp_count),
        [
            sds(query.shape, bf16),
            sds(out_weight.shape, bf16),
            sds((1, width), f32),
            sds((block, span), f32),
            sds((block, block), bf16),
            sds((own_rows, width), f32),
            sds((own_rows, LANES), bf16),
        ]
        + [sds((width, per_expert), bf16)] * experts,
        [
            (HBM, a)
            for a in (
                doc_lengths, expert_ids.T, gate_codes.T, query, out_weight, residual,
                norm_gain.reshape(1, width), w_gate[0],
            )
        ],
        scratch=[
            pltpu.SMEM(doc_lengths.shape, jnp.int32),
            pltpu.VMEM((2, block), jnp.int32),
            pltpu.VMEM((2, block), jnp.int32),
            pltpu.VMEM(residual.shape, bf16),
            pltpu.SemaphoreType.DMA((7 + experts,)),
        ],
        vmem=6,
        name="prepare",
        cost_us=6.0,
    )
    half = block // pp_count
    keep, send = call(
        functools.partial(attention_kernel, back, kv_heads, group),
        [sds((half, width), f32), sds((block - half, width), bf16)],
        [(VMEM, a) for a in (query_v, mask, order, *pieces, weight_v)],
        scratch=[pltpu.VMEM(query.shape, bf16)],
        name="attention",
        cost_us=2.4,
    )

    (own,), sends = add(
        [keep] + [xor_swap(send, "pp", 1)], [own_rows], [own_rows] * (tp_count - 1), "sum_cores"
    )
    got = [xor_swap(sends[k - 1], "tp", k) for k in range(1, tp_count)]
    up_v, token = load(w_up[0], experts, 1, [own], "load_up")
    stream, normed = call(
        functools.partial(norm_kernel, tp_count),
        [sds((own_rows, width), f32), sds((own_rows, width + LANES), bf16)],
        [(VMEM, a) for a in (residual_own, gain_v, info, own, *got)] + [(ANY, token)],
        name="norm",
        cost_us=0.2,
    )

    groups = min(4, sec_count)
    near = {k: xor_swap(normed, "sec", k) if k else normed for k in range(0, sec_count, 2)}
    near.update({k + 1: xor_swap(near[k], "sec", 1) for k in list(near) if k + 1 < sec_count})
    near = [near[k] for k in range(sec_count)]
    per_group = sec_count // groups
    near = [
        jnp.concatenate(near[g * per_group : (g + 1) * per_group], axis=0)
        if per_group > 1
        else near[g]
        for g in range(groups)
    ]
    rows = [[r] + [xor_swap(r, "tp", k) for k in range(1, tp_count)] for r in near]
    rows = [rows[g][k] for k in range(tp_count) for g in range(groups)]
    rows = rows + [xor_swap(r, "pp", k) for k in range(1, pp_count) for r in rows]

    halves = max(1, sec_count // E)
    count = sec_count * block
    capacity = sec_count * MOSTB
    down = w_down[0]
    tile = min(512, down.shape[0] // experts)
    kept = count // pp_count
    keep, send = call(
        functools.partial(experts_kernel, experts, capacity, tile, halves, len(rows), experts, 1),
        [sds((kept, width), f32), sds((count - kept, width), bf16)],
        [(VMEM, a) for a in (*rows, *gate_v, *up_v)] + [(HBM, w_up[0]), (HBM, down)],
        scratch=[
            pltpu.VMEM((count, width + LANES), bf16),
            pltpu.VMEM((experts * capacity, count), bf16),
            pltpu.VMEM((experts * capacity, LANES), f32),
            pltpu.VMEM((experts * capacity, width), bf16),
            pltpu.VMEM((experts * capacity, down.shape[0] // experts), bf16),
            *[pltpu.VMEM((width, per_expert), bf16)] * (experts - 1),
            pltpu.VMEM((per_expert, width), bf16),
            pltpu.SemaphoreType.DMA((experts,)),
            pltpu.SemaphoreType.DMA((experts,)),
        ],
        vmem=24,
        name="experts",
        cost_us=12.0,
    )

    piece = kept // (tp_count * groups)
    own, sends = add(
        [keep, xor_swap(send, "pp", 1)], [piece] * groups, [piece] * (groups * (tp_count - 1)), "sum_cores2"
    )
    final = [stream]
    for g in list(range(1, groups)) + [0]:
        got = [xor_swap(sends[(k - 1) * groups + g], "tp", k) for k in range(1, tp_count)]
        if g == 0 and per_group == 1:
            final += [own[0]] + got
            continue
        kept_rows = own_rows if g == 0 else 0
        mine, out = add(
            [own[g]] + got,
            [own_rows] if g == 0 else [],
            [own_rows] * (per_group - (g == 0)),
            "sum_x%d" % g,
        )
        final += list(mine)
        for j, o in enumerate(out):
            final.append(xor_swap(o, "sec", g * per_group + j + (g == 0)))
    return call(
        functools.partial(add_kernel, 0, len(final)),
        [sds((own_rows, width), bf16)],
        [(VMEM, a) for a in final],
        name="total",
        cost_us=0.2,
    )[0]


def solution(mesh):
    in_specs = (
        P(("groups", "sec"), ("tp", "pp")),
        P(("groups", "sec"), "tp"),
        P(("groups", "sec"), "tp"),
        P(("groups", "sec"), None),
        P(("tp", "pp"), None),
        P(),
        P(("groups", "sec"), None),
        P(("groups", "sec"), None),
        P("groups"),
        P(("tp", "pp"), None, "sec"),
        P(("tp", "pp"), None, "sec"),
        P(("tp", "pp"), "sec", None),
    )
    out_specs = P(("groups", "sec", "tp", "pp"), None)
    return jax.shard_map(
        per_device, mesh=mesh, in_specs=in_specs, out_specs=out_specs, check_vma=False
    )
```

```python
import functools

import jax
import jax.numpy as jnp
from jax import lax
from jax.experimental import pallas as pl
from jax.experimental.pallas import tpu as pltpu
from jax.sharding import PartitionSpec as P

QUERY_HEAD_COUNT = 32
KEY_VALUE_HEADS = 8
HEAD_DIMENSION = 128
E = 8
MOSTB = 32
LANES = 128

neg_fill = -1e30
norm_eps = 1e-05

VMEM = pl.BlockSpec(memory_space=pltpu.VMEM)
SMEM = pl.BlockSpec(memory_space=pltpu.SMEM)
HBM = pl.BlockSpec(memory_space=pltpu.HBM)
ANY = pl.BlockSpec(memory_space=pl.ANY)
MIB = 2**20


def dot(a, b):
    return jnp.dot(a, b, preferred_element_type=jnp.float32)


def xor_swap(x, axis, k):
    n = lax.axis_size(axis)
    return lax.ppermute(x, axis, [(i, i ^ k) for i in range(n)])


def call(kernel, out_shape, args, scratch=(), vmem=8, name=None, cost_us=1.0):
    args = [
        (s, pltpu.with_memory_space_constraint(a, pltpu.HBM) if s is HBM else a) for s, a in args
    ]
    single = not isinstance(out_shape, (tuple, list))
    return pl.pallas_call(
        kernel,
        out_shape=out_shape,
        in_specs=[s for s, _ in args],
        out_specs=VMEM if single else [VMEM] * len(out_shape),
        scratch_shapes=list(scratch),
        compiler_params=pltpu.CompilerParams(vmem_limit_bytes=vmem * MIB),
        cost_estimate=pl.CostEstimate(
            flops=0, bytes_accessed=int(cost_us * 3.4e6), transcendentals=0
        ),
        name=name,
    )(*[a for _, a in args])


def sds(shape, dtype):
    return jax.ShapeDtypeStruct(shape, dtype)


def position():
    rank = lax.axis_index("tp") * lax.axis_size("pp") + lax.axis_index("pp")
    return lax.axis_index("sec"), rank


def columns(source, targets, first=0):
    per = targets[0].shape[1] if targets else 0
    return [(source.at[:, pl.ds((first + i) * per, per)], t) for i, t in enumerate(targets)]


def prepare_kernel(
    back, tp_count, pp_count, lengths_hbm, ids_hbm, codes_hbm, query_hbm, weight_hbm, residual_hbm,
    gain_hbm, *refs
):
    gate_hbm, query_ref, weight_ref, gain_ref, mask_ref, order_ref, residual_ref, info_ref = refs[
        :8
    ]
    gate_refs = refs[8:-5]
    lengths, ids, codes, residual_all, sem = refs[-5:]
    pairs = [
        (lengths_hbm, lengths),
        (ids_hbm, ids),
        (codes_hbm, codes),
        (residual_hbm, residual_all),
        (query_hbm, query_ref),
        (gain_hbm, gain_ref),
        (weight_hbm, weight_ref),
    ] + columns(gate_hbm, gate_refs)
    copies = [pltpu.make_async_copy(a, b, sem.at[i]) for i, (a, b) in enumerate(pairs)]
    for c in copies:
        c.start()
    sec, rank = position()
    block = query_ref.shape[0]
    own_rows = residual_ref.shape[0]
    at = lax.broadcasted_iota(jnp.int32, (block, block), 0)
    to = lax.broadcasted_iota(jnp.int32, (block, block), 1)
    chunk = lax.div(at, own_rows)
    flip = lax.rem(chunk, tp_count) * pp_count + lax.div(chunk, tp_count)
    source = (rank ^ flip) * own_rows + lax.rem(at, own_rows)
    order_ref[...] = jnp.where(to == source, 1.0, 0.0).astype(jnp.bfloat16)
    own = lax.broadcasted_iota(jnp.int32, (own_rows, block), 0) + rank * own_rows
    own = jnp.where(own == lax.broadcasted_iota(jnp.int32, (own_rows, block), 1), 1.0, 0.0)
    own = own.astype(jnp.bfloat16)
    for c in copies[:4]:
        c.wait()
    span = (back + 1) * block
    rows = sec * block + lax.broadcasted_iota(jnp.int32, (block, span), 0)
    cols = (sec - back) * block + lax.broadcasted_iota(jnp.int32, (block, span), 1)
    first = jnp.zeros((block, span), jnp.int32)
    end = jnp.int32(0)
    for d in range(lengths.shape[0]):
        end = end + lengths[d]
        first = jnp.where(rows >= end, end, first)
    mask_ref[...] = jnp.where((cols <= rows) & (cols >= first), 1.0, 0.0)
    residual_ref[...] = dot(own, residual_all[...])
    info = jnp.concatenate(
        [ids[...], codes[...], jnp.zeros((LANES - 4, block), jnp.int32)], axis=0
    ).astype(jnp.float32)
    info_ref[...] = lax.dot_general(
        own, info.astype(jnp.bfloat16), (((1,), (1,)), ((), ())), preferred_element_type=jnp.float32
    ).astype(jnp.bfloat16)
    for c in copies[4:]:
        c.wait()


def load_kernel(n_after, source, *refs):
    *targets, token_ref, sem = refs[n_after:]
    copies = [
        pltpu.make_async_copy(a, b, sem.at[i])
        for i, (a, b) in enumerate(columns(source, targets))
    ]
    for c in copies:
        c.start()
    token_ref[...] = jnp.zeros_like(token_ref)
    for c in copies:
        c.wait()


def load(array, parts, wanted, after, name):
    rows, cols = array.shape
    out = call(
        functools.partial(load_kernel, len(after)),
        [sds((rows, cols // parts), array.dtype)] * wanted + [sds((8, LANES), jnp.float32)],
        [(HBM, array)] + [(ANY, a) for a in after],
        scratch=[pltpu.SemaphoreType.DMA((wanted,))],
        vmem=1,
        name=name,
        cost_us=array.size * wanted / parts * 2 / 3.4e6,
    )
    return out[:-1], out[-1]


def attention_kernel(back, kv_heads, group, q_ref, mask_ref, order_ref, *refs):
    kv_refs = refs[: back + 1]
    weight_ref, keep_ref, send_ref, attended_ref = refs[back + 1 :]
    block = q_ref.shape[0]
    head = HEAD_DIMENSION
    allowed = jnp.concatenate([mask_ref[...]] * group, axis=0) > 0.5
    for g in range(kv_heads):
        q = jnp.concatenate(
            [q_ref[:, (g * group + t) * head : (g * group + t + 1) * head] for t in range(group)],
            axis=0,
        )
        k = jnp.concatenate([r[:, g * head : (g + 1) * head] for r in kv_refs], axis=0)
        v = jnp.concatenate(
            [r[:, (kv_heads + g) * head : (kv_heads + g + 1) * head] for r in kv_refs], axis=0
        )
        scores = lax.dot_general(
            q, k, (((1,), (1,)), ((), ())), preferred_element_type=jnp.float32
        ) * (head**-0.5)
        scores = jnp.where(allowed, scores, neg_fill)
        top = jnp.max(scores, axis=1, keepdims=True)
        weights = jnp.where(allowed, jnp.exp(scores - top), 0.0)
        total = jnp.sum(weights, axis=1, keepdims=True)
        summed = dot(weights.astype(jnp.bfloat16), v) / total
        for t in range(group):
            attended_ref[:, (g * group + t) * head : (g * group + t + 1) * head] = summed[
                t * block : (t + 1) * block
            ].astype(jnp.bfloat16)
    attended = dot(order_ref[...], attended_ref[...]).astype(jnp.bfloat16)
    mixed = dot(attended, weight_ref[...])
    kept = keep_ref.shape[0]
    keep_ref[...] = mixed[:kept]
    send_ref[...] = mixed[kept:].astype(jnp.bfloat16)


def add_kernel(keep_rows, n_in, *refs):
    total = refs[0][...].astype(jnp.float32)
    for r in refs[1:n_in]:
        total = total + r[...].astype(jnp.float32)
    start = 0
    for r in refs[n_in:]:
        r[...] = total[start : start + r.shape[0]].astype(r.dtype)
        start += r.shape[0]


def add(arrays, keep, send, name):
    width = arrays[0].shape[1]
    out = [sds((r, width), jnp.float32) for r in keep]
    out += [sds((r, width), jnp.bfloat16) for r in send]
    out = call(
        functools.partial(add_kernel, sum(keep), len(arrays)),
        out,
        [(VMEM, a) for a in arrays],
        name=name,
        cost_us=0.2,
    )
    return out[: len(keep)], out[len(keep) :]


def norm_kernel(n_parts, residual_ref, gain_ref, info_ref, *refs):
    parts = refs[:n_parts]
    stream_ref, normed_ref = refs[-2:]
    width = residual_ref.shape[1]
    mixed = parts[0][...].astype(jnp.float32)
    for p in parts[1:]:
        mixed = mixed + p[...].astype(jnp.float32)
    stream = residual_ref[...] + mixed
    stream_ref[...] = stream
    meansq = jnp.mean(stream * stream, axis=1, keepdims=True)
    normed_ref[:, :width] = (stream * lax.rsqrt(meansq + norm_eps) * gain_ref[...]).astype(
        jnp.bfloat16
    )
    normed_ref[:, width:] = info_ref[...]


def experts_kernel(experts, capacity, tile, halves, n_rows, n_gate, n_up, *refs):
    rows_in = refs[:n_rows]
    gate_refs = list(refs[n_rows : n_rows + n_gate])
    up_refs = list(refs[n_rows + n_gate : n_rows + n_gate + n_up])
    refs = refs[n_rows + n_gate + n_up :]
    up_hbm, down_hbm, keep_ref, send_ref, rows_ref, pick_ref, packed_ref, hidden_ref = refs[:8]
    up_late = list(refs[8 : 8 + experts - n_up])
    down_ref, up_sem, down_sem = refs[8 + experts - n_up :]
    per_expert, width = down_hbm.shape[0] // experts, down_hbm.shape[1]
    up_copies = [
        pltpu.make_async_copy(a, b, up_sem.at[i])
        for i, (a, b) in enumerate(columns(up_hbm, up_late, n_up))
    ]
    up_refs += up_late
    down_copies = [
        pltpu.make_async_copy(
            down_hbm.at[pl.ds(x * per_expert, per_expert)], down_ref, down_sem.at[x]
        )
        for x in range(experts)
    ]
    for c in down_copies[:1] + up_copies:
        c.start()
    count = 0
    for r in rows_in:
        rows_ref[count : count + r.shape[0], :] = r[...]
        count += r.shape[0]
    at0 = lax.broadcasted_iota(jnp.int32, (count, count), 0)
    at1 = lax.broadcasted_iota(jnp.int32, (count, count), 1)
    eye = jnp.where(at0 == at1, 1.0, 0.0).astype(jnp.bfloat16)
    before = jnp.where(at0 < at1, 1.0, 0.0).astype(jnp.bfloat16)
    info = lax.dot_general(
        rows_ref[:, width:], eye, (((0,), (0,)), ((), ())), preferred_element_type=jnp.float32
    )
    id0, id1, code0, code1 = (info[i : i + 1, :] for i in range(4))
    slot_of = lax.broadcasted_iota(jnp.int32, (capacity, count), 0).astype(jnp.float32)
    first = lax.axis_index("sec") * experts if halves == 1 else lax.axis_index("sec") // halves
    picks, shares = [], []
    for x in range(experts):
        e = (first + x).astype(jnp.float32)
        hit0 = jnp.where(id0 == e, 1.0, 0.0)
        hit1 = jnp.where(id1 == e, 1.0, 0.0)
        member = hit0 + hit1
        share = (hit0 * code0 + hit1 * code1) / (code0 + code1)
        slot = dot(jnp.broadcast_to(member, (8, count)).astype(jnp.bfloat16), before)[:1]
        slot = jnp.where(member > 0.5, slot, -1.0)
        pick = slot == slot_of
        shares.append(jnp.sum(jnp.where(pick, share, 0.0), axis=1, keepdims=True))
        picks.append(jnp.where(pick, 1.0, 0.0).astype(jnp.bfloat16))
    pick_ref[...] = jnp.concatenate(picks, axis=0)
    column = min(512, width)

    for c in range(0, width, column):
        packed_ref[:, c : c + column] = dot(pick_ref[...], rows_ref[:, c : c + column]).astype(
            jnp.bfloat16
        )
    for x in range(experts):
        mine = slice(x * capacity, (x + 1) * capacity)
        if x >= n_up:
            up_copies[x - n_up].wait()
        gate_ref, up_ref = gate_refs[x], up_refs[x]

        for s in range(0, per_expert, tile):
            cut = slice(s, s + tile)
            gate = dot(packed_ref[mine, :], gate_ref[:, cut])
            up = dot(packed_ref[mine, :], up_ref[:, cut])
            half = 0.5 * gate
            hidden_ref[mine, cut] = ((half + half * jnp.tanh(half)) * up).astype(jnp.bfloat16)
        down_copies[x].wait()

        for c in range(0, width, column):
            out = dot(hidden_ref[mine, :], down_ref[:, c : c + column])
            packed_ref[mine, c : c + column] = (out * shares[x]).astype(jnp.bfloat16)
        if x + 1 < experts:
            down_copies[x + 1].start()
    kept = keep_ref.shape[0]

    for c in range(0, width, column):
        out = lax.dot_general(
            pick_ref[...], packed_ref[:, c : c + column], (((0,), (0,)), ((), ())),
            preferred_element_type=jnp.float32,
        )
        keep_ref[:, c : c + column] = out[:kept]
        send_ref[:, c : c + column] = out[kept:].astype(jnp.bfloat16)


def per_device(
    query,
    keys,
    values,
    residual,
    out_weight,
    norm_gain,
    expert_ids,
    gate_codes,
    doc_lengths,
    w_gate,
    w_up,
    w_down,
):
    block, width = residual.shape
    head = HEAD_DIMENSION
    group_width = QUERY_HEAD_COUNT // KEY_VALUE_HEADS
    q_heads = query.shape[1] // head
    sec_count, tp_count, pp_count = (lax.axis_size(a) for a in ("sec", "tp", "pp"))
    own_rows = block // (tp_count * pp_count)
    bf16, f32 = jnp.bfloat16, jnp.float32

    kv_heads = max(1, q_heads // group_width)
    group = q_heads // kv_heads
    kv_start = lax.axis_index("pp") * q_heads // group_width * head
    kv = jnp.concatenate(
        [lax.dynamic_slice_in_dim(a, kv_start, kv_heads * head, 1) for a in (keys, values)], axis=1
    )
    back = -(-(sec_count * block // 2 - 1) // block)
    pieces = [
        lax.ppermute(kv, "sec", [(i, (i + k) % sec_count) for i in range(sec_count)])
        for k in range(back, 0, -1)
    ] + [kv]

    experts = max(1, E // sec_count)
    per_expert = w_gate.shape[2] // experts
    span = (back + 1) * block
    query_v, weight_v, gain_v, mask, order, residual_own, info, *gate_v = call(
        functools.partial(prepare_kernel, back, tp_count, pp_count),
        [
            sds(query.shape, bf16),
            sds(out_weight.shape, bf16),
            sds((1, width), f32),
            sds((block, span), f32),
            sds((block, block), bf16),
            sds((own_rows, width), f32),
            sds((own_rows, LANES), bf16),
        ]
        + [sds((width, per_expert), bf16)] * experts,
        [
            (HBM, a)
            for a in (
                doc_lengths, expert_ids.T, gate_codes.T, query, out_weight, residual,
                norm_gain.reshape(1, width), w_gate[0],
            )
        ],
        scratch=[
            pltpu.SMEM(doc_lengths.shape, jnp.int32),
            pltpu.VMEM((2, block), jnp.int32),
            pltpu.VMEM((2, block), jnp.int32),
            pltpu.VMEM(residual.shape, bf16),
            pltpu.SemaphoreType.DMA((7 + experts,)),
        ],
        vmem=6,
        name="prepare",
        cost_us=6.0,
    )
    half = block // pp_count
    keep, send = call(
        functools.partial(attention_kernel, back, kv_heads, group),
        [sds((half, width), f32), sds((block - half, width), bf16)],
        [(VMEM, a) for a in (query_v, mask, order, *pieces, weight_v)],
        scratch=[pltpu.VMEM(query.shape, bf16)],
        name="attention",
        cost_us=2.4,
    )

    (own,), sends = add(
        [keep] + [xor_swap(send, "pp", 1)], [own_rows], [own_rows] * (tp_count - 1), "sum_cores"
    )
    got = [xor_swap(sends[k - 1], "tp", k) for k in range(1, tp_count)]
    up_v, token = load(w_up[0], experts, 1, [own], "load_up")
    stream, normed = call(
        functools.partial(norm_kernel, tp_count),
        [sds((own_rows, width), f32), sds((own_rows, width + LANES), bf16)],
        [(VMEM, a) for a in (residual_own, gain_v, info, own, *got)] + [(ANY, token)],
        name="norm",
        cost_us=0.2,
    )

    groups = min(4, sec_count)
    near = {k: xor_swap(normed, "sec", k) if k else normed for k in range(0, sec_count, 2)}
    near.update({k + 1: xor_swap(near[k], "sec", 1) for k in list(near) if k + 1 < sec_count})
    near = [near[k] for k in range(sec_count)]
    per_group = sec_count // groups
    near = [
        jnp.concatenate(near[g * per_group : (g + 1) * per_group], axis=0)
        if per_group > 1
        else near[g]
        for g in range(groups)
    ]
    rows = [[r] + [xor_swap(r, "tp", k) for k in range(1, tp_count)] for r in near]
    rows = [rows[g][k] for k in range(tp_count) for g in range(groups)]
    rows = rows + [xor_swap(r, "pp", k) for k in range(1, pp_count) for r in rows]

    halves = max(1, sec_count // E)
    count = sec_count * block
    capacity = sec_count * MOSTB
    down = w_down[0]
    tile = min(512, down.shape[0] // experts)
    kept = count // pp_count
    keep, send = call(
        functools.partial(experts_kernel, experts, capacity, tile, halves, len(rows), experts, 1),
        [sds((kept, width), f32), sds((count - kept, width), bf16)],
        [(VMEM, a) for a in (*rows, *gate_v, *up_v)] + [(HBM, w_up[0]), (HBM, down)],
        scratch=[
            pltpu.VMEM((count, width + LANES), bf16),
            pltpu.VMEM((experts * capacity, count), bf16),
            pltpu.VMEM((experts * capacity, width), bf16),
            pltpu.VMEM((experts * capacity, down.shape[0] // experts), bf16),
            *[pltpu.VMEM((width, per_expert), bf16)] * (experts - 1),
            pltpu.VMEM((per_expert, width), bf16),
            pltpu.SemaphoreType.DMA((experts,)),
            pltpu.SemaphoreType.DMA((experts,)),
        ],
        vmem=24,
        name="experts",
        cost_us=12.0,
    )

    piece = kept // (tp_count * groups)
    own, sends = add(
        [keep, xor_swap(send, "pp", 1)], [piece] * groups, [piece] * (groups * (tp_count - 1)), "sum_cores2"
    )
    final = [stream]
    for g in list(range(1, groups)) + [0]:
        got = [xor_swap(sends[(k - 1) * groups + g], "tp", k) for k in range(1, tp_count)]
        if g == 0 and per_group == 1:
            final += [own[0]] + got
            continue
        kept_rows = own_rows if g == 0 else 0
        mine, out = add(
            [own[g]] + got,
            [own_rows] if g == 0 else [],
            [own_rows] * (per_group - (g == 0)),
            "sum_x%d" % g,
        )
        final += list(mine)
        for j, o in enumerate(out):
            final.append(xor_swap(o, "sec", g * per_group + j + (g == 0)))
    return call(
        functools.partial(add_kernel, 0, len(final)),
        [sds((own_rows, width), bf16)],
        [(VMEM, a) for a in final],
        name="total",
        cost_us=0.2,
    )[0]


def solution(mesh):
    in_specs = (
        P(("groups", "sec"), ("tp", "pp")),
        P(("groups", "sec"), "tp"),
        P(("groups", "sec"), "tp"),
        P(("groups", "sec"), None),
        P(("tp", "pp"), None),
        P(),
        P(("groups", "sec"), None),
        P(("groups", "sec"), None),
        P("groups"),
        P(("tp", "pp"), None, "sec"),
        P(("tp", "pp"), None, "sec"),
        P(("tp", "pp"), "sec", None),
    )
    out_specs = P(("groups", "sec", "tp", "pp"), None)
    return jax.shard_map(
        per_device, mesh=mesh, in_specs=in_specs, out_specs=out_specs, check_vma=False
    )
```

```python
import functools

import jax
import jax.numpy as jnp
from jax import lax
from jax.experimental import pallas as pl
from jax.experimental.pallas import tpu as pltpu
from jax.sharding import PartitionSpec as P

QUERY_HEAD_COUNT = 32
KEY_VALUE_HEADS = 8
HEAD_DIMENSION = 128
E = 8
MOSTB = 32
LANES = 128

neg_fill = -1e30
norm_eps = 1e-05

VMEM = pl.BlockSpec(memory_space=pltpu.VMEM)
SMEM = pl.BlockSpec(memory_space=pltpu.SMEM)
HBM = pl.BlockSpec(memory_space=pltpu.HBM)
ANY = pl.BlockSpec(memory_space=pl.ANY)
MIB = 2**20


def dot(a, b):
    return jnp.dot(a, b, preferred_element_type=jnp.float32)


def xor_swap(x, axis, k):
    n = lax.axis_size(axis)
    return lax.ppermute(x, axis, [(i, i ^ k) for i in range(n)])


def call(kernel, out_shape, args, scratch=(), vmem=8, name=None, cost_us=1.0):
    args = [
        (s, pltpu.with_memory_space_constraint(a, pltpu.HBM) if s is HBM else a) for s, a in args
    ]
    single = not isinstance(out_shape, (tuple, list))
    return pl.pallas_call(
        kernel,
        out_shape=out_shape,
        in_specs=[s for s, _ in args],
        out_specs=VMEM if single else [VMEM] * len(out_shape),
        scratch_shapes=list(scratch),
        compiler_params=pltpu.CompilerParams(vmem_limit_bytes=vmem * MIB),
        cost_estimate=pl.CostEstimate(
            flops=0, bytes_accessed=int(cost_us * 3.4e6), transcendentals=0
        ),
        name=name,
    )(*[a for _, a in args])


def sds(shape, dtype):
    return jax.ShapeDtypeStruct(shape, dtype)


def position():
    rank = lax.axis_index("tp") * lax.axis_size("pp") + lax.axis_index("pp")
    return lax.axis_index("sec"), rank


def columns(source, targets, first=0):
    per = targets[0].shape[1] if targets else 0
    return [(source.at[:, pl.ds((first + i) * per, per)], t) for i, t in enumerate(targets)]


def prepare_kernel(
    back, tp_count, pp_count, lengths_hbm, ids_hbm, codes_hbm, query_hbm, weight_hbm, residual_hbm,
    gain_hbm, *refs
):
    gate_hbm, query_ref, weight_ref, gain_ref, mask_ref, order_ref, residual_ref, info_ref = refs[
        :8
    ]
    gate_refs = refs[8:-5]
    lengths, ids, codes, residual_all, sem = refs[-5:]
    pairs = [
        (lengths_hbm, lengths),
        (ids_hbm, ids),
        (codes_hbm, codes),
        (residual_hbm, residual_all),
        (query_hbm, query_ref),
        (gain_hbm, gain_ref),
        (weight_hbm, weight_ref),
    ] + columns(gate_hbm, gate_refs)
    copies = [pltpu.make_async_copy(a, b, sem.at[i]) for i, (a, b) in enumerate(pairs)]
    for c in copies:
        c.start()
    sec, rank = position()
    block = query_ref.shape[0]
    own_rows = residual_ref.shape[0]
    at = lax.broadcasted_iota(jnp.int32, (block, block), 0)
    to = lax.broadcasted_iota(jnp.int32, (block, block), 1)
    chunk = lax.div(at, own_rows)
    flip = lax.rem(chunk, tp_count) * pp_count + lax.div(chunk, tp_count)
    source = (rank ^ flip) * own_rows + lax.rem(at, own_rows)
    order_ref[...] = jnp.where(to == source, 1.0, 0.0).astype(jnp.bfloat16)
    own = lax.broadcasted_iota(jnp.int32, (own_rows, block), 0) + rank * own_rows
    own = jnp.where(own == lax.broadcasted_iota(jnp.int32, (own_rows, block), 1), 1.0, 0.0)
    own = own.astype(jnp.bfloat16)
    for c in copies[:4]:
        c.wait()
    span = (back + 1) * block
    rows = sec * block + lax.broadcasted_iota(jnp.int32, (block, span), 0)
    cols = (sec - back) * block + lax.broadcasted_iota(jnp.int32, (block, span), 1)
    first = jnp.zeros((block, span), jnp.int32)
    end = jnp.int32(0)
    for d in range(lengths.shape[0]):
        end = end + lengths[d]
        first = jnp.where(rows >= end, end, first)
    mask_ref[...] = jnp.where((cols <= rows) & (cols >= first), 1.0, 0.0)
    residual_ref[...] = dot(own, residual_all[...])
    info = jnp.concatenate(
        [ids[...], codes[...], jnp.zeros((LANES - 4, block), jnp.int32)], axis=0
    ).astype(jnp.float32)
    info_ref[...] = lax.dot_general(
        own, info.astype(jnp.bfloat16), (((1,), (1,)), ((), ())), preferred_element_type=jnp.float32
    ).astype(jnp.bfloat16)
    for c in copies[4:]:
        c.wait()


def load_kernel(n_after, source, *refs):
    *targets, token_ref, sem = refs[n_after:]
    copies = [
        pltpu.make_async_copy(a, b, sem.at[i])
        for i, (a, b) in enumerate(columns(source, targets))
    ]
    for c in copies:
        c.start()
    token_ref[...] = jnp.zeros_like(token_ref)
    for c in copies:
        c.wait()


def load(array, parts, wanted, after, name):
    rows, cols = array.shape
    out = call(
        functools.partial(load_kernel, len(after)),
        [sds((rows, cols // parts), array.dtype)] * wanted + [sds((8, LANES), jnp.float32)],
        [(HBM, array)] + [(ANY, a) for a in after],
        scratch=[pltpu.SemaphoreType.DMA((wanted,))],
        vmem=1,
        name=name,
        cost_us=array.size * wanted / parts * 2 / 3.4e6,
    )
    return out[:-1], out[-1]


def attention_kernel(back, kv_heads, group, q_ref, mask_ref, order_ref, *refs):
    kv_refs = refs[: back + 1]
    weight_ref, keep_ref, send_ref, attended_ref = refs[back + 1 :]
    block = q_ref.shape[0]
    head = HEAD_DIMENSION
    allowed = jnp.concatenate([mask_ref[...]] * group, axis=0) > 0.5
    for g in range(kv_heads):
        q = jnp.concatenate(
            [q_ref[:, (g * group + t) * head : (g * group + t + 1) * head] for t in range(group)],
            axis=0,
        )
        k = jnp.concatenate([r[:, g * head : (g + 1) * head] for r in kv_refs], axis=0)
        v = jnp.concatenate(
            [r[:, (kv_heads + g) * head : (kv_heads + g + 1) * head] for r in kv_refs], axis=0
        )
        scores = lax.dot_general(
            q, k, (((1,), (1,)), ((), ())), preferred_element_type=jnp.float32
        ) * (head**-0.5)
        scores = jnp.where(allowed, scores, neg_fill)
        top = jnp.max(scores, axis=1, keepdims=True)
        weights = jnp.where(allowed, jnp.exp(scores - top), 0.0)
        total = jnp.sum(weights, axis=1, keepdims=True)
        summed = dot(weights.astype(jnp.bfloat16), v) / total
        for t in range(group):
            attended_ref[:, (g * group + t) * head : (g * group + t + 1) * head] = summed[
                t * block : (t + 1) * block
            ].astype(jnp.bfloat16)
    attended = dot(order_ref[...], attended_ref[...]).astype(jnp.bfloat16)
    mixed = dot(attended, weight_ref[...])
    kept = keep_ref.shape[0]
    keep_ref[...] = mixed[:kept]
    send_ref[...] = mixed[kept:].astype(jnp.bfloat16)


def add_kernel(keep_rows, n_in, *refs):
    total = refs[0][...].astype(jnp.float32)
    for r in refs[1:n_in]:
        total = total + r[...].astype(jnp.float32)
    start = 0
    for r in refs[n_in:]:
        r[...] = total[start : start + r.shape[0]].astype(r.dtype)
        start += r.shape[0]


def add(arrays, keep, send, name):
    width = arrays[0].shape[1]
    out = [sds((r, width), jnp.float32) for r in keep]
    out += [sds((r, width), jnp.bfloat16) for r in send]
    out = call(
        functools.partial(add_kernel, sum(keep), len(arrays)),
        out,
        [(VMEM, a) for a in arrays],
        name=name,
        cost_us=0.2,
    )
    return out[: len(keep)], out[len(keep) :]


def norm_kernel(n_parts, residual_ref, gain_ref, info_ref, *refs):
    parts = refs[:n_parts]
    stream_ref, normed_ref = refs[-2:]
    width = residual_ref.shape[1]
    mixed = parts[0][...].astype(jnp.float32)
    for p in parts[1:]:
        mixed = mixed + p[...].astype(jnp.float32)
    stream = residual_ref[...] + mixed
    stream_ref[...] = stream
    meansq = jnp.mean(stream * stream, axis=1, keepdims=True)
    normed_ref[:, :width] = (stream * lax.rsqrt(meansq + norm_eps) * gain_ref[...]).astype(
        jnp.bfloat16
    )
    normed_ref[:, width:] = info_ref[...]


class Stream:
    def __init__(self, groups, sem, window):
        self.copies, self.last, self.window = [], {}, window
        for name, pairs in groups:
            for source, target in pairs:
                at = len(self.copies)
                self.copies.append(pltpu.make_async_copy(source, target, sem.at[at]))
            self.last[name] = len(self.copies)
        self.started = self.ended = 0
        self.limit = len(self.copies)
        self.clock = 0.0

    def fill(self):
        while self.started < self.limit and self.started - self.ended < self.window:
            self.copies[self.started].start()
            self.started += 1

    def end_one(self):
        self.copies[self.ended].wait()
        self.ended += 1
        self.fill()

    def need(self, name):
        while self.ended < self.last[name]:
            self.end_one()

    def step(self, cost):
        self.clock += cost
        while self.ended < self.started and self.ended + 2 <= self.clock:
            self.end_one()


def experts_kernel(experts, capacity, tile, halves, n_rows, *refs):
    rows_in = refs[:n_rows]
    gate_first, up_first, gate_hbm, up_hbm, down_hbm, keep_ref, send_ref = refs[
        n_rows : n_rows + 7
    ]
    rows_ref, pick_ref, packed_ref, hidden_ref, half_ref, gate_ref, up_ref, down_ref, sem = refs[
        n_rows + 7 :
    ]
    per_expert, width = down_hbm.shape[0] // experts, down_hbm.shape[1]
    column = min(512, width)
    cuts = 4

    def quarters(source, target, x, columns):
        rows = target.shape[0] // cuts
        pairs = []
        for i in range(cuts):
            to = pl.ds(i * rows, rows)
            if columns:
                part = source.at[to, pl.ds(x * per_expert, per_expert)]
            else:
                part = source.at[pl.ds(x * per_expert + i * rows, rows)]
            pairs.append((part, target.at[to]))
        return pairs

    groups = []
    for x in range(experts):
        if x:
            groups.append((("gate", x), quarters(gate_hbm, gate_ref.at[x - 1], x, True)))
            groups.append((("up", x), quarters(up_hbm, up_ref.at[x - 1], x, True)))
        groups.append((("down", x), quarters(down_hbm, down_ref, x, False)))
    stream = Stream(groups, sem, 3)
    stream.limit = stream.last["up", 1] if experts > 1 else stream.limit
    stream.fill()
    count = 0
    for r in rows_in:
        rows_ref[count : count + r.shape[0], :] = r[...]
        count += r.shape[0]
    at0 = lax.broadcasted_iota(jnp.int32, (count, count), 0)
    at1 = lax.broadcasted_iota(jnp.int32, (count, count), 1)
    eye = jnp.where(at0 == at1, 1.0, 0.0).astype(jnp.bfloat16)
    before = jnp.where(at0 < at1, 1.0, 0.0).astype(jnp.bfloat16)
    info = lax.dot_general(
        rows_ref[:, width:], eye, (((0,), (0,)), ((), ())), preferred_element_type=jnp.float32
    )
    id0, id1, code0, code1 = (info[i : i + 1, :] for i in range(4))
    slot_of = lax.broadcasted_iota(jnp.int32, (capacity, count), 0).astype(jnp.float32)
    first = lax.axis_index("sec") * experts if halves == 1 else lax.axis_index("sec") // halves
    picks, shares = [], []
    for x in range(experts):
        e = (first + x).astype(jnp.float32)
        hit0 = jnp.where(id0 == e, 1.0, 0.0)
        hit1 = jnp.where(id1 == e, 1.0, 0.0)
        member = hit0 + hit1
        share = (hit0 * code0 + hit1 * code1) / (code0 + code1)
        slot = dot(jnp.broadcast_to(member, (8, count)).astype(jnp.bfloat16), before)[:1]
        slot = jnp.where(member > 0.5, slot, -1.0)
        pick = slot == slot_of
        shares.append(jnp.sum(jnp.where(pick, share, 0.0), axis=1, keepdims=True))
        picks.append(jnp.where(pick, 1.0, 0.0).astype(jnp.bfloat16))
    pick_ref[...] = jnp.concatenate(picks, axis=0)
    column = min(512, width)

    for c in range(0, width, column):
        packed_ref[:, c : c + column] = dot(pick_ref[...], rows_ref[:, c : c + column]).astype(
            jnp.bfloat16
        )
    for x in range(experts):
        mine = slice(x * capacity, (x + 1) * capacity)
        if x:
            stream.need(("gate", x))
        for s in range(0, per_expert, tile):
            cut = slice(s, s + tile)
            stream.step(0.7)
            gate = dot(packed_ref[mine, :], gate_ref[x - 1, :, cut] if x else gate_first[:, cut])
            half = 0.5 * gate
            half_ref[:, cut] = half + half * jnp.tanh(half)
        if x:
            stream.need(("up", x))
        for s in range(0, per_expert, tile):
            cut = slice(s, s + tile)
            stream.step(0.7)
            up = dot(packed_ref[mine, :], up_ref[x - 1, :, cut] if x else up_first[:, cut])
            hidden_ref[mine, cut] = (half_ref[:, cut] * up).astype(jnp.bfloat16)
        stream.need(("down", x))
        for c in range(0, width, column):
            stream.step(0.7)
            out = dot(hidden_ref[mine, :], down_ref[:, c : c + column])
            packed_ref[mine, c : c + column] = (out * shares[x]).astype(jnp.bfloat16)
        stream.limit = stream.last["up", x + 2] if x + 2 < experts else len(stream.copies)
        stream.fill()
    kept = keep_ref.shape[0]

    for c in range(0, width, column):
        out = lax.dot_general(
            pick_ref[...], packed_ref[:, c : c + column], (((0,), (0,)), ((), ())),
            preferred_element_type=jnp.float32,
        )
        keep_ref[:, c : c + column] = out[:kept]
        send_ref[:, c : c + column] = out[kept:].astype(jnp.bfloat16)


def per_device(
    query,
    keys,
    values,
    residual,
    out_weight,
    norm_gain,
    expert_ids,
    gate_codes,
    doc_lengths,
    w_gate,
    w_up,
    w_down,
):
    block, width = residual.shape
    head = HEAD_DIMENSION
    group_width = QUERY_HEAD_COUNT // KEY_VALUE_HEADS
    q_heads = query.shape[1] // head
    sec_count, tp_count, pp_count = (lax.axis_size(a) for a in ("sec", "tp", "pp"))
    own_rows = block // (tp_count * pp_count)
    bf16, f32 = jnp.bfloat16, jnp.float32

    kv_heads = max(1, q_heads // group_width)
    group = q_heads // kv_heads
    kv_start = lax.axis_index("pp") * q_heads // group_width * head
    kv = jnp.concatenate(
        [lax.dynamic_slice_in_dim(a, kv_start, kv_heads * head, 1) for a in (keys, values)], axis=1
    )
    back = -(-(sec_count * block // 2 - 1) // block)
    pieces = [
        lax.ppermute(kv, "sec", [(i, (i + k) % sec_count) for i in range(sec_count)])
        for k in range(back, 0, -1)
    ] + [kv]

    experts = max(1, E // sec_count)
    per_expert = w_gate.shape[2] // experts
    span = (back + 1) * block
    query_v, weight_v, gain_v, mask, order, residual_own, info, *gate_v = call(
        functools.partial(prepare_kernel, back, tp_count, pp_count),
        [
            sds(query.shape, bf16),
            sds(out_weight.shape, bf16),
            sds((1, width), f32),
            sds((block, span), f32),
            sds((block, block), bf16),
            sds((own_rows, width), f32),
            sds((own_rows, LANES), bf16),
        ]
        + [sds((width, per_expert), bf16)],
        [
            (HBM, a)
            for a in (
                doc_lengths, expert_ids.T, gate_codes.T, query, out_weight, residual,
                norm_gain.reshape(1, width), w_gate[0],
            )
        ],
        scratch=[
            pltpu.SMEM(doc_lengths.shape, jnp.int32),
            pltpu.VMEM((2, block), jnp.int32),
            pltpu.VMEM((2, block), jnp.int32),
            pltpu.VMEM(residual.shape, bf16),
            pltpu.SemaphoreType.DMA((8,)),
        ],
        vmem=6,
        name="prepare",
        cost_us=4.0,
    )
    half = block // pp_count
    keep, send = call(
        functools.partial(attention_kernel, back, kv_heads, group),
        [sds((half, width), f32), sds((block - half, width), bf16)],
        [(VMEM, a) for a in (query_v, mask, order, *pieces, weight_v)],
        scratch=[pltpu.VMEM(query.shape, bf16)],
        name="attention",
        cost_us=2.4,
    )

    (own,), sends = add(
        [keep] + [xor_swap(send, "pp", 1)], [own_rows], [own_rows] * (tp_count - 1), "sum_cores"
    )
    got = [xor_swap(sends[k - 1], "tp", k) for k in range(1, tp_count)]
    up_v, token = load(w_up[0], experts, 1, [own], "load_up")
    stream, normed = call(
        functools.partial(norm_kernel, tp_count),
        [sds((own_rows, width), f32), sds((own_rows, width + LANES), bf16)],
        [(VMEM, a) for a in (residual_own, gain_v, info, own, *got)] + [(ANY, token)],
        name="norm",
        cost_us=0.2,
    )

    groups = min(4, sec_count)
    near = {k: xor_swap(normed, "sec", k) if k else normed for k in range(0, sec_count, 2)}
    near.update({k + 1: xor_swap(near[k], "sec", 1) for k in list(near) if k + 1 < sec_count})
    near = [near[k] for k in range(sec_count)]
    per_group = sec_count // groups
    near = [
        jnp.concatenate(near[g * per_group : (g + 1) * per_group], axis=0)
        if per_group > 1
        else near[g]
        for g in range(groups)
    ]
    rows = [[r] + [xor_swap(r, "tp", k) for k in range(1, tp_count)] for r in near]
    rows = [rows[g][k] for k in range(tp_count) for g in range(groups)]
    rows = rows + [xor_swap(r, "pp", k) for k in range(1, pp_count) for r in rows]

    halves = max(1, sec_count // E)
    count = sec_count * block
    capacity = sec_count * MOSTB
    down = w_down[0]
    tile = min(512, down.shape[0] // experts)
    kept = count // pp_count
    keep, send = call(
        functools.partial(experts_kernel, experts, capacity, tile, halves, len(rows)),
        [sds((kept, width), f32), sds((count - kept, width), bf16)],
        [(VMEM, a) for a in (*rows, *gate_v, *up_v)]
        + [(HBM, a) for a in (w_gate[0], w_up[0], down)],
        scratch=[
            pltpu.VMEM((count, width + LANES), bf16),
            pltpu.VMEM((experts * capacity, count), bf16),
            pltpu.VMEM((experts * capacity, width), bf16),
            pltpu.VMEM((experts * capacity, down.shape[0] // experts), bf16),
            pltpu.VMEM((capacity, per_expert), f32),
            pltpu.VMEM((max(1, experts - 1), width, per_expert), bf16),
            pltpu.VMEM((max(1, experts - 1), width, per_expert), bf16),
            pltpu.VMEM((per_expert, width), bf16),
            pltpu.SemaphoreType.DMA((4 * (3 * experts - 2),)),
        ],
        vmem=33,
        name="experts",
        cost_us=12.0,
    )

    piece = kept // (tp_count * groups)
    own, sends = add(
        [keep, xor_swap(send, "pp", 1)], [piece] * groups, [piece] * (groups * (tp_count - 1)), "sum_cores2"
    )
    final = [stream]
    for g in list(range(1, groups)) + [0]:
        got = [xor_swap(sends[(k - 1) * groups + g], "tp", k) for k in range(1, tp_count)]
        if g == 0 and per_group == 1:
            final += [own[0]] + got
            continue
        kept_rows = own_rows if g == 0 else 0
        mine, out = add(
            [own[g]] + got,
            [own_rows] if g == 0 else [],
            [own_rows] * (per_group - (g == 0)),
            "sum_x%d" % g,
        )
        final += list(mine)
        for j, o in enumerate(out):
            final.append(xor_swap(o, "sec", g * per_group + j + (g == 0)))
    return call(
        functools.partial(add_kernel, 0, len(final)),
        [sds((own_rows, width), bf16)],
        [(VMEM, a) for a in final],
        name="total",
        cost_us=0.2,
    )[0]


def solution(mesh):
    in_specs = (
        P(("groups", "sec"), ("tp", "pp")),
        P(("groups", "sec"), "tp"),
        P(("groups", "sec"), "tp"),
        P(("groups", "sec"), None),
        P(("tp", "pp"), None),
        P(),
        P(("groups", "sec"), None),
        P(("groups", "sec"), None),
        P("groups"),
        P(("tp", "pp"), None, "sec"),
        P(("tp", "pp"), None, "sec"),
        P(("tp", "pp"), "sec", None),
    )
    out_specs = P(("groups", "sec", "tp", "pp"), None)
    return jax.shard_map(
        per_device, mesh=mesh, in_specs=in_specs, out_specs=out_specs, check_vma=False
    )
```

```python
import functools

import jax
import jax.numpy as jnp
from jax import lax
from jax.experimental import pallas as pl
from jax.experimental.pallas import tpu as pltpu
from jax.sharding import PartitionSpec as P

QUERY_HEAD_COUNT = 32
KEY_VALUE_HEADS = 8
HEAD_DIMENSION = 128
E = 8
MOSTB = 32
LANES = 128

neg_fill = -1e30
norm_eps = 1e-05

VMEM = pl.BlockSpec(memory_space=pltpu.VMEM)
SMEM = pl.BlockSpec(memory_space=pltpu.SMEM)
HBM = pl.BlockSpec(memory_space=pltpu.HBM)
ANY = pl.BlockSpec(memory_space=pl.ANY)
MIB = 2**20


def dot(a, b):
    return jnp.dot(a, b, preferred_element_type=jnp.float32)


def xor_swap(x, axis, k):
    n = lax.axis_size(axis)
    return lax.ppermute(x, axis, [(i, i ^ k) for i in range(n)])


def call(kernel, out_shape, args, scratch=(), vmem=8, name=None, cost_us=1.0):
    args = [
        (s, pltpu.with_memory_space_constraint(a, pltpu.HBM) if s is HBM else a) for s, a in args
    ]
    single = not isinstance(out_shape, (tuple, list))
    return pl.pallas_call(
        kernel,
        out_shape=out_shape,
        in_specs=[s for s, _ in args],
        out_specs=VMEM if single else [VMEM] * len(out_shape),
        scratch_shapes=list(scratch),
        compiler_params=pltpu.CompilerParams(vmem_limit_bytes=vmem * MIB),
        cost_estimate=pl.CostEstimate(
            flops=0, bytes_accessed=int(cost_us * 3.4e6), transcendentals=0
        ),
        name=name,
    )(*[a for _, a in args])


def sds(shape, dtype):
    return jax.ShapeDtypeStruct(shape, dtype)


def position():
    rank = lax.axis_index("tp") * lax.axis_size("pp") + lax.axis_index("pp")
    return lax.axis_index("sec"), rank


def columns(source, targets, first=0):
    per = targets[0].shape[1] if targets else 0
    return [(source.at[:, pl.ds((first + i) * per, per)], t) for i, t in enumerate(targets)]


def prepare_kernel(
    back, tp_count, pp_count, lengths_hbm, ids_hbm, codes_hbm, query_hbm, weight_hbm, residual_hbm,
    gain_hbm, *refs
):
    gate_hbm, query_ref, weight_ref, gain_ref, mask_ref, order_ref, residual_ref, info_ref = refs[
        :8
    ]
    gate_refs = refs[8:-5]
    lengths, ids, codes, residual_all, sem = refs[-5:]
    pairs = [
        (lengths_hbm, lengths),
        (ids_hbm, ids),
        (codes_hbm, codes),
        (residual_hbm, residual_all),
        (query_hbm, query_ref),
        (gain_hbm, gain_ref),
        (weight_hbm, weight_ref),
    ] + columns(gate_hbm, gate_refs)
    copies = [pltpu.make_async_copy(a, b, sem.at[i]) for i, (a, b) in enumerate(pairs)]
    for c in copies:
        c.start()
    sec, rank = position()
    block = query_ref.shape[0]
    own_rows = residual_ref.shape[0]
    at = lax.broadcasted_iota(jnp.int32, (block, block), 0)
    to = lax.broadcasted_iota(jnp.int32, (block, block), 1)
    chunk = lax.div(at, own_rows)
    flip = lax.rem(chunk, tp_count) * pp_count + lax.div(chunk, tp_count)
    source = (rank ^ flip) * own_rows + lax.rem(at, own_rows)
    order_ref[...] = jnp.where(to == source, 1.0, 0.0).astype(jnp.bfloat16)
    own = lax.broadcasted_iota(jnp.int32, (own_rows, block), 0) + rank * own_rows
    own = jnp.where(own == lax.broadcasted_iota(jnp.int32, (own_rows, block), 1), 1.0, 0.0)
    own = own.astype(jnp.bfloat16)
    for c in copies[:4]:
        c.wait()
    span = (back + 1) * block
    rows = sec * block + lax.broadcasted_iota(jnp.int32, (block, span), 0)
    cols = (sec - back) * block + lax.broadcasted_iota(jnp.int32, (block, span), 1)
    first = jnp.zeros((block, span), jnp.int32)
    end = jnp.int32(0)
    for d in range(lengths.shape[0]):
        end = end + lengths[d]
        first = jnp.where(rows >= end, end, first)
    mask_ref[...] = jnp.where((cols <= rows) & (cols >= first), 1.0, 0.0)
    residual_ref[...] = dot(own, residual_all[...])
    info = jnp.concatenate(
        [ids[...], codes[...], jnp.zeros((LANES - 4, block), jnp.int32)], axis=0
    ).astype(jnp.float32)
    info_ref[...] = lax.dot_general(
        own, info.astype(jnp.bfloat16), (((1,), (1,)), ((), ())), preferred_element_type=jnp.float32
    ).astype(jnp.bfloat16)
    for c in copies[4:]:
        c.wait()


def load_kernel(n_after, source, *refs):
    *targets, token_ref, sem = refs[n_after:]
    copies = [
        pltpu.make_async_copy(a, b, sem.at[i])
        for i, (a, b) in enumerate(columns(source, targets))
    ]
    for c in copies:
        c.start()
    token_ref[...] = jnp.zeros_like(token_ref)
    for c in copies:
        c.wait()


def load(array, parts, wanted, after, name):
    rows, cols = array.shape
    out = call(
        functools.partial(load_kernel, len(after)),
        [sds((rows, cols // parts), array.dtype)] * wanted + [sds((8, LANES), jnp.float32)],
        [(HBM, array)] + [(ANY, a) for a in after],
        scratch=[pltpu.SemaphoreType.DMA((wanted,))],
        vmem=1,
        name=name,
        cost_us=array.size * wanted / parts * 2 / 3.4e6,
    )
    return out[:-1], out[-1]


def attention_kernel(back, kv_heads, group, q_ref, mask_ref, order_ref, *refs):
    kv_refs = refs[: back + 1]
    weight_ref, keep_ref, send_ref, attended_ref = refs[back + 1 :]
    block = q_ref.shape[0]
    head = HEAD_DIMENSION
    allowed = jnp.concatenate([mask_ref[...]] * group, axis=0) > 0.5
    for g in range(kv_heads):
        q = jnp.concatenate(
            [q_ref[:, (g * group + t) * head : (g * group + t + 1) * head] for t in range(group)],
            axis=0,
        )
        k = jnp.concatenate([r[:, g * head : (g + 1) * head] for r in kv_refs], axis=0)
        v = jnp.concatenate(
            [r[:, (kv_heads + g) * head : (kv_heads + g + 1) * head] for r in kv_refs], axis=0
        )
        scores = lax.dot_general(
            q, k, (((1,), (1,)), ((), ())), preferred_element_type=jnp.float32
        ) * (head**-0.5)
        scores = jnp.where(allowed, scores, neg_fill)
        top = jnp.max(scores, axis=1, keepdims=True)
        weights = jnp.where(allowed, jnp.exp(scores - top), 0.0)
        total = jnp.sum(weights, axis=1, keepdims=True)
        summed = dot(weights.astype(jnp.bfloat16), v) / total
        for t in range(group):
            attended_ref[:, (g * group + t) * head : (g * group + t + 1) * head] = summed[
                t * block : (t + 1) * block
            ].astype(jnp.bfloat16)
    attended = dot(order_ref[...], attended_ref[...]).astype(jnp.bfloat16)
    mixed = dot(attended, weight_ref[...])
    kept = keep_ref.shape[0]
    keep_ref[...] = mixed[:kept]
    send_ref[...] = mixed[kept:].astype(jnp.bfloat16)


def add_kernel(keep_rows, n_in, *refs):
    total = refs[0][...].astype(jnp.float32)
    for r in refs[1:n_in]:
        total = total + r[...].astype(jnp.float32)
    start = 0
    for r in refs[n_in:]:
        r[...] = total[start : start + r.shape[0]].astype(r.dtype)
        start += r.shape[0]


def add(arrays, keep, send, name):
    width = arrays[0].shape[1]
    out = [sds((r, width), jnp.float32) for r in keep]
    out += [sds((r, width), jnp.bfloat16) for r in send]
    out = call(
        functools.partial(add_kernel, sum(keep), len(arrays)),
        out,
        [(VMEM, a) for a in arrays],
        name=name,
        cost_us=0.2,
    )
    return out[: len(keep)], out[len(keep) :]


def norm_kernel(n_parts, residual_ref, gain_ref, info_ref, *refs):
    parts = refs[:n_parts]
    stream_ref, normed_ref = refs[-2:]
    width = residual_ref.shape[1]
    mixed = parts[0][...].astype(jnp.float32)
    for p in parts[1:]:
        mixed = mixed + p[...].astype(jnp.float32)
    stream = residual_ref[...] + mixed
    stream_ref[...] = stream
    meansq = jnp.mean(stream * stream, axis=1, keepdims=True)
    normed_ref[:, :width] = (stream * lax.rsqrt(meansq + norm_eps) * gain_ref[...]).astype(
        jnp.bfloat16
    )
    normed_ref[:, width:] = info_ref[...]


class Stream:
    def __init__(self, groups, sem, window):
        self.copies, self.last, self.window = [], {}, window
        for name, pairs in groups:
            for source, target in pairs:
                at = len(self.copies)
                self.copies.append(pltpu.make_async_copy(source, target, sem.at[at]))
            self.last[name] = len(self.copies)
        self.started = self.ended = 0
        self.limit = len(self.copies)
        self.clock = 0.0

    def fill(self):
        while self.started < self.limit and self.started - self.ended < self.window:
            self.copies[self.started].start()
            self.started += 1

    def end_one(self):
        self.copies[self.ended].wait()
        self.ended += 1
        self.fill()

    def need(self, name, but=0):
        while self.ended < self.last[name] - but:
            self.end_one()

    def step(self, cost):
        self.clock += cost
        while self.ended < self.started and self.ended + 2 <= self.clock:
            self.end_one()


def experts_kernel(experts, capacity, tile, halves, n_rows, *refs):
    rows_in = refs[:n_rows]
    gate_first, up_first, gate_hbm, up_hbm, down_hbm, keep_ref, send_ref = refs[
        n_rows : n_rows + 7
    ]
    rows_ref, pick_ref, packed_ref, hidden_ref, half_ref, sum_ref, gate_ref, up_ref, down_ref, sem = refs[
        n_rows + 7 :
    ]
    per_expert, width = down_hbm.shape[0] // experts, down_hbm.shape[1]
    column = min(512, width)
    cuts = 4

    def quarters(source, target, x, columns):
        rows = target.shape[0] // cuts
        pairs = []
        for i in range(cuts):
            to = pl.ds(i * rows, rows)
            if columns:
                part = source.at[to, pl.ds(x * per_expert, per_expert)]
            else:
                part = source.at[pl.ds(x * per_expert + i * rows, rows)]
            pairs.append((part, target.at[to]))
        return pairs

    groups = []
    for x in range(experts):
        if x:
            groups.append((("gate", x), quarters(gate_hbm, gate_ref.at[x - 1], x, True)))
            groups.append((("up", x), quarters(up_hbm, up_ref.at[x - 1], x, True)))
        groups.append((("down", x), quarters(down_hbm, down_ref, x, False)))
    stream = Stream(groups, sem, 4)
    stream.limit = stream.last["up", 1] if experts > 1 else stream.limit
    stream.fill()
    count = 0
    for r in rows_in:
        rows_ref[count : count + r.shape[0], :] = r[...]
        count += r.shape[0]
    at0 = lax.broadcasted_iota(jnp.int32, (count, count), 0)
    at1 = lax.broadcasted_iota(jnp.int32, (count, count), 1)
    eye = jnp.where(at0 == at1, 1.0, 0.0).astype(jnp.bfloat16)
    before = jnp.where(at0 < at1, 1.0, 0.0).astype(jnp.bfloat16)
    info = lax.dot_general(
        rows_ref[:, width:], eye, (((0,), (0,)), ((), ())), preferred_element_type=jnp.float32
    )
    id0, id1, code0, code1 = (info[i : i + 1, :] for i in range(4))
    slot_of = lax.broadcasted_iota(jnp.int32, (capacity, count), 0).astype(jnp.float32)
    first = lax.axis_index("sec") * experts if halves == 1 else lax.axis_index("sec") // halves
    picks, shares = [], []
    for x in range(experts):
        e = (first + x).astype(jnp.float32)
        hit0 = jnp.where(id0 == e, 1.0, 0.0)
        hit1 = jnp.where(id1 == e, 1.0, 0.0)
        member = hit0 + hit1
        share = (hit0 * code0 + hit1 * code1) / (code0 + code1)
        slot = dot(jnp.broadcast_to(member, (8, count)).astype(jnp.bfloat16), before)[:1]
        slot = jnp.where(member > 0.5, slot, -1.0)
        pick = slot == slot_of
        shares.append(jnp.sum(jnp.where(pick, share, 0.0), axis=1, keepdims=True))
        picks.append(jnp.where(pick, 1.0, 0.0).astype(jnp.bfloat16))
    pick_ref[...] = jnp.concatenate(picks, axis=0)
    column = min(512, width)

    for c in range(0, width, column):
        packed_ref[:, c : c + column] = dot(pick_ref[...], rows_ref[:, c : c + column]).astype(
            jnp.bfloat16
        )
    for x in range(experts):
        mine = slice(x * capacity, (x + 1) * capacity)
        if x:
            stream.need(("gate", x))
        for s in range(0, per_expert, tile):
            cut = slice(s, s + tile)
            stream.step(0.85)
            gate = dot(packed_ref[mine, :], gate_ref[x - 1, :, cut] if x else gate_first[:, cut])
            half = 0.5 * gate
            half_ref[:, cut] = half + half * jnp.tanh(half)
        if x:
            stream.need(("up", x))
        for s in range(0, per_expert, tile):
            cut = slice(s, s + tile)
            stream.step(0.85)
            up = dot(packed_ref[mine, :], up_ref[x - 1, :, cut] if x else up_first[:, cut])
            hidden_ref[mine, cut] = (half_ref[:, cut] * up).astype(jnp.bfloat16)
        rows = per_expert // cuts
        for i in range(cuts):
            stream.need(("down", x), cuts - 1 - i)
            part = slice(i * rows, (i + 1) * rows)
            out = dot(hidden_ref[mine, part], down_ref[part, :])
            if i:
                out = out + sum_ref[...]
            if i < cuts - 1:
                sum_ref[...] = out
            else:
                packed_ref[mine, :] = (out * shares[x]).astype(jnp.bfloat16)
            stream.step(0.85)
        stream.limit = stream.last["up", x + 2] if x + 2 < experts else len(stream.copies)
        stream.fill()
    kept = keep_ref.shape[0]

    for c in range(0, width, column):
        out = lax.dot_general(
            pick_ref[...], packed_ref[:, c : c + column], (((0,), (0,)), ((), ())),
            preferred_element_type=jnp.float32,
        )
        keep_ref[:, c : c + column] = out[:kept]
        send_ref[:, c : c + column] = out[kept:].astype(jnp.bfloat16)


def per_device(
    query,
    keys,
    values,
    residual,
    out_weight,
    norm_gain,
    expert_ids,
    gate_codes,
    doc_lengths,
    w_gate,
    w_up,
    w_down,
):
    block, width = residual.shape
    head = HEAD_DIMENSION
    group_width = QUERY_HEAD_COUNT // KEY_VALUE_HEADS
    q_heads = query.shape[1] // head
    sec_count, tp_count, pp_count = (lax.axis_size(a) for a in ("sec", "tp", "pp"))
    own_rows = block // (tp_count * pp_count)
    bf16, f32 = jnp.bfloat16, jnp.float32

    kv_heads = max(1, q_heads // group_width)
    group = q_heads // kv_heads
    kv_start = lax.axis_index("pp") * q_heads // group_width * head
    kv = jnp.concatenate(
        [lax.dynamic_slice_in_dim(a, kv_start, kv_heads * head, 1) for a in (keys, values)], axis=1
    )
    back = -(-(sec_count * block // 2 - 1) // block)
    pieces = [
        lax.ppermute(kv, "sec", [(i, (i + k) % sec_count) for i in range(sec_count)])
        for k in range(back, 0, -1)
    ] + [kv]

    experts = max(1, E // sec_count)
    per_expert = w_gate.shape[2] // experts
    span = (back + 1) * block
    query_v, weight_v, gain_v, mask, order, residual_own, info, *gate_v = call(
        functools.partial(prepare_kernel, back, tp_count, pp_count),
        [
            sds(query.shape, bf16),
            sds(out_weight.shape, bf16),
            sds((1, width), f32),
            sds((block, span), f32),
            sds((block, block), bf16),
            sds((own_rows, width), f32),
            sds((own_rows, LANES), bf16),
        ]
        + [sds((width, per_expert), bf16)],
        [
            (HBM, a)
            for a in (
                doc_lengths, expert_ids.T, gate_codes.T, query, out_weight, residual,
                norm_gain.reshape(1, width), w_gate[0],
            )
        ],
        scratch=[
            pltpu.SMEM(doc_lengths.shape, jnp.int32),
            pltpu.VMEM((2, block), jnp.int32),
            pltpu.VMEM((2, block), jnp.int32),
            pltpu.VMEM(residual.shape, bf16),
            pltpu.SemaphoreType.DMA((8,)),
        ],
        vmem=6,
        name="prepare",
        cost_us=4.0,
    )
    half = block // pp_count
    keep, send = call(
        functools.partial(attention_kernel, back, kv_heads, group),
        [sds((half, width), f32), sds((block - half, width), bf16)],
        [(VMEM, a) for a in (query_v, mask, order, *pieces, weight_v)],
        scratch=[pltpu.VMEM(query.shape, bf16)],
        name="attention",
        cost_us=2.4,
    )

    (own,), sends = add(
        [keep] + [xor_swap(send, "pp", 1)], [own_rows], [own_rows] * (tp_count - 1), "sum_cores"
    )
    got = [xor_swap(sends[k - 1], "tp", k) for k in range(1, tp_count)]
    up_v, token = load(w_up[0], experts, 1, [own], "load_up")
    stream, normed = call(
        functools.partial(norm_kernel, tp_count),
        [sds((own_rows, width), f32), sds((own_rows, width + LANES), bf16)],
        [(VMEM, a) for a in (residual_own, gain_v, info, own, *got)] + [(ANY, token)],
        name="norm",
        cost_us=0.2,
    )

    groups = min(4, sec_count)
    near = {k: xor_swap(normed, "sec", k) if k else normed for k in range(0, sec_count, 2)}
    near.update({k + 1: xor_swap(near[k], "sec", 1) for k in list(near) if k + 1 < sec_count})
    near = [near[k] for k in range(sec_count)]
    per_group = sec_count // groups
    near = [
        jnp.concatenate(near[g * per_group : (g + 1) * per_group], axis=0)
        if per_group > 1
        else near[g]
        for g in range(groups)
    ]
    rows = [[r] + [xor_swap(r, "tp", k) for k in range(1, tp_count)] for r in near]
    rows = [rows[g][k] for k in range(tp_count) for g in range(groups)]
    rows = rows + [xor_swap(r, "pp", k) for k in range(1, pp_count) for r in rows]

    halves = max(1, sec_count // E)
    count = sec_count * block
    capacity = sec_count * MOSTB
    down = w_down[0]
    tile = min(512, down.shape[0] // experts)
    kept = count // pp_count
    keep, send = call(
        functools.partial(experts_kernel, experts, capacity, tile, halves, len(rows)),
        [sds((kept, width), f32), sds((count - kept, width), bf16)],
        [(VMEM, a) for a in (*rows, *gate_v, *up_v)]
        + [(HBM, a) for a in (w_gate[0], w_up[0], down)],
        scratch=[
            pltpu.VMEM((count, width + LANES), bf16),
            pltpu.VMEM((experts * capacity, count), bf16),
            pltpu.VMEM((experts * capacity, width), bf16),
            pltpu.VMEM((experts * capacity, down.shape[0] // experts), bf16),
            pltpu.VMEM((capacity, per_expert), f32),
            pltpu.VMEM((capacity, width), f32),
            pltpu.VMEM((max(1, experts - 1), width, per_expert), bf16),
            pltpu.VMEM((max(1, experts - 1), width, per_expert), bf16),
            pltpu.VMEM((per_expert, width), bf16),
            pltpu.SemaphoreType.DMA((4 * (3 * experts - 2),)),
        ],
        vmem=33,
        name="experts",
        cost_us=12.0,
    )

    piece = kept // (tp_count * groups)
    own, sends = add(
        [keep, xor_swap(send, "pp", 1)], [piece] * groups, [piece] * (groups * (tp_count - 1)), "sum_cores2"
    )
    final = [stream]
    for g in list(range(1, groups)) + [0]:
        got = [xor_swap(sends[(k - 1) * groups + g], "tp", k) for k in range(1, tp_count)]
        if g == 0 and per_group == 1:
            final += [own[0]] + got
            continue
        kept_rows = own_rows if g == 0 else 0
        mine, out = add(
            [own[g]] + got,
            [own_rows] if g == 0 else [],
            [own_rows] * (per_group - (g == 0)),
            "sum_x%d" % g,
        )
        final += list(mine)
        for j, o in enumerate(out):
            final.append(xor_swap(o, "sec", g * per_group + j + (g == 0)))
    return call(
        functools.partial(add_kernel, 0, len(final)),
        [sds((own_rows, width), bf16)],
        [(VMEM, a) for a in final],
        name="total",
        cost_us=0.2,
    )[0]


def solution(mesh):
    in_specs = (
        P(("groups", "sec"), ("tp", "pp")),
        P(("groups", "sec"), "tp"),
        P(("groups", "sec"), "tp"),
        P(("groups", "sec"), None),
        P(("tp", "pp"), None),
        P(),
        P(("groups", "sec"), None),
        P(("groups", "sec"), None),
        P("groups"),
        P(("tp", "pp"), None, "sec"),
        P(("tp", "pp"), None, "sec"),
        P(("tp", "pp"), "sec", None),
    )
    out_specs = P(("groups", "sec", "tp", "pp"), None)
    return jax.shard_map(
        per_device, mesh=mesh, in_specs=in_specs, out_specs=out_specs, check_vma=False
    )
```

```python
import functools

import jax
import jax.numpy as jnp
from jax import lax
from jax.experimental import pallas as pl
from jax.experimental.pallas import tpu as pltpu
from jax.sharding import PartitionSpec as P

QUERY_HEAD_COUNT = 32
KEY_VALUE_HEADS = 8
HEAD_DIMENSION = 128
E = 8
MOSTB = 32
LANES = 128

neg_fill = -1e30
norm_eps = 1e-05

VMEM = pl.BlockSpec(memory_space=pltpu.VMEM)
SMEM = pl.BlockSpec(memory_space=pltpu.SMEM)
HBM = pl.BlockSpec(memory_space=pltpu.HBM)
ANY = pl.BlockSpec(memory_space=pl.ANY)
MIB = 2**20


def dot(a, b):
    return jnp.dot(a, b, preferred_element_type=jnp.float32)


def xor_swap(x, axis, k):
    n = lax.axis_size(axis)
    return lax.ppermute(x, axis, [(i, i ^ k) for i in range(n)])


def call(kernel, out_shape, args, scratch=(), vmem=8, name=None, cost_us=1.0):
    args = [
        (s, pltpu.with_memory_space_constraint(a, pltpu.HBM) if s is HBM else a) for s, a in args
    ]
    single = not isinstance(out_shape, (tuple, list))
    return pl.pallas_call(
        kernel,
        out_shape=out_shape,
        in_specs=[s for s, _ in args],
        out_specs=VMEM if single else [VMEM] * len(out_shape),
        scratch_shapes=list(scratch),
        compiler_params=pltpu.CompilerParams(vmem_limit_bytes=vmem * MIB),
        cost_estimate=pl.CostEstimate(
            flops=0, bytes_accessed=int(cost_us * 3.4e6), transcendentals=0
        ),
        name=name,
    )(*[a for _, a in args])


def sds(shape, dtype):
    return jax.ShapeDtypeStruct(shape, dtype)


def position():
    rank = lax.axis_index("tp") * lax.axis_size("pp") + lax.axis_index("pp")
    return lax.axis_index("sec"), rank


def columns(source, targets, first=0):
    per = targets[0].shape[1] if targets else 0
    return [(source.at[:, pl.ds((first + i) * per, per)], t) for i, t in enumerate(targets)]


def prepare_kernel(
    back, tp_count, pp_count, lengths_hbm, ids_hbm, codes_hbm, query_hbm, weight_hbm, residual_hbm,
    gain_hbm, *refs
):
    gate_hbm, query_ref, weight_ref, gain_ref, mask_ref, order_ref, residual_ref, info_ref = refs[
        :8
    ]
    gate_refs = refs[8:-5]
    lengths, ids, codes, residual_all, sem = refs[-5:]
    pairs = [
        (lengths_hbm, lengths),
        (ids_hbm, ids),
        (codes_hbm, codes),
        (residual_hbm, residual_all),
        (query_hbm, query_ref),
        (gain_hbm, gain_ref),
        (weight_hbm, weight_ref),
    ] + columns(gate_hbm, gate_refs)
    copies = [pltpu.make_async_copy(a, b, sem.at[i]) for i, (a, b) in enumerate(pairs)]
    for c in copies:
        c.start()
    sec, rank = position()
    block = query_ref.shape[0]
    own_rows = residual_ref.shape[0]
    at = lax.broadcasted_iota(jnp.int32, (block, block), 0)
    to = lax.broadcasted_iota(jnp.int32, (block, block), 1)
    chunk = lax.div(at, own_rows)
    flip = lax.rem(chunk, tp_count) * pp_count + lax.div(chunk, tp_count)
    source = (rank ^ flip) * own_rows + lax.rem(at, own_rows)
    order_ref[...] = jnp.where(to == source, 1.0, 0.0).astype(jnp.bfloat16)
    own = lax.broadcasted_iota(jnp.int32, (own_rows, block), 0) + rank * own_rows
    own = jnp.where(own == lax.broadcasted_iota(jnp.int32, (own_rows, block), 1), 1.0, 0.0)
    own = own.astype(jnp.bfloat16)
    for c in copies[:4]:
        c.wait()
    span = (back + 1) * block
    rows = sec * block + lax.broadcasted_iota(jnp.int32, (block, span), 0)
    cols = (sec - back) * block + lax.broadcasted_iota(jnp.int32, (block, span), 1)
    first = jnp.zeros((block, span), jnp.int32)
    end = jnp.int32(0)
    for d in range(lengths.shape[0]):
        end = end + lengths[d]
        first = jnp.where(rows >= end, end, first)
    mask_ref[...] = jnp.where((cols <= rows) & (cols >= first), 1.0, 0.0)
    residual_ref[...] = dot(own, residual_all[...])
    info = jnp.concatenate(
        [ids[...], codes[...], jnp.zeros((LANES - 4, block), jnp.int32)], axis=0
    ).astype(jnp.float32)
    info_ref[...] = lax.dot_general(
        own, info.astype(jnp.bfloat16), (((1,), (1,)), ((), ())), preferred_element_type=jnp.float32
    ).astype(jnp.bfloat16)
    for c in copies[4:]:
        c.wait()


def load_kernel(part, n_after, source, *refs):
    target, token_ref, sem = refs[n_after:]
    rows, cols = target.shape
    copy = pltpu.make_async_copy(
        source.at[pl.ds(0, rows), pl.ds(part * cols, cols)], target, sem
    )
    copy.start()
    token_ref[...] = jnp.zeros_like(token_ref)
    copy.wait()


def load(array, rows, columns, part, after, name):
    return call(
        functools.partial(load_kernel, part, len(after)),
        [sds((rows, columns), array.dtype), sds((8, LANES), jnp.float32)],
        [(HBM, array)] + [(ANY, a) for a in after],
        scratch=[pltpu.SemaphoreType.DMA],
        vmem=1,
        name=name,
        cost_us=rows * columns * 2 / 3.4e6,
    )


def join_kernel(n, *refs):
    start = 0
    for r in refs[:n]:
        refs[-1][start : start + r.shape[0], :] = r[...]
        start += r.shape[0]


def join(arrays, name, after=()):
    return call(
        functools.partial(join_kernel, len(arrays)),
        sds((sum(a.shape[0] for a in arrays), arrays[0].shape[1]), arrays[0].dtype),
        [(VMEM, a) for a in arrays] + [(ANY, a) for a in after],
        name=name,
        cost_us=0.1,
    )


def attention_kernel(back, kv_heads, group, q_ref, mask_ref, order_ref, *refs):
    kv_refs = refs[: back + 1]
    weight_ref, keep_ref, send_ref, attended_ref = refs[back + 1 :]
    block = q_ref.shape[0]
    head = HEAD_DIMENSION
    allowed = jnp.concatenate([mask_ref[...]] * group, axis=0) > 0.5
    for g in range(kv_heads):
        q = jnp.concatenate(
            [q_ref[:, (g * group + t) * head : (g * group + t + 1) * head] for t in range(group)],
            axis=0,
        )
        k = jnp.concatenate([r[:, g * head : (g + 1) * head] for r in kv_refs], axis=0)
        v = jnp.concatenate(
            [r[:, (kv_heads + g) * head : (kv_heads + g + 1) * head] for r in kv_refs], axis=0
        )
        scores = lax.dot_general(
            q, k, (((1,), (1,)), ((), ())), preferred_element_type=jnp.float32
        ) * (head**-0.5)
        scores = jnp.where(allowed, scores, neg_fill)
        top = jnp.max(scores, axis=1, keepdims=True)
        weights = jnp.where(allowed, jnp.exp(scores - top), 0.0)
        total = jnp.sum(weights, axis=1, keepdims=True)
        summed = dot(weights.astype(jnp.bfloat16), v) / total
        for t in range(group):
            attended_ref[:, (g * group + t) * head : (g * group + t + 1) * head] = summed[
                t * block : (t + 1) * block
            ].astype(jnp.bfloat16)
    attended = dot(order_ref[...], attended_ref[...]).astype(jnp.bfloat16)
    mixed = dot(attended, weight_ref[...])
    kept = keep_ref.shape[0]
    keep_ref[...] = mixed[:kept]
    send_ref[...] = mixed[kept:].astype(jnp.bfloat16)


def add_kernel(keep_rows, n_in, *refs):
    total = refs[0][...].astype(jnp.float32)
    for r in refs[1:n_in]:
        total = total + r[...].astype(jnp.float32)
    start = 0
    for r in refs[n_in:]:
        r[...] = total[start : start + r.shape[0]].astype(r.dtype)
        start += r.shape[0]


def add(arrays, keep, send, name):
    width = arrays[0].shape[1]
    out = [sds((r, width), jnp.float32) for r in keep]
    out += [sds((r, width), jnp.bfloat16) for r in send]
    out = call(
        functools.partial(add_kernel, sum(keep), len(arrays)),
        out,
        [(VMEM, a) for a in arrays],
        name=name,
        cost_us=0.2,
    )
    return out[: len(keep)], out[len(keep) :]


def norm_kernel(n_parts, residual_ref, gain_ref, info_ref, *refs):
    parts = refs[:n_parts]
    stream_ref, normed_ref = refs[-2:]
    width = residual_ref.shape[1]
    mixed = parts[0][...].astype(jnp.float32)
    for p in parts[1:]:
        mixed = mixed + p[...].astype(jnp.float32)
    stream = residual_ref[...] + mixed
    stream_ref[...] = stream
    meansq = jnp.mean(stream * stream, axis=1, keepdims=True)
    normed_ref[:, :width] = (stream * lax.rsqrt(meansq + norm_eps) * gain_ref[...]).astype(
        jnp.bfloat16
    )
    normed_ref[:, width:] = info_ref[...]


class Stream:
    def __init__(self, groups, sem, window):
        self.copies, self.last, self.window = [], {}, window
        for name, pairs in groups:
            for source, target in pairs:
                at = len(self.copies)
                self.copies.append(pltpu.make_async_copy(source, target, sem.at[at]))
            self.last[name] = len(self.copies)
        self.started = self.ended = 0
        self.limit = len(self.copies)
        self.clock = 0.0

    def fill(self):
        while self.started < self.limit and self.started - self.ended < self.window:
            self.copies[self.started].start()
            self.started += 1

    def end_one(self):
        self.copies[self.ended].wait()
        self.ended += 1
        self.fill()

    def need(self, name, but=0):
        while self.ended < self.last[name] - but:
            self.end_one()

    def step(self, cost):
        self.clock += cost
        while self.ended < self.started and self.ended + 2 <= self.clock:
            self.end_one()


def experts_kernel(experts, capacity, tile, halves, n_rows, n_late, *refs):
    rows_in = refs[:n_rows]
    gate_first, up_first, *gate_late = refs[n_rows : n_rows + 2 + n_late]
    n_rows += n_late
    gate_hbm, up_hbm, down_hbm, keep_ref, send_ref = refs[n_rows + 2 : n_rows + 7]
    rows_ref, pick_ref, packed_ref, hidden_ref, half_ref, sum_ref, gate_ref, up_ref, down_ref, sem = refs[
        n_rows + 7 :
    ]
    per_expert, width = down_hbm.shape[0] // experts, down_hbm.shape[1]
    column = min(512, width)
    cuts = 4
    early = gate_late[0].shape[0] if n_late else 0

    def pieces(source, target, x, columns, first=0, cuts=cuts):
        rows = target.shape[0] // cuts
        pairs = []
        for i in range(cuts):
            to = pl.ds(i * rows, rows)
            if columns:
                part = source.at[pl.ds(first + i * rows, rows), pl.ds(x * per_expert, per_expert)]
            else:
                part = source.at[pl.ds(x * per_expert + i * rows, rows)]
            pairs.append((part, target.at[to]))
        return pairs

    groups = []
    for x in range(experts):
        if x:
            some = (early, cuts // 2) if early else (0, cuts)
            groups.append((("gate", x), pieces(gate_hbm, gate_ref.at[x - 1], x, True, *some)))
            groups.append((("up", x), pieces(up_hbm, up_ref.at[x - 1], x, True)))
        groups.append((("down", x), pieces(down_hbm, down_ref, x, False)))
    stream = Stream(groups, sem, 4)
    stream.limit = stream.last["up", 1] if experts > 1 else stream.limit
    stream.fill()
    count = 0
    for r in rows_in:
        rows_ref[count : count + r.shape[0], :] = r[...]
        count += r.shape[0]
    at0 = lax.broadcasted_iota(jnp.int32, (count, count), 0)
    at1 = lax.broadcasted_iota(jnp.int32, (count, count), 1)
    eye = jnp.where(at0 == at1, 1.0, 0.0).astype(jnp.bfloat16)
    before = jnp.where(at0 < at1, 1.0, 0.0).astype(jnp.bfloat16)
    info = lax.dot_general(
        rows_ref[:, width:], eye, (((0,), (0,)), ((), ())), preferred_element_type=jnp.float32
    )
    id0, id1, code0, code1 = (info[i : i + 1, :] for i in range(4))
    slot_of = lax.broadcasted_iota(jnp.int32, (capacity, count), 0).astype(jnp.float32)
    first = lax.axis_index("sec") * experts if halves == 1 else lax.axis_index("sec") // halves
    picks, shares = [], []
    for x in range(experts):
        e = (first + x).astype(jnp.float32)
        hit0 = jnp.where(id0 == e, 1.0, 0.0)
        hit1 = jnp.where(id1 == e, 1.0, 0.0)
        member = hit0 + hit1
        share = (hit0 * code0 + hit1 * code1) / (code0 + code1)
        slot = dot(jnp.broadcast_to(member, (8, count)).astype(jnp.bfloat16), before)[:1]
        slot = jnp.where(member > 0.5, slot, -1.0)
        pick = slot == slot_of
        shares.append(jnp.sum(jnp.where(pick, share, 0.0), axis=1, keepdims=True))
        picks.append(jnp.where(pick, 1.0, 0.0).astype(jnp.bfloat16))
    pick_ref[...] = jnp.concatenate(picks, axis=0)
    column = min(512, width)

    for c in range(0, width, column):
        packed_ref[:, c : c + column] = dot(pick_ref[...], rows_ref[:, c : c + column]).astype(
            jnp.bfloat16
        )
    for x in range(experts):
        mine = slice(x * capacity, (x + 1) * capacity)
        if x:
            stream.need(("gate", x))
        for s in range(0, per_expert, tile):
            cut = slice(s, s + tile)
            stream.step(0.85)
            if x == 1 and n_late:
                gate = dot(packed_ref[mine, :early], gate_late[0][:, cut])
                gate = gate + dot(packed_ref[mine, early:], gate_ref[0, :, cut])
            else:
                gate = dot(packed_ref[mine, :], gate_ref[x - 1, :, cut] if x else gate_first[:, cut])
            half = 0.5 * gate
            half_ref[:, cut] = half + half * jnp.tanh(half)
        if x:
            stream.need(("up", x))
        for s in range(0, per_expert, tile):
            cut = slice(s, s + tile)
            stream.step(0.85)
            up = dot(packed_ref[mine, :], up_ref[x - 1, :, cut] if x else up_first[:, cut])
            hidden_ref[mine, cut] = (half_ref[:, cut] * up).astype(jnp.bfloat16)
        rows = per_expert // cuts
        for i in range(cuts):
            stream.need(("down", x), cuts - 1 - i)
            part = slice(i * rows, (i + 1) * rows)
            out = dot(hidden_ref[mine, part], down_ref[part, :])
            if i:
                out = out + sum_ref[...]
            if i < cuts - 1:
                sum_ref[...] = out
            else:
                packed_ref[mine, :] = (out * shares[x]).astype(jnp.bfloat16)
            stream.step(0.85)
        stream.limit = stream.last["up", x + 2] if x + 2 < experts else len(stream.copies)
        stream.fill()
    kept = keep_ref.shape[0]

    for c in range(0, width, column):
        out = lax.dot_general(
            pick_ref[...], packed_ref[:, c : c + column], (((0,), (0,)), ((), ())),
            preferred_element_type=jnp.float32,
        )
        keep_ref[:, c : c + column] = out[:kept]
        send_ref[:, c : c + column] = out[kept:].astype(jnp.bfloat16)


def per_device(
    query,
    keys,
    values,
    residual,
    out_weight,
    norm_gain,
    expert_ids,
    gate_codes,
    doc_lengths,
    w_gate,
    w_up,
    w_down,
):
    block, width = residual.shape
    head = HEAD_DIMENSION
    group_width = QUERY_HEAD_COUNT // KEY_VALUE_HEADS
    q_heads = query.shape[1] // head
    sec_count, tp_count, pp_count = (lax.axis_size(a) for a in ("sec", "tp", "pp"))
    own_rows = block // (tp_count * pp_count)
    bf16, f32 = jnp.bfloat16, jnp.float32

    kv_heads = max(1, q_heads // group_width)
    group = q_heads // kv_heads
    kv_start = lax.axis_index("pp") * q_heads // group_width * head
    kv = jnp.concatenate(
        [lax.dynamic_slice_in_dim(a, kv_start, kv_heads * head, 1) for a in (keys, values)], axis=1
    )
    back = -(-(sec_count * block // 2 - 1) // block)
    pieces = [
        lax.ppermute(kv, "sec", [(i, (i + k) % sec_count) for i in range(sec_count)])
        for k in range(back, 0, -1)
    ] + [kv]

    experts = max(1, E // sec_count)
    per_expert = w_gate.shape[2] // experts
    span = (back + 1) * block
    query_v, weight_v, gain_v, mask, order, residual_own, info, *gate_v = call(
        functools.partial(prepare_kernel, back, tp_count, pp_count),
        [
            sds(query.shape, bf16),
            sds(out_weight.shape, bf16),
            sds((1, width), f32),
            sds((block, span), f32),
            sds((block, block), bf16),
            sds((own_rows, width), f32),
            sds((own_rows, LANES), bf16),
        ]
        + [sds((width, per_expert), bf16)],
        [
            (HBM, a)
            for a in (
                doc_lengths, expert_ids.T, gate_codes.T, query, out_weight, residual,
                norm_gain.reshape(1, width), w_gate[0],
            )
        ],
        scratch=[
            pltpu.SMEM(doc_lengths.shape, jnp.int32),
            pltpu.VMEM((2, block), jnp.int32),
            pltpu.VMEM((2, block), jnp.int32),
            pltpu.VMEM(residual.shape, bf16),
            pltpu.SemaphoreType.DMA((8,)),
        ],
        vmem=6,
        name="prepare",
        cost_us=4.0,
    )
    half = block // pp_count
    keep, send = call(
        functools.partial(attention_kernel, back, kv_heads, group),
        [sds((half, width), f32), sds((block - half, width), bf16)],
        [(VMEM, a) for a in (query_v, mask, order, *pieces, weight_v)],
        scratch=[pltpu.VMEM(query.shape, bf16)],
        name="attention",
        cost_us=2.4,
    )

    (own,), sends = add(
        [keep] + [xor_swap(send, "pp", 1)], [own_rows], [own_rows] * (tp_count - 1), "sum_cores"
    )
    got = [xor_swap(sends[k - 1], "tp", k) for k in range(1, tp_count)]
    up_v, token = load(w_up[0], width, per_expert, 0, [own], "load_up")
    stream, normed = call(
        functools.partial(norm_kernel, tp_count),
        [sds((own_rows, width), f32), sds((own_rows, width + LANES), bf16)],
        [(VMEM, a) for a in (residual_own, gain_v, info, own, *got)] + [(ANY, token)],
        name="norm",
        cost_us=0.2,
    )

    groups = min(4, sec_count)
    near = {k: xor_swap(normed, "sec", k) if k else normed for k in range(0, sec_count, 2)}
    gate_late, late_rows = [], 0
    if experts == 2 and sec_count > 2:
        gate_late, token = load(w_gate[0], width // 2, per_expert, 1, [normed], "load_gate")
        gate_late, late_rows = [gate_late], width // 2
        near[2] = join([near[2]], "join", [token])
    near.update({k + 1: xor_swap(near[k], "sec", 1) for k in list(near) if k + 1 < sec_count})
    near = [near[k] for k in range(sec_count)]
    per_group = sec_count // groups
    near = [
        jnp.concatenate(near[g * per_group : (g + 1) * per_group], axis=0)
        if per_group > 1
        else near[g]
        for g in range(groups)
    ]
    rows = [[r] + [xor_swap(r, "tp", k) for k in range(1, tp_count)] for r in near]
    rows = [rows[g][k] for k in range(tp_count) for g in range(groups)]
    rows = rows + [xor_swap(r, "pp", k) for k in range(1, pp_count) for r in rows]

    halves = max(1, sec_count // E)
    count = sec_count * block
    capacity = sec_count * MOSTB
    down = w_down[0]
    tile = min(512, down.shape[0] // experts)
    kept = count // pp_count
    keep, send = call(
        functools.partial(experts_kernel, experts, capacity, tile, halves, len(rows), len(gate_late)),
        [sds((kept, width), f32), sds((count - kept, width), bf16)],
        [(VMEM, a) for a in (*rows, *gate_v, up_v, *gate_late)]
        + [(HBM, a) for a in (w_gate[0], w_up[0], down)],
        scratch=[
            pltpu.VMEM((count, width + LANES), bf16),
            pltpu.VMEM((experts * capacity, count), bf16),
            pltpu.VMEM((experts * capacity, width), bf16),
            pltpu.VMEM((experts * capacity, down.shape[0] // experts), bf16),
            pltpu.VMEM((capacity, per_expert), f32),
            pltpu.VMEM((capacity, width), f32),
            pltpu.VMEM((max(1, experts - 1), width - late_rows, per_expert), bf16),
            pltpu.VMEM((max(1, experts - 1), width, per_expert), bf16),
            pltpu.VMEM((per_expert, width), bf16),
            pltpu.SemaphoreType.DMA((4 * (3 * experts - 2),)),
        ],
        vmem=30,
        name="experts",
        cost_us=12.0,
    )

    piece = kept // (tp_count * groups)
    own, sends = add(
        [keep, xor_swap(send, "pp", 1)], [piece] * groups, [piece] * (groups * (tp_count - 1)), "sum_cores2"
    )
    final = [stream]
    for g in range(groups - 1, -1, -1):
        got = [xor_swap(sends[(k - 1) * groups + g], "tp", k) for k in range(1, tp_count)]
        if g == 0 and per_group == 1:
            final += [own[0]] + got
            continue
        kept_rows = own_rows if g == 0 else 0
        mine, out = add(
            [own[g]] + got,
            [own_rows] if g == 0 else [],
            [own_rows] * (per_group - (g == 0)),
            "sum_x%d" % g,
        )
        final += list(mine)
        for j, o in enumerate(out):
            final.append(xor_swap(o, "sec", g * per_group + j + (g == 0)))
    return call(
        functools.partial(add_kernel, 0, len(final)),
        [sds((own_rows, width), bf16)],
        [(VMEM, a) for a in final],
        name="total",
        cost_us=0.2,
    )[0]


def solution(mesh):
    in_specs = (
        P(("groups", "sec"), ("tp", "pp")),
        P(("groups", "sec"), "tp"),
        P(("groups", "sec"), "tp"),
        P(("groups", "sec"), None),
        P(("tp", "pp"), None),
        P(),
        P(("groups", "sec"), None),
        P(("groups", "sec"), None),
        P("groups"),
        P(("tp", "pp"), None, "sec"),
        P(("tp", "pp"), None, "sec"),
        P(("tp", "pp"), "sec", None),
    )
    out_specs = P(("groups", "sec", "tp", "pp"), None)
    return jax.shard_map(
        per_device, mesh=mesh, in_specs=in_specs, out_specs=out_specs, check_vma=False
    )
```

```python
import functools

import jax
import jax.numpy as jnp
from jax import lax
from jax.experimental import pallas as pl
from jax.experimental.pallas import tpu as pltpu
from jax.sharding import PartitionSpec as P

QUERY_HEAD_COUNT = 32
KEY_VALUE_HEADS = 8
HEAD_DIMENSION = 128
E = 8
MOSTB = 32
LANES = 128

neg_fill = -1e30
norm_eps = 1e-05

VMEM = pl.BlockSpec(memory_space=pltpu.VMEM)
SMEM = pl.BlockSpec(memory_space=pltpu.SMEM)
HBM = pl.BlockSpec(memory_space=pltpu.HBM)
ANY = pl.BlockSpec(memory_space=pl.ANY)
MIB = 2**20


def dot(a, b):
    return jnp.dot(a, b, preferred_element_type=jnp.float32)


def xor_swap(x, axis, k):
    n = lax.axis_size(axis)
    return lax.ppermute(x, axis, [(i, i ^ k) for i in range(n)])


def call(kernel, out_shape, args, scratch=(), vmem=8, name=None, cost_us=1.0):
    args = [
        (s, pltpu.with_memory_space_constraint(a, pltpu.HBM) if s is HBM else a) for s, a in args
    ]
    single = not isinstance(out_shape, (tuple, list))
    return pl.pallas_call(
        kernel,
        out_shape=out_shape,
        in_specs=[s for s, _ in args],
        out_specs=VMEM if single else [VMEM] * len(out_shape),
        scratch_shapes=list(scratch),
        compiler_params=pltpu.CompilerParams(vmem_limit_bytes=vmem * MIB),
        cost_estimate=pl.CostEstimate(
            flops=0, bytes_accessed=int(cost_us * 3.4e6), transcendentals=0
        ),
        name=name,
    )(*[a for _, a in args])


def sds(shape, dtype):
    return jax.ShapeDtypeStruct(shape, dtype)


def position():
    rank = lax.axis_index("tp") * lax.axis_size("pp") + lax.axis_index("pp")
    return lax.axis_index("sec"), rank


def columns(source, targets, first=0):
    per = targets[0].shape[1] if targets else 0
    return [
        (source.at[pl.ds(0, t.shape[0]), pl.ds((first + i) * per, per)], t)
        for i, t in enumerate(targets)
    ]


def prepare_kernel(
    back, tp_count, pp_count, lengths_hbm, ids_hbm, codes_hbm, query_hbm, weight_hbm, residual_hbm,
    gain_hbm, *refs
):
    gate_hbm, query_ref, weight_ref, gain_ref, mask_ref, order_ref, residual_ref, info_ref = refs[
        :8
    ]
    gate_refs = refs[8:-5]
    lengths, ids, codes, residual_all, sem = refs[-5:]
    pairs = [
        (lengths_hbm, lengths),
        (ids_hbm, ids),
        (codes_hbm, codes),
        (residual_hbm, residual_all),
        (query_hbm, query_ref),
        (gain_hbm, gain_ref),
        (weight_hbm, weight_ref),
    ] + columns(gate_hbm, gate_refs)
    copies = [pltpu.make_async_copy(a, b, sem.at[i]) for i, (a, b) in enumerate(pairs)]
    for c in copies:
        c.start()
    sec, rank = position()
    block = query_ref.shape[0]
    own_rows = residual_ref.shape[0]
    at = lax.broadcasted_iota(jnp.int32, (block, block), 0)
    to = lax.broadcasted_iota(jnp.int32, (block, block), 1)
    chunk = lax.div(at, own_rows)
    flip = lax.rem(chunk, tp_count) * pp_count + lax.div(chunk, tp_count)
    source = (rank ^ flip) * own_rows + lax.rem(at, own_rows)
    order_ref[...] = jnp.where(to == source, 1.0, 0.0).astype(jnp.bfloat16)
    own = lax.broadcasted_iota(jnp.int32, (own_rows, block), 0) + rank * own_rows
    own = jnp.where(own == lax.broadcasted_iota(jnp.int32, (own_rows, block), 1), 1.0, 0.0)
    own = own.astype(jnp.bfloat16)
    for c in copies[:4]:
        c.wait()
    span = (back + 1) * block
    rows = sec * block + lax.broadcasted_iota(jnp.int32, (block, span), 0)
    cols = (sec - back) * block + lax.broadcasted_iota(jnp.int32, (block, span), 1)
    first = jnp.zeros((block, span), jnp.int32)
    end = jnp.int32(0)
    for d in range(lengths.shape[0]):
        end = end + lengths[d]
        first = jnp.where(rows >= end, end, first)
    mask_ref[...] = jnp.where((cols <= rows) & (cols >= first), 1.0, 0.0)
    residual_ref[...] = dot(own, residual_all[...])
    info = jnp.concatenate(
        [ids[...], codes[...], jnp.zeros((LANES - 4, block), jnp.int32)], axis=0
    ).astype(jnp.float32)
    info_ref[...] = lax.dot_general(
        own, info.astype(jnp.bfloat16), (((1,), (1,)), ((), ())), preferred_element_type=jnp.float32
    ).astype(jnp.bfloat16)
    for c in copies[4:]:
        c.wait()


def load_kernel(first, n_after, source, *refs):
    target, token_ref, sem = refs[n_after:]
    rows, cols = target.shape
    copy = pltpu.make_async_copy(
        source.at[pl.ds(first, rows), pl.ds(0, cols)], target, sem
    )
    copy.start()
    token_ref[...] = jnp.zeros_like(token_ref)
    copy.wait()


def load(array, first, rows, columns, after, name):
    return call(
        functools.partial(load_kernel, first, len(after)),
        [sds((rows, columns), array.dtype), sds((8, LANES), jnp.float32)],
        [(HBM, array)] + [(ANY, a) for a in after],
        scratch=[pltpu.SemaphoreType.DMA],
        vmem=1,
        name=name,
        cost_us=rows * columns * 2 / 3.4e6,
    )


def join_kernel(n, *refs):
    start = 0
    for r in refs[:n]:
        refs[-1][start : start + r.shape[0], :] = r[...]
        start += r.shape[0]


def join(arrays, name, after=()):
    return call(
        functools.partial(join_kernel, len(arrays)),
        sds((sum(a.shape[0] for a in arrays), arrays[0].shape[1]), arrays[0].dtype),
        [(VMEM, a) for a in arrays] + [(ANY, a) for a in after],
        name=name,
        cost_us=0.1,
    )


def attention_kernel(back, kv_heads, group, q_ref, mask_ref, order_ref, *refs):
    kv_refs = refs[: back + 1]
    weight_ref, keep_ref, send_ref, attended_ref = refs[back + 1 :]
    block = q_ref.shape[0]
    head = HEAD_DIMENSION
    allowed = jnp.concatenate([mask_ref[...]] * group, axis=0) > 0.5
    for g in range(kv_heads):
        q = jnp.concatenate(
            [q_ref[:, (g * group + t) * head : (g * group + t + 1) * head] for t in range(group)],
            axis=0,
        )
        k = jnp.concatenate([r[:, g * head : (g + 1) * head] for r in kv_refs], axis=0)
        v = jnp.concatenate(
            [r[:, (kv_heads + g) * head : (kv_heads + g + 1) * head] for r in kv_refs], axis=0
        )
        scores = lax.dot_general(
            q, k, (((1,), (1,)), ((), ())), preferred_element_type=jnp.float32
        ) * (head**-0.5)
        scores = jnp.where(allowed, scores, neg_fill)
        top = jnp.max(scores, axis=1, keepdims=True)
        weights = jnp.where(allowed, jnp.exp(scores - top), 0.0)
        total = jnp.sum(weights, axis=1, keepdims=True)
        summed = dot(weights.astype(jnp.bfloat16), v) / total
        for t in range(group):
            attended_ref[:, (g * group + t) * head : (g * group + t + 1) * head] = summed[
                t * block : (t + 1) * block
            ].astype(jnp.bfloat16)
    attended = dot(order_ref[...], attended_ref[...]).astype(jnp.bfloat16)
    mixed = dot(attended, weight_ref[...])
    kept = keep_ref.shape[0]
    keep_ref[...] = mixed[:kept]
    send_ref[...] = mixed[kept:].astype(jnp.bfloat16)


def add_kernel(keep_rows, n_in, *refs):
    total = refs[0][...].astype(jnp.float32)
    for r in refs[1:n_in]:
        total = total + r[...].astype(jnp.float32)
    start = 0
    for r in refs[n_in:]:
        r[...] = total[start : start + r.shape[0]].astype(r.dtype)
        start += r.shape[0]


def add(arrays, keep, send, name):
    width = arrays[0].shape[1]
    out = [sds((r, width), jnp.float32) for r in keep]
    out += [sds((r, width), jnp.bfloat16) for r in send]
    out = call(
        functools.partial(add_kernel, sum(keep), len(arrays)),
        out,
        [(VMEM, a) for a in arrays],
        name=name,
        cost_us=0.2,
    )
    return out[: len(keep)], out[len(keep) :]


def norm_kernel(n_parts, residual_ref, gain_ref, info_ref, *refs):
    parts = refs[:n_parts]
    stream_ref, normed_ref = refs[-2:]
    width = residual_ref.shape[1]
    mixed = parts[0][...].astype(jnp.float32)
    for p in parts[1:]:
        mixed = mixed + p[...].astype(jnp.float32)
    stream = residual_ref[...] + mixed
    stream_ref[...] = stream
    meansq = jnp.mean(stream * stream, axis=1, keepdims=True)
    normed_ref[:, :width] = (stream * lax.rsqrt(meansq + norm_eps) * gain_ref[...]).astype(
        jnp.bfloat16
    )
    normed_ref[:, width:] = info_ref[...]


class Stream:
    def __init__(self, groups, sem, window):
        self.copies, self.last, self.window = [], {}, window
        for name, pairs in groups:
            for source, target in pairs:
                at = len(self.copies)
                self.copies.append(pltpu.make_async_copy(source, target, sem.at[at]))
            self.last[name] = len(self.copies)
        self.started = self.ended = 0
        self.limit = len(self.copies)
        self.clock = 0.0

    def fill(self):
        while self.started < self.limit and self.started - self.ended < self.window:
            self.copies[self.started].start()
            self.started += 1

    def end_one(self):
        self.copies[self.ended].wait()
        self.ended += 1
        self.fill()

    def need(self, name, but=0):
        while self.ended < self.last[name] - but:
            self.end_one()

    def step(self, cost):
        self.clock += cost
        while self.ended < self.started and self.ended + 2 <= self.clock:
            self.end_one()


def experts_kernel(experts, capacity, tile, halves, n_rows, *refs):
    rows_in = refs[:n_rows]
    gate_top, gate_low, up_first, gate_hbm, up_hbm, down_hbm, keep_ref, send_ref = refs[
        n_rows : n_rows + 8
    ]
    rows_ref, pick_ref, packed_ref, hidden_ref, half_ref, sum_ref, gate_ref, up_ref, down_ref, sem = refs[
        n_rows + 8 :
    ]
    per_expert, width = down_hbm.shape[0] // experts, down_hbm.shape[1]
    column = min(512, width)
    cuts = 4
    top = gate_top.shape[0]

    def pieces(source, target, x, columns):
        rows = target.shape[0] // cuts
        pairs = []
        for i in range(cuts):
            to = pl.ds(i * rows, rows)
            if columns:
                part = source.at[to, pl.ds(x * per_expert, per_expert)]
            else:
                part = source.at[pl.ds(x * per_expert + i * rows, rows)]
            pairs.append((part, target.at[to]))
        return pairs

    groups = []
    for x in range(experts):
        if x:
            groups.append((("gate", x), pieces(gate_hbm, gate_ref.at[x - 1], x, True)))
            groups.append((("up", x), pieces(up_hbm, up_ref.at[x - 1], x, True)))
        groups.append((("down", x), pieces(down_hbm, down_ref, x, False)))
    stream = Stream(groups, sem, 4)
    stream.limit = stream.last["up", 1] if experts > 1 else stream.limit
    stream.fill()
    count = 0
    for r in rows_in:
        rows_ref[count : count + r.shape[0], :] = r[...]
        count += r.shape[0]
    at0 = lax.broadcasted_iota(jnp.int32, (count, count), 0)
    at1 = lax.broadcasted_iota(jnp.int32, (count, count), 1)
    eye = jnp.where(at0 == at1, 1.0, 0.0).astype(jnp.bfloat16)
    before = jnp.where(at0 < at1, 1.0, 0.0).astype(jnp.bfloat16)
    info = lax.dot_general(
        rows_ref[:, width:], eye, (((0,), (0,)), ((), ())), preferred_element_type=jnp.float32
    )
    id0, id1, code0, code1 = (info[i : i + 1, :] for i in range(4))
    slot_of = lax.broadcasted_iota(jnp.int32, (capacity, count), 0).astype(jnp.float32)
    first = lax.axis_index("sec") * experts if halves == 1 else lax.axis_index("sec") // halves
    picks, shares = [], []
    for x in range(experts):
        e = (first + x).astype(jnp.float32)
        hit0 = jnp.where(id0 == e, 1.0, 0.0)
        hit1 = jnp.where(id1 == e, 1.0, 0.0)
        member = hit0 + hit1
        share = (hit0 * code0 + hit1 * code1) / (code0 + code1)
        slot = dot(jnp.broadcast_to(member, (8, count)).astype(jnp.bfloat16), before)[:1]
        slot = jnp.where(member > 0.5, slot, -1.0)
        pick = slot == slot_of
        shares.append(jnp.sum(jnp.where(pick, share, 0.0), axis=1, keepdims=True))
        picks.append(jnp.where(pick, 1.0, 0.0).astype(jnp.bfloat16))
    pick_ref[...] = jnp.concatenate(picks, axis=0)
    column = min(512, width)

    for c in range(0, width, column):
        packed_ref[:, c : c + column] = dot(pick_ref[...], rows_ref[:, c : c + column]).astype(
            jnp.bfloat16
        )
    for x in range(experts):
        mine = slice(x * capacity, (x + 1) * capacity)
        if x:
            stream.need(("gate", x))
        for s in range(0, per_expert, tile):
            cut = slice(s, s + tile)
            stream.step(0.85)
            if x:
                gate = dot(packed_ref[mine, :], gate_ref[x - 1, :, cut])
            else:
                gate = dot(packed_ref[mine, :top], gate_top[:, cut])
                gate = gate + dot(packed_ref[mine, top:], gate_low[:, cut])
            half = 0.5 * gate
            half_ref[:, cut] = half + half * jnp.tanh(half)
        if x:
            stream.need(("up", x))
        for s in range(0, per_expert, tile):
            cut = slice(s, s + tile)
            stream.step(0.85)
            up = dot(packed_ref[mine, :], up_ref[x - 1, :, cut] if x else up_first[:, cut])
            hidden_ref[mine, cut] = (half_ref[:, cut] * up).astype(jnp.bfloat16)
        rows = per_expert // cuts
        for i in range(cuts):
            stream.need(("down", x), cuts - 1 - i)
            part = slice(i * rows, (i + 1) * rows)
            out = dot(hidden_ref[mine, part], down_ref[part, :])
            if i:
                out = out + sum_ref[...]
            if i < cuts - 1:
                sum_ref[...] = out
            else:
                packed_ref[mine, :] = (out * shares[x]).astype(jnp.bfloat16)
            stream.step(0.85)
        stream.limit = stream.last["up", x + 2] if x + 2 < experts else len(stream.copies)
        stream.fill()
    kept = keep_ref.shape[0]

    for c in range(0, width, column):
        out = lax.dot_general(
            pick_ref[...], packed_ref[:, c : c + column], (((0,), (0,)), ((), ())),
            preferred_element_type=jnp.float32,
        )
        keep_ref[:, c : c + column] = out[:kept]
        send_ref[:, c : c + column] = out[kept:].astype(jnp.bfloat16)


def per_device(
    query,
    keys,
    values,
    residual,
    out_weight,
    norm_gain,
    expert_ids,
    gate_codes,
    doc_lengths,
    w_gate,
    w_up,
    w_down,
):
    block, width = residual.shape
    head = HEAD_DIMENSION
    group_width = QUERY_HEAD_COUNT // KEY_VALUE_HEADS
    q_heads = query.shape[1] // head
    sec_count, tp_count, pp_count = (lax.axis_size(a) for a in ("sec", "tp", "pp"))
    own_rows = block // (tp_count * pp_count)
    bf16, f32 = jnp.bfloat16, jnp.float32

    kv_heads = max(1, q_heads // group_width)
    group = q_heads // kv_heads
    kv_start = lax.axis_index("pp") * q_heads // group_width * head
    kv = jnp.concatenate(
        [lax.dynamic_slice_in_dim(a, kv_start, kv_heads * head, 1) for a in (keys, values)], axis=1
    )
    back = -(-(sec_count * block // 2 - 1) // block)
    pieces = [
        lax.ppermute(kv, "sec", [(i, (i + k) % sec_count) for i in range(sec_count)])
        for k in range(back, 0, -1)
    ] + [kv]

    experts = max(1, E // sec_count)
    per_expert = w_gate.shape[2] // experts
    span = (back + 1) * block
    query_v, weight_v, gain_v, mask, order, residual_own, info, *gate_v = call(
        functools.partial(prepare_kernel, back, tp_count, pp_count),
        [
            sds(query.shape, bf16),
            sds(out_weight.shape, bf16),
            sds((1, width), f32),
            sds((block, span), f32),
            sds((block, block), bf16),
            sds((own_rows, width), f32),
            sds((own_rows, LANES), bf16),
        ]
        + [sds((width // 2, per_expert), bf16)],
        [
            (HBM, a)
            for a in (
                doc_lengths, expert_ids.T, gate_codes.T, query, out_weight, residual,
                norm_gain.reshape(1, width), w_gate[0],
            )
        ],
        scratch=[
            pltpu.SMEM(doc_lengths.shape, jnp.int32),
            pltpu.VMEM((2, block), jnp.int32),
            pltpu.VMEM((2, block), jnp.int32),
            pltpu.VMEM(residual.shape, bf16),
            pltpu.SemaphoreType.DMA((8,)),
        ],
        vmem=6,
        name="prepare",
        cost_us=3.0,
    )
    half = block // pp_count
    keep, send = call(
        functools.partial(attention_kernel, back, kv_heads, group),
        [sds((half, width), f32), sds((block - half, width), bf16)],
        [(VMEM, a) for a in (query_v, mask, order, *pieces, weight_v)],
        scratch=[pltpu.VMEM(query.shape, bf16)],
        name="attention",
        cost_us=2.4,
    )

    (own,), sends = add(
        [keep] + [xor_swap(send, "pp", 1)], [own_rows], [own_rows] * (tp_count - 1), "sum_cores"
    )
    got = [xor_swap(sends[k - 1], "tp", k) for k in range(1, tp_count)]
    up_v, token = load(w_up[0], 0, width, per_expert, [own], "load_up")
    stream, normed = call(
        functools.partial(norm_kernel, tp_count),
        [sds((own_rows, width), f32), sds((own_rows, width + LANES), bf16)],
        [(VMEM, a) for a in (residual_own, gain_v, info, own, *got)] + [(ANY, token)],
        name="norm",
        cost_us=0.2,
    )

    groups = min(4, sec_count)
    near = {k: xor_swap(normed, "sec", k) if k else normed for k in range(0, sec_count, 2)}
    gate_late, token = load(w_gate[0], width // 2, width // 2, per_expert, [normed], "load_gate")
    if sec_count > 2:
        near[2] = join([near[2]], "join", [token])
    near.update({k + 1: xor_swap(near[k], "sec", 1) for k in list(near) if k + 1 < sec_count})
    near = [near[k] for k in range(sec_count)]
    per_group = sec_count // groups
    near = [
        jnp.concatenate(near[g * per_group : (g + 1) * per_group], axis=0)
        if per_group > 1
        else near[g]
        for g in range(groups)
    ]
    rows = [[r] + [xor_swap(r, "tp", k) for k in range(1, tp_count)] for r in near]
    rows = [rows[g][k] for k in range(tp_count) for g in range(groups)]
    rows = rows + [xor_swap(r, "pp", k) for k in range(1, pp_count) for r in rows]

    halves = max(1, sec_count // E)
    count = sec_count * block
    capacity = sec_count * MOSTB
    down = w_down[0]
    tile = min(512, down.shape[0] // experts)
    kept = count // pp_count
    keep, send = call(
        functools.partial(experts_kernel, experts, capacity, tile, halves, len(rows)),
        [sds((kept, width), f32), sds((count - kept, width), bf16)],
        [(VMEM, a) for a in (*rows, *gate_v, gate_late, up_v)]
        + [(HBM, a) for a in (w_gate[0], w_up[0], down)],
        scratch=[
            pltpu.VMEM((count, width + LANES), bf16),
            pltpu.VMEM((experts * capacity, count), bf16),
            pltpu.VMEM((experts * capacity, width), bf16),
            pltpu.VMEM((experts * capacity, down.shape[0] // experts), bf16),
            pltpu.VMEM((capacity, per_expert), f32),
            pltpu.VMEM((capacity, width), f32),
            pltpu.VMEM((max(1, experts - 1), width, per_expert), bf16),
            pltpu.VMEM((max(1, experts - 1), width, per_expert), bf16),
            pltpu.VMEM((per_expert, width), bf16),
            pltpu.SemaphoreType.DMA((4 * (3 * experts - 2),)),
        ],
        vmem=33,
        name="experts",
        cost_us=12.0,
    )

    piece = kept // (tp_count * groups)
    own, sends = add(
        [keep, xor_swap(send, "pp", 1)], [piece] * groups, [piece] * (groups * (tp_count - 1)), "sum_cores2"
    )
    final = [stream]
    for g in range(groups - 1, -1, -1):
        got = [xor_swap(sends[(k - 1) * groups + g], "tp", k) for k in range(1, tp_count)]
        if g == 0 and per_group == 1:
            final += [own[0]] + got
            continue
        kept_rows = own_rows if g == 0 else 0
        mine, out = add(
            [own[g]] + got,
            [own_rows] if g == 0 else [],
            [own_rows] * (per_group - (g == 0)),
            "sum_x%d" % g,
        )
        final += list(mine)
        for j, o in enumerate(out):
            final.append(xor_swap(o, "sec", g * per_group + j + (g == 0)))
    return call(
        functools.partial(add_kernel, 0, len(final)),
        [sds((own_rows, width), bf16)],
        [(VMEM, a) for a in final],
        name="total",
        cost_us=0.2,
    )[0]


def solution(mesh):
    in_specs = (
        P(("groups", "sec"), ("tp", "pp")),
        P(("groups", "sec"), "tp"),
        P(("groups", "sec"), "tp"),
        P(("groups", "sec"), None),
        P(("tp", "pp"), None),
        P(),
        P(("groups", "sec"), None),
        P(("groups", "sec"), None),
        P("groups"),
        P(("tp", "pp"), None, "sec"),
        P(("tp", "pp"), None, "sec"),
        P(("tp", "pp"), "sec", None),
    )
    out_specs = P(("groups", "sec", "tp", "pp"), None)
    return jax.shard_map(
        per_device, mesh=mesh, in_specs=in_specs, out_specs=out_specs, check_vma=False
    )
```

```python
import functools

import jax
import jax.numpy as jnp
from jax import lax
from jax.experimental import pallas as pl
from jax.experimental.pallas import tpu as pltpu
from jax.sharding import PartitionSpec as P

QUERY_HEAD_COUNT = 32
KEY_VALUE_HEADS = 8
HEAD_DIMENSION = 128
E = 8
MOSTB = 32
LANES = 128

neg_fill = -1e30
norm_eps = 1e-05

VMEM = pl.BlockSpec(memory_space=pltpu.VMEM)
SMEM = pl.BlockSpec(memory_space=pltpu.SMEM)
HBM = pl.BlockSpec(memory_space=pltpu.HBM)
ANY = pl.BlockSpec(memory_space=pl.ANY)
MIB = 2**20


def dot(a, b):
    return jnp.dot(a, b, preferred_element_type=jnp.float32)


def xor_swap(x, axis, k):
    n = lax.axis_size(axis)
    return lax.ppermute(x, axis, [(i, i ^ k) for i in range(n)])


def call(kernel, out_shape, args, scratch=(), vmem=8, name=None, cost_us=1.0):
    args = [
        (s, pltpu.with_memory_space_constraint(a, pltpu.HBM) if s is HBM else a) for s, a in args
    ]
    single = not isinstance(out_shape, (tuple, list))
    return pl.pallas_call(
        kernel,
        out_shape=out_shape,
        in_specs=[s for s, _ in args],
        out_specs=VMEM if single else [VMEM] * len(out_shape),
        scratch_shapes=list(scratch),
        compiler_params=pltpu.CompilerParams(vmem_limit_bytes=vmem * MIB),
        cost_estimate=pl.CostEstimate(
            flops=0, bytes_accessed=int(cost_us * 3.4e6), transcendentals=0
        ),
        name=name,
    )(*[a for _, a in args])


def sds(shape, dtype):
    return jax.ShapeDtypeStruct(shape, dtype)


def position():
    rank = lax.axis_index("tp") * lax.axis_size("pp") + lax.axis_index("pp")
    return lax.axis_index("sec"), rank


def columns(source, targets, first=0):
    per = targets[0].shape[1] if targets else 0
    return [
        (source.at[pl.ds(0, t.shape[0]), pl.ds((first + i) * per, per)], t)
        for i, t in enumerate(targets)
    ]


def prepare_kernel(
    back, tp_count, pp_count, lengths_hbm, ids_hbm, codes_hbm, query_hbm, weight_hbm, residual_hbm,
    gain_hbm, *refs
):
    gate_hbm, query_ref, weight_ref, gain_ref, mask_ref, order_ref, residual_ref, info_ref = refs[
        :8
    ]
    gate_refs = refs[8:-5]
    lengths, ids, codes, residual_all, sem = refs[-5:]
    pairs = [
        (lengths_hbm, lengths),
        (ids_hbm, ids),
        (codes_hbm, codes),
        (residual_hbm, residual_all),
        (query_hbm, query_ref),
        (gain_hbm, gain_ref),
        (weight_hbm, weight_ref),
    ] + columns(gate_hbm, gate_refs)
    copies = [pltpu.make_async_copy(a, b, sem.at[i]) for i, (a, b) in enumerate(pairs)]
    for c in copies:
        c.start()
    sec, rank = position()
    block = query_ref.shape[0]
    own_rows = residual_ref.shape[0]
    at = lax.broadcasted_iota(jnp.int32, (block, block), 0)
    to = lax.broadcasted_iota(jnp.int32, (block, block), 1)
    chunk = lax.div(at, own_rows)
    flip = lax.rem(chunk, tp_count) * pp_count + lax.div(chunk, tp_count)
    source = (rank ^ flip) * own_rows + lax.rem(at, own_rows)
    order_ref[...] = jnp.where(to == source, 1.0, 0.0).astype(jnp.bfloat16)
    own = lax.broadcasted_iota(jnp.int32, (own_rows, block), 0) + rank * own_rows
    own = jnp.where(own == lax.broadcasted_iota(jnp.int32, (own_rows, block), 1), 1.0, 0.0)
    own = own.astype(jnp.bfloat16)
    for c in copies[:4]:
        c.wait()
    span = (back + 1) * block
    rows = sec * block + lax.broadcasted_iota(jnp.int32, (block, span), 0)
    cols = (sec - back) * block + lax.broadcasted_iota(jnp.int32, (block, span), 1)
    first = jnp.zeros((block, span), jnp.int32)
    end = jnp.int32(0)
    for d in range(lengths.shape[0]):
        end = end + lengths[d]
        first = jnp.where(rows >= end, end, first)
    mask_ref[...] = jnp.where((cols <= rows) & (cols >= first), 1.0, 0.0)
    residual_ref[...] = dot(own, residual_all[...])
    info = jnp.concatenate(
        [ids[...], codes[...], jnp.zeros((LANES - 4, block), jnp.int32)], axis=0
    ).astype(jnp.float32)
    info_ref[...] = lax.dot_general(
        own, info.astype(jnp.bfloat16), (((1,), (1,)), ((), ())), preferred_element_type=jnp.float32
    ).astype(jnp.bfloat16)
    for c in copies[4:]:
        c.wait()


def load_kernel(first, n_after, source, *refs):
    target, token_ref, sem = refs[n_after:]
    rows, cols = target.shape
    copy = pltpu.make_async_copy(
        source.at[pl.ds(first, rows), pl.ds(0, cols)], target, sem
    )
    copy.start()
    token_ref[...] = jnp.zeros_like(token_ref)
    copy.wait()


def load(array, first, rows, columns, after, name):
    return call(
        functools.partial(load_kernel, first, len(after)),
        [sds((rows, columns), array.dtype), sds((8, LANES), jnp.float32)],
        [(HBM, array)] + [(ANY, a) for a in after],
        scratch=[pltpu.SemaphoreType.DMA],
        vmem=1,
        name=name,
        cost_us=rows * columns * 2 / 3.4e6,
    )


def join_kernel(n, *refs):
    start = 0
    for r in refs[:n]:
        refs[-1][start : start + r.shape[0], :] = r[...]
        start += r.shape[0]


def join(arrays, name, after=()):
    return call(
        functools.partial(join_kernel, len(arrays)),
        sds((sum(a.shape[0] for a in arrays), arrays[0].shape[1]), arrays[0].dtype),
        [(VMEM, a) for a in arrays] + [(ANY, a) for a in after],
        name=name,
        cost_us=0.1,
    )


def attention_kernel(back, kv_heads, group, q_ref, mask_ref, order_ref, *refs):
    kv_refs = refs[: back + 1]
    weight_ref, keep_ref, send_ref, attended_ref = refs[back + 1 :]
    block = q_ref.shape[0]
    head = HEAD_DIMENSION
    allowed = jnp.concatenate([mask_ref[...]] * group, axis=0) > 0.5
    for g in range(kv_heads):
        q = jnp.concatenate(
            [q_ref[:, (g * group + t) * head : (g * group + t + 1) * head] for t in range(group)],
            axis=0,
        )
        k = jnp.concatenate([r[:, g * head : (g + 1) * head] for r in kv_refs], axis=0)
        v = jnp.concatenate(
            [r[:, (kv_heads + g) * head : (kv_heads + g + 1) * head] for r in kv_refs], axis=0
        )
        scores = lax.dot_general(
            q, k, (((1,), (1,)), ((), ())), preferred_element_type=jnp.float32
        ) * (head**-0.5)
        scores = jnp.where(allowed, scores, neg_fill)
        top = jnp.max(scores, axis=1, keepdims=True)
        weights = jnp.where(allowed, jnp.exp(scores - top), 0.0)
        total = jnp.sum(weights, axis=1, keepdims=True)
        summed = dot(weights.astype(jnp.bfloat16), v) / total
        for t in range(group):
            attended_ref[:, (g * group + t) * head : (g * group + t + 1) * head] = summed[
                t * block : (t + 1) * block
            ].astype(jnp.bfloat16)
    attended = dot(order_ref[...], attended_ref[...]).astype(jnp.bfloat16)
    mixed = dot(attended, weight_ref[...])
    kept = keep_ref.shape[0]
    keep_ref[...] = mixed[:kept]
    send_ref[...] = mixed[kept:].astype(jnp.bfloat16)


def add_kernel(keep_rows, n_in, *refs):
    total = refs[0][...].astype(jnp.float32)
    for r in refs[1:n_in]:
        total = total + r[...].astype(jnp.float32)
    start = 0
    for r in refs[n_in:]:
        r[...] = total[start : start + r.shape[0]].astype(r.dtype)
        start += r.shape[0]


def add(arrays, keep, send, name):
    width = arrays[0].shape[1]
    out = [sds((r, width), jnp.float32) for r in keep]
    out += [sds((r, width), jnp.bfloat16) for r in send]
    out = call(
        functools.partial(add_kernel, sum(keep), len(arrays)),
        out,
        [(VMEM, a) for a in arrays],
        name=name,
        cost_us=0.2,
    )
    return out[: len(keep)], out[len(keep) :]


def norm_kernel(n_parts, residual_ref, gain_ref, info_ref, *refs):
    parts = refs[:n_parts]
    stream_ref, normed_ref = refs[-2:]
    width = residual_ref.shape[1]
    mixed = parts[0][...].astype(jnp.float32)
    for p in parts[1:]:
        mixed = mixed + p[...].astype(jnp.float32)
    stream = residual_ref[...] + mixed
    stream_ref[...] = stream
    meansq = jnp.mean(stream * stream, axis=1, keepdims=True)
    normed_ref[:, :width] = (stream * lax.rsqrt(meansq + norm_eps) * gain_ref[...]).astype(
        jnp.bfloat16
    )
    normed_ref[:, width:] = info_ref[...]


class Stream:
    def __init__(self, groups, sem, window):
        self.copies, self.last, self.window = [], {}, window
        for name, pairs in groups:
            for source, target in pairs:
                at = len(self.copies)
                self.copies.append(pltpu.make_async_copy(source, target, sem.at[at]))
            self.last[name] = len(self.copies)
        self.started = self.ended = 0
        self.limit = len(self.copies)
        self.clock = 0.0

    def fill(self):
        while self.started < self.limit and self.started - self.ended < self.window:
            self.copies[self.started].start()
            self.started += 1

    def end_one(self):
        self.copies[self.ended].wait()
        self.ended += 1
        self.fill()

    def need(self, name, but=0):
        while self.ended < self.last[name] - but:
            self.end_one()

    def step(self, cost):
        self.clock += cost
        while self.ended < self.started and self.ended + 2 <= self.clock:
            self.end_one()


def experts_kernel(experts, capacity, tile, halves, n_rows, *refs):
    rows_in = refs[:n_rows]
    gate_top, gate_low, up_first, gate_hbm, up_hbm, down_hbm = refs[n_rows : n_rows + 6]
    send_ref, pick_ref, packed_ref = refs[n_rows + 6 : n_rows + 9]
    rows_ref, hidden_ref, half_ref, sum_ref, up_low, gate_ref, up_ref, down_ref, sem = refs[
        n_rows + 9 :
    ]
    per_expert, width = down_hbm.shape[0] // experts, down_hbm.shape[1]
    column = min(512, width)
    cuts = 4
    top, high = gate_top.shape[0], up_first.shape[0]

    def pieces(source, target, x, columns):
        rows = target.shape[0] // cuts
        pairs = []
        for i in range(cuts):
            to = pl.ds(i * rows, rows)
            if columns:
                part = source.at[to, pl.ds(x * per_expert, per_expert)]
            else:
                part = source.at[pl.ds(x * per_expert + i * rows, rows)]
            pairs.append((part, target.at[to]))
        return pairs

    groups = []
    if high < width:
        low = up_hbm.at[pl.ds(high, width - high), pl.ds(0, per_expert)]
        groups.append((("up", 0), [(low, up_low)]))
    for x in range(experts):
        if x:
            groups.append((("gate", x), pieces(gate_hbm, gate_ref.at[x - 1], x, True)))
            groups.append((("up", x), pieces(up_hbm, up_ref.at[x - 1], x, True)))
        groups.append((("down", x), pieces(down_hbm, down_ref, x, False)))
    stream = Stream(groups, sem, 4)
    stream.limit = stream.last["up", 1] if experts > 1 else stream.limit
    stream.fill()
    count = 0
    for r in rows_in:
        rows_ref[count : count + r.shape[0], :] = r[...]
        count += r.shape[0]
    at0 = lax.broadcasted_iota(jnp.int32, (count, count), 0)
    at1 = lax.broadcasted_iota(jnp.int32, (count, count), 1)
    eye = jnp.where(at0 == at1, 1.0, 0.0).astype(jnp.bfloat16)
    before = jnp.where(at0 < at1, 1.0, 0.0).astype(jnp.bfloat16)
    info = lax.dot_general(
        rows_ref[:, width:], eye, (((0,), (0,)), ((), ())), preferred_element_type=jnp.float32
    )
    id0, id1, code0, code1 = (info[i : i + 1, :] for i in range(4))
    slot_of = lax.broadcasted_iota(jnp.int32, (capacity, count), 0).astype(jnp.float32)
    first = lax.axis_index("sec") * experts if halves == 1 else lax.axis_index("sec") // halves
    picks, shares = [], []
    for x in range(experts):
        e = (first + x).astype(jnp.float32)
        hit0 = jnp.where(id0 == e, 1.0, 0.0)
        hit1 = jnp.where(id1 == e, 1.0, 0.0)
        member = hit0 + hit1
        share = (hit0 * code0 + hit1 * code1) / (code0 + code1)
        slot = dot(jnp.broadcast_to(member, (8, count)).astype(jnp.bfloat16), before)[:1]
        slot = jnp.where(member > 0.5, slot, -1.0)
        pick = slot == slot_of
        shares.append(jnp.sum(jnp.where(pick, share, 0.0), axis=1, keepdims=True))
        picks.append(jnp.where(pick, 1.0, 0.0).astype(jnp.bfloat16))
    pick_ref[...] = jnp.concatenate(picks, axis=0)
    column = min(512, width)

    for c in range(0, width, column):
        packed_ref[:, c : c + column] = dot(pick_ref[...], rows_ref[:, c : c + column]).astype(
            jnp.bfloat16
        )
    for x in range(experts):
        mine = slice(x * capacity, (x + 1) * capacity)
        if x:
            stream.need(("gate", x))
        for s in range(0, per_expert, tile):
            cut = slice(s, s + tile)
            stream.step(0.85)
            if x:
                gate = dot(packed_ref[mine, :], gate_ref[x - 1, :, cut])
            else:
                gate = dot(packed_ref[mine, :top], gate_top[:, cut])
                gate = gate + dot(packed_ref[mine, top:], gate_low[:, cut])
            half = 0.5 * gate
            half_ref[:, cut] = half + half * jnp.tanh(half)
        stream.need(("up", x))
        for s in range(0, per_expert, tile):
            cut = slice(s, s + tile)
            stream.step(0.85)
            if x:
                up = dot(packed_ref[mine, :], up_ref[x - 1, :, cut])
            else:
                up = dot(packed_ref[mine, :high], up_first[:, cut])
                up = up + dot(packed_ref[mine, high:], up_low[:, cut])
            hidden_ref[mine, cut] = (half_ref[:, cut] * up).astype(jnp.bfloat16)
        rows = per_expert // cuts
        for i in range(cuts):
            stream.need(("down", x), cuts - 1 - i)
            part = slice(i * rows, (i + 1) * rows)
            out = dot(hidden_ref[mine, part], down_ref[part, :])
            if i:
                out = out + sum_ref[...]
            if i < cuts - 1:
                sum_ref[...] = out
            else:
                packed_ref[mine, :] = (out * shares[x]).astype(jnp.bfloat16)
            stream.step(0.85)
        stream.limit = stream.last["up", x + 2] if x + 2 < experts else len(stream.copies)
        stream.fill()
    spread(pick_ref, packed_ref, send_ref, pick_ref.shape[1] - send_ref.shape[0])


def spread(pick_ref, packed_ref, out_ref, first):
    rows, width = out_ref.shape
    column = min(512, width)
    for c in range(0, width, column):
        out_ref[:, c : c + column] = lax.dot_general(
            pick_ref[:, first : first + rows], packed_ref[:, c : c + column],
            (((0,), (0,)), ((), ())), preferred_element_type=jnp.float32,
        ).astype(out_ref.dtype)


def keep_kernel(pick_ref, packed_ref, out_ref):
    spread(pick_ref, packed_ref, out_ref, 0)


def per_device(
    query,
    keys,
    values,
    residual,
    out_weight,
    norm_gain,
    expert_ids,
    gate_codes,
    doc_lengths,
    w_gate,
    w_up,
    w_down,
):
    block, width = residual.shape
    head = HEAD_DIMENSION
    group_width = QUERY_HEAD_COUNT // KEY_VALUE_HEADS
    q_heads = query.shape[1] // head
    sec_count, tp_count, pp_count = (lax.axis_size(a) for a in ("sec", "tp", "pp"))
    own_rows = block // (tp_count * pp_count)
    bf16, f32 = jnp.bfloat16, jnp.float32

    kv_heads = max(1, q_heads // group_width)
    group = q_heads // kv_heads
    kv_start = lax.axis_index("pp") * q_heads // group_width * head
    kv = jnp.concatenate(
        [lax.dynamic_slice_in_dim(a, kv_start, kv_heads * head, 1) for a in (keys, values)], axis=1
    )
    back = -(-(sec_count * block // 2 - 1) // block)
    pieces = [
        lax.ppermute(kv, "sec", [(i, (i + k) % sec_count) for i in range(sec_count)])
        for k in range(back, 0, -1)
    ] + [kv]

    experts = max(1, E // sec_count)
    per_expert = w_gate.shape[2] // experts
    span = (back + 1) * block
    query_v, weight_v, gain_v, mask, order, residual_own, info, *gate_v = call(
        functools.partial(prepare_kernel, back, tp_count, pp_count),
        [
            sds(query.shape, bf16),
            sds(out_weight.shape, bf16),
            sds((1, width), f32),
            sds((block, span), f32),
            sds((block, block), bf16),
            sds((own_rows, width), f32),
            sds((own_rows, LANES), bf16),
        ]
        + [sds((width // 2, per_expert), bf16)],
        [
            (HBM, a)
            for a in (
                doc_lengths, expert_ids.T, gate_codes.T, query, out_weight, residual,
                norm_gain.reshape(1, width), w_gate[0],
            )
        ],
        scratch=[
            pltpu.SMEM(doc_lengths.shape, jnp.int32),
            pltpu.VMEM((2, block), jnp.int32),
            pltpu.VMEM((2, block), jnp.int32),
            pltpu.VMEM(residual.shape, bf16),
            pltpu.SemaphoreType.DMA((8,)),
        ],
        vmem=6,
        name="prepare",
        cost_us=3.0,
    )
    half = block // pp_count
    keep, send = call(
        functools.partial(attention_kernel, back, kv_heads, group),
        [sds((half, width), f32), sds((block - half, width), bf16)],
        [(VMEM, a) for a in (query_v, mask, order, *pieces, weight_v)],
        scratch=[pltpu.VMEM(query.shape, bf16)],
        name="attention",
        cost_us=2.4,
    )

    (own,), sends = add(
        [keep] + [xor_swap(send, "pp", 1)], [own_rows], [own_rows] * (tp_count - 1), "sum_cores"
    )
    got = [xor_swap(sends[k - 1], "tp", k) for k in range(1, tp_count)]
    up_v, token = load(w_up[0], 0, width * 3 // 4, per_expert, [own], "load_up")
    stream, normed = call(
        functools.partial(norm_kernel, tp_count),
        [sds((own_rows, width), f32), sds((own_rows, width + LANES), bf16)],
        [(VMEM, a) for a in (residual_own, gain_v, info, own, *got)] + [(ANY, token)],
        name="norm",
        cost_us=0.2,
    )

    groups = min(4, sec_count)
    near = {k: xor_swap(normed, "sec", k) if k else normed for k in range(0, sec_count, 2)}
    gate_late, token = load(w_gate[0], width // 2, width // 2, per_expert, [normed], "load_gate")
    if sec_count > 2:
        near[2] = join([near[2]], "join", [token])
    near.update({k + 1: xor_swap(near[k], "sec", 1) for k in list(near) if k + 1 < sec_count})
    near = [near[k] for k in range(sec_count)]
    per_group = sec_count // groups
    near = [
        jnp.concatenate(near[g * per_group : (g + 1) * per_group], axis=0)
        if per_group > 1
        else near[g]
        for g in range(groups)
    ]
    rows = [[r] + [xor_swap(r, "tp", k) for k in range(1, tp_count)] for r in near]
    rows = [rows[g][k] for k in range(tp_count) for g in range(groups)]
    rows = rows + [xor_swap(r, "pp", k) for k in range(1, pp_count) for r in rows]

    halves = max(1, sec_count // E)
    count = sec_count * block
    capacity = sec_count * MOSTB
    down = w_down[0]
    tile = min(512, down.shape[0] // experts)
    kept = count // pp_count
    slots = experts * capacity
    send, pick, weighted = call(
        functools.partial(experts_kernel, experts, capacity, tile, halves, len(rows)),
        [sds((count - kept, width), bf16), sds((slots, count), bf16), sds((slots, width), bf16)],
        [(VMEM, a) for a in (*rows, *gate_v, gate_late, up_v)]
        + [(HBM, a) for a in (w_gate[0], w_up[0], down)],
        scratch=[
            pltpu.VMEM((count, width + LANES), bf16),
            pltpu.VMEM((slots, down.shape[0] // experts), bf16),
            pltpu.VMEM((capacity, per_expert), f32),
            pltpu.VMEM((capacity, width), f32),
            pltpu.VMEM((width - up_v.shape[0], per_expert), bf16),
            pltpu.VMEM((max(1, experts - 1), width, per_expert), bf16),
            pltpu.VMEM((max(1, experts - 1), width, per_expert), bf16),
            pltpu.VMEM((per_expert, width), bf16),
            pltpu.SemaphoreType.DMA((4 * (3 * experts - 2) + 1,)),
        ],
        vmem=33,
        name="experts",
        cost_us=12.0,
    )

    keep = call(
        keep_kernel,
        sds((kept, width), f32),
        [(VMEM, pick), (VMEM, weighted)],
        name="keep",
        cost_us=0.4,
    )
    piece = kept // (tp_count * groups)
    own, sends = add(
        [keep, xor_swap(send, "pp", 1)], [piece] * groups, [piece] * (groups * (tp_count - 1)), "sum_cores2"
    )
    final = [stream]
    for g in range(groups - 1, -1, -1):
        got = [xor_swap(sends[(k - 1) * groups + g], "tp", k) for k in range(1, tp_count)]
        if g == 0 and per_group == 1:
            final += [own[0]] + got
            continue
        kept_rows = own_rows if g == 0 else 0
        mine, out = add(
            [own[g]] + got,
            [own_rows] if g == 0 else [],
            [own_rows] * (per_group - (g == 0)),
            "sum_x%d" % g,
        )
        final += list(mine)
        for j, o in enumerate(out):
            final.append(xor_swap(o, "sec", g * per_group + j + (g == 0)))
    return call(
        functools.partial(add_kernel, 0, len(final)),
        [sds((own_rows, width), bf16)],
        [(VMEM, a) for a in final],
        name="total",
        cost_us=0.2,
    )[0]


def solution(mesh):
    in_specs = (
        P(("groups", "sec"), ("tp", "pp")),
        P(("groups", "sec"), "tp"),
        P(("groups", "sec"), "tp"),
        P(("groups", "sec"), None),
        P(("tp", "pp"), None),
        P(),
        P(("groups", "sec"), None),
        P(("groups", "sec"), None),
        P("groups"),
        P(("tp", "pp"), None, "sec"),
        P(("tp", "pp"), None, "sec"),
        P(("tp", "pp"), "sec", None),
    )
    out_specs = P(("groups", "sec", "tp", "pp"), None)
    return jax.shard_map(
        per_device, mesh=mesh, in_specs=in_specs, out_specs=out_specs, check_vma=False
    )
```

```python
import functools

import jax
import jax.numpy as jnp
from jax import lax
from jax.experimental import pallas as pl
from jax.experimental.pallas import tpu as pltpu
from jax.sharding import PartitionSpec as P

QUERY_HEAD_COUNT = 32
KEY_VALUE_HEADS = 8
HEAD_DIMENSION = 128
E = 8
MOSTB = 32
LANES = 128

neg_fill = -1e30
norm_eps = 1e-05

VMEM = pl.BlockSpec(memory_space=pltpu.VMEM)
SMEM = pl.BlockSpec(memory_space=pltpu.SMEM)
HBM = pl.BlockSpec(memory_space=pltpu.HBM)
ANY = pl.BlockSpec(memory_space=pl.ANY)
MIB = 2**20


def dot(a, b):
    return jnp.dot(a, b, preferred_element_type=jnp.float32)


def xor_swap(x, axis, k):
    n = lax.axis_size(axis)
    return lax.ppermute(x, axis, [(i, i ^ k) for i in range(n)])


def call(kernel, out_shape, args, scratch=(), vmem=8, name=None, cost_us=1.0):
    args = [
        (s, pltpu.with_memory_space_constraint(a, pltpu.HBM) if s is HBM else a) for s, a in args
    ]
    single = not isinstance(out_shape, (tuple, list))
    return pl.pallas_call(
        kernel,
        out_shape=out_shape,
        in_specs=[s for s, _ in args],
        out_specs=VMEM if single else [VMEM] * len(out_shape),
        scratch_shapes=list(scratch),
        compiler_params=pltpu.CompilerParams(vmem_limit_bytes=vmem * MIB),
        cost_estimate=pl.CostEstimate(
            flops=0, bytes_accessed=int(cost_us * 3.4e6), transcendentals=0
        ),
        name=name,
    )(*[a for _, a in args])


def sds(shape, dtype):
    return jax.ShapeDtypeStruct(shape, dtype)


def position():
    rank = lax.axis_index("tp") * lax.axis_size("pp") + lax.axis_index("pp")
    return lax.axis_index("sec"), rank


def columns(source, targets, first=0):
    per = targets[0].shape[1] if targets else 0
    return [
        (source.at[pl.ds(0, t.shape[0]), pl.ds((first + i) * per, per)], t)
        for i, t in enumerate(targets)
    ]


def prepare_kernel(
    back, tp_count, pp_count, lengths_hbm, ids_hbm, codes_hbm, query_hbm, weight_hbm, residual_hbm,
    gain_hbm, *refs
):
    gate_hbm, query_ref, weight_ref, gain_ref, mask_ref, order_ref, residual_ref, info_ref = refs[
        :8
    ]
    gate_refs = refs[8:-5]
    lengths, ids, codes, residual_all, sem = refs[-5:]
    pairs = [
        (lengths_hbm, lengths),
        (ids_hbm, ids),
        (codes_hbm, codes),
        (residual_hbm, residual_all),
        (query_hbm, query_ref),
        (gain_hbm, gain_ref),
        (weight_hbm, weight_ref),
    ] + columns(gate_hbm, gate_refs)
    copies = [pltpu.make_async_copy(a, b, sem.at[i]) for i, (a, b) in enumerate(pairs)]
    for c in copies:
        c.start()
    sec, rank = position()
    block = query_ref.shape[0]
    own_rows = residual_ref.shape[0]
    at = lax.broadcasted_iota(jnp.int32, (block, block), 0)
    to = lax.broadcasted_iota(jnp.int32, (block, block), 1)
    chunk = lax.div(at, own_rows)
    flip = lax.rem(chunk, tp_count) * pp_count + lax.div(chunk, tp_count)
    source = (rank ^ flip) * own_rows + lax.rem(at, own_rows)
    order_ref[...] = jnp.where(to == source, 1.0, 0.0).astype(jnp.bfloat16)
    own = lax.broadcasted_iota(jnp.int32, (own_rows, block), 0) + rank * own_rows
    own = jnp.where(own == lax.broadcasted_iota(jnp.int32, (own_rows, block), 1), 1.0, 0.0)
    own = own.astype(jnp.bfloat16)
    for c in copies[:4]:
        c.wait()
    span = (back + 1) * block
    rows = sec * block + lax.broadcasted_iota(jnp.int32, (block, span), 0)
    cols = (sec - back) * block + lax.broadcasted_iota(jnp.int32, (block, span), 1)
    first = jnp.zeros((block, span), jnp.int32)
    end = jnp.int32(0)
    for d in range(lengths.shape[0]):
        end = end + lengths[d]
        first = jnp.where(rows >= end, end, first)
    mask_ref[...] = jnp.where((cols <= rows) & (cols >= first), 1.0, 0.0)
    residual_ref[...] = dot(own, residual_all[...])
    info = jnp.concatenate(
        [ids[...], codes[...], jnp.zeros((LANES - 4, block), jnp.int32)], axis=0
    ).astype(jnp.float32)
    info_ref[...] = lax.dot_general(
        own, info.astype(jnp.bfloat16), (((1,), (1,)), ((), ())), preferred_element_type=jnp.float32
    ).astype(jnp.bfloat16)
    for c in copies[4:]:
        c.wait()


def load_kernel(first, n_after, source, *refs):
    target, token_ref, sem = refs[n_after:]
    rows, cols = target.shape
    copy = pltpu.make_async_copy(
        source.at[pl.ds(first, rows), pl.ds(0, cols)], target, sem
    )
    copy.start()
    token_ref[...] = jnp.zeros_like(token_ref)
    copy.wait()


def load(array, first, rows, columns, after, name):
    return call(
        functools.partial(load_kernel, first, len(after)),
        [sds((rows, columns), array.dtype), sds((8, LANES), jnp.float32)],
        [(HBM, array)] + [(ANY, a) for a in after],
        scratch=[pltpu.SemaphoreType.DMA],
        vmem=1,
        name=name,
        cost_us=rows * columns * 2 / 3.4e6,
    )


def join_kernel(n, *refs):
    start = 0
    for r in refs[:n]:
        refs[-1][start : start + r.shape[0], :] = r[...]
        start += r.shape[0]


def join(arrays, name, after=()):
    return call(
        functools.partial(join_kernel, len(arrays)),
        sds((sum(a.shape[0] for a in arrays), arrays[0].shape[1]), arrays[0].dtype),
        [(VMEM, a) for a in arrays] + [(ANY, a) for a in after],
        name=name,
        cost_us=0.1,
    )


def attention_kernel(back, kv_heads, group, q_ref, mask_ref, order_ref, *refs):
    kv_refs = refs[: back + 1]
    weight_ref, keep_ref, send_ref, attended_ref = refs[back + 1 :]
    block = q_ref.shape[0]
    head = HEAD_DIMENSION
    allowed = jnp.concatenate([mask_ref[...]] * group, axis=0) > 0.5
    for g in range(kv_heads):
        q = jnp.concatenate(
            [q_ref[:, (g * group + t) * head : (g * group + t + 1) * head] for t in range(group)],
            axis=0,
        )
        k = jnp.concatenate([r[:, g * head : (g + 1) * head] for r in kv_refs], axis=0)
        v = jnp.concatenate(
            [r[:, (kv_heads + g) * head : (kv_heads + g + 1) * head] for r in kv_refs], axis=0
        )
        scores = lax.dot_general(
            q, k, (((1,), (1,)), ((), ())), preferred_element_type=jnp.float32
        ) * (head**-0.5)
        scores = jnp.where(allowed, scores, neg_fill)
        top = jnp.max(scores, axis=1, keepdims=True)
        weights = jnp.where(allowed, jnp.exp(scores - top), 0.0)
        total = jnp.sum(weights, axis=1, keepdims=True)
        summed = dot(weights.astype(jnp.bfloat16), v) / total
        for t in range(group):
            attended_ref[:, (g * group + t) * head : (g * group + t + 1) * head] = summed[
                t * block : (t + 1) * block
            ].astype(jnp.bfloat16)
    attended = dot(order_ref[...], attended_ref[...]).astype(jnp.bfloat16)
    mixed = dot(attended, weight_ref[...])
    kept = keep_ref.shape[0]
    keep_ref[...] = mixed[:kept]
    send_ref[...] = mixed[kept:].astype(jnp.bfloat16)


def add_kernel(keep_rows, n_in, *refs):
    total = refs[0][...].astype(jnp.float32)
    for r in refs[1:n_in]:
        total = total + r[...].astype(jnp.float32)
    start = 0
    for r in refs[n_in:]:
        r[...] = total[start : start + r.shape[0]].astype(r.dtype)
        start += r.shape[0]


def add(arrays, keep, send, name):
    width = arrays[0].shape[1]
    out = [sds((r, width), jnp.float32) for r in keep]
    out += [sds((r, width), jnp.bfloat16) for r in send]
    out = call(
        functools.partial(add_kernel, sum(keep), len(arrays)),
        out,
        [(VMEM, a) for a in arrays],
        name=name,
        cost_us=0.2,
    )
    return out[: len(keep)], out[len(keep) :]


def norm_kernel(n_parts, residual_ref, gain_ref, info_ref, *refs):
    parts = refs[:n_parts]
    stream_ref, normed_ref = refs[-2:]
    width = residual_ref.shape[1]
    mixed = parts[0][...].astype(jnp.float32)
    for p in parts[1:]:
        mixed = mixed + p[...].astype(jnp.float32)
    stream = residual_ref[...] + mixed
    stream_ref[...] = stream
    meansq = jnp.mean(stream * stream, axis=1, keepdims=True)
    normed_ref[:, :width] = (stream * lax.rsqrt(meansq + norm_eps) * gain_ref[...]).astype(
        jnp.bfloat16
    )
    normed_ref[:, width:] = info_ref[...]


class Stream:
    def __init__(self, groups, sem, window):
        self.copies, self.last, self.window = [], {}, window
        for name, pairs in groups:
            for source, target in pairs:
                at = len(self.copies)
                self.copies.append(pltpu.make_async_copy(source, target, sem.at[at]))
            self.last[name] = len(self.copies)
        self.started = self.ended = 0
        self.limit = len(self.copies)
        self.clock = 0.0

    def fill(self):
        while self.started < self.limit and self.started - self.ended < self.window:
            self.copies[self.started].start()
            self.started += 1

    def end_one(self):
        self.copies[self.ended].wait()
        self.ended += 1
        self.fill()

    def need(self, name, but=0):
        while self.ended < self.last[name] - but:
            self.end_one()

    def step(self, cost):
        self.clock += cost
        while self.ended < self.started and self.ended + 2 <= self.clock:
            self.end_one()


def experts_kernel(experts, capacity, tile, halves, n_rows, *refs):
    rows_in = refs[:n_rows]
    gate_top, gate_low, up_first, gate_hbm, up_hbm, down_hbm = refs[n_rows : n_rows + 6]
    send_ref, pick_ref, packed_ref = refs[n_rows + 6 : n_rows + 9]
    rows_ref, hidden_ref, half_ref, sum_ref, up_low, gate_ref, up_ref, down_ref, sem = refs[
        n_rows + 9 :
    ]
    per_expert, width = down_hbm.shape[0] // experts, down_hbm.shape[1]
    column = min(512, width)
    cuts = 4
    top, high = gate_top.shape[0], up_first.shape[0]

    def pieces(source, target, x, columns):
        rows = target.shape[0] // cuts
        pairs = []
        for i in range(cuts):
            to = pl.ds(i * rows, rows)
            if columns:
                part = source.at[to, pl.ds(x * per_expert, per_expert)]
            else:
                part = source.at[pl.ds(x * per_expert + i * rows, rows)]
            pairs.append((part, target.at[to]))
        return pairs

    groups = []
    if high < width:
        low = up_hbm.at[pl.ds(high, width - high), pl.ds(0, per_expert)]
        groups.append((("up", 0), [(low, up_low)]))
    for x in range(experts):
        if x:
            groups.append((("gate", x), pieces(gate_hbm, gate_ref.at[x - 1], x, True)))
            groups.append((("up", x), pieces(up_hbm, up_ref.at[x - 1], x, True)))
        groups.append((("down", x), pieces(down_hbm, down_ref, x, False)))
    stream = Stream(groups, sem, 4)
    stream.limit = stream.last["up", 1] if experts > 1 else stream.limit
    stream.fill()
    count = 0
    for r in rows_in:
        rows_ref[count : count + r.shape[0], :] = r[...]
        count += r.shape[0]
    at0 = lax.broadcasted_iota(jnp.int32, (count, count), 0)
    at1 = lax.broadcasted_iota(jnp.int32, (count, count), 1)
    eye = jnp.where(at0 == at1, 1.0, 0.0).astype(jnp.bfloat16)
    before = jnp.where(at0 < at1, 1.0, 0.0).astype(jnp.bfloat16)
    info = lax.dot_general(
        rows_ref[:, width:], eye, (((0,), (0,)), ((), ())), preferred_element_type=jnp.float32
    )
    id0, id1, code0, code1 = (info[i : i + 1, :] for i in range(4))
    slot_of = lax.broadcasted_iota(jnp.int32, (capacity, count), 0).astype(jnp.float32)
    first = lax.axis_index("sec") * experts if halves == 1 else lax.axis_index("sec") // halves
    picks, shares = [], []
    for x in range(experts):
        e = (first + x).astype(jnp.float32)
        hit0 = jnp.where(id0 == e, 1.0, 0.0)
        hit1 = jnp.where(id1 == e, 1.0, 0.0)
        member = hit0 + hit1
        share = (hit0 * code0 + hit1 * code1) / (code0 + code1)
        slot = dot(jnp.broadcast_to(member, (8, count)).astype(jnp.bfloat16), before)[:1]
        slot = jnp.where(member > 0.5, slot, -1.0)
        pick = slot == slot_of
        shares.append(jnp.sum(jnp.where(pick, share, 0.0), axis=1, keepdims=True))
        picks.append(jnp.where(pick, 1.0, 0.0).astype(jnp.bfloat16))
    pick_ref[...] = jnp.concatenate(picks, axis=0)
    column = min(512, width)

    for c in range(0, width, column):
        packed_ref[:, c : c + column] = dot(pick_ref[...], rows_ref[:, c : c + column]).astype(
            jnp.bfloat16
        )
    for x in range(experts):
        mine = slice(x * capacity, (x + 1) * capacity)
        if x:
            stream.need(("gate", x))
        for s in range(0, per_expert, tile):
            cut = slice(s, s + tile)
            stream.step(0.85)
            if x:
                gate = dot(packed_ref[mine, :], gate_ref[x - 1, :, cut])
            else:
                gate = dot(packed_ref[mine, :top], gate_top[:, cut])
                gate = gate + dot(packed_ref[mine, top:], gate_low[:, cut])
            half = 0.5 * gate
            half_ref[:, cut] = half + half * jnp.tanh(half)
        stream.need(("up", x))
        for s in range(0, per_expert, tile):
            cut = slice(s, s + tile)
            stream.step(0.85)
            if x:
                up = dot(packed_ref[mine, :], up_ref[x - 1, :, cut])
            else:
                up = dot(packed_ref[mine, :high], up_first[:, cut])
                up = up + dot(packed_ref[mine, high:], up_low[:, cut])
            hidden_ref[mine, cut] = (half_ref[:, cut] * up).astype(jnp.bfloat16)
        rows = per_expert // cuts
        for i in range(cuts):
            stream.need(("down", x), cuts - 1 - i)
            part = slice(i * rows, (i + 1) * rows)
            out = dot(hidden_ref[mine, part], down_ref[part, :])
            if i:
                out = out + sum_ref[...]
            if i < cuts - 1:
                sum_ref[...] = out
            else:
                packed_ref[mine, :] = (out * shares[x]).astype(jnp.bfloat16)
            stream.step(0.85)
        stream.limit = stream.last["up", x + 2] if x + 2 < experts else len(stream.copies)
        stream.fill()
    spread(pick_ref, packed_ref, send_ref, pick_ref.shape[1] - send_ref.shape[0])


def spread(pick_ref, packed_ref, out_ref, first):
    rows, width = out_ref.shape
    column = min(512, width)
    for c in range(0, width, column):
        out_ref[:, c : c + column] = lax.dot_general(
            pick_ref[:, first : first + rows], packed_ref[:, c : c + column],
            (((0,), (0,)), ((), ())), preferred_element_type=jnp.float32,
        ).astype(out_ref.dtype)


def keep_kernel(pick_ref, packed_ref, out_ref):
    spread(pick_ref, packed_ref, out_ref, 0)


def per_device(
    query,
    keys,
    values,
    residual,
    out_weight,
    norm_gain,
    expert_ids,
    gate_codes,
    doc_lengths,
    w_gate,
    w_up,
    w_down,
):
    block, width = residual.shape
    head = HEAD_DIMENSION
    group_width = QUERY_HEAD_COUNT // KEY_VALUE_HEADS
    q_heads = query.shape[1] // head
    sec_count, tp_count, pp_count = (lax.axis_size(a) for a in ("sec", "tp", "pp"))
    own_rows = block // (tp_count * pp_count)
    bf16, f32 = jnp.bfloat16, jnp.float32

    kv_heads = max(1, q_heads // group_width)
    group = q_heads // kv_heads
    kv_start = lax.axis_index("pp") * q_heads // group_width * head
    kv = jnp.concatenate(
        [lax.dynamic_slice_in_dim(a, kv_start, kv_heads * head, 1) for a in (keys, values)], axis=1
    )
    back = -(-(sec_count * block // 2 - 1) // block)
    pieces = [
        lax.ppermute(kv, "sec", [(i, (i + k) % sec_count) for i in range(sec_count)])
        for k in range(back, 0, -1)
    ] + [kv]

    experts = max(1, E // sec_count)
    per_expert = w_gate.shape[2] // experts
    span = (back + 1) * block
    query_v, weight_v, gain_v, mask, order, residual_own, info, *gate_v = call(
        functools.partial(prepare_kernel, back, tp_count, pp_count),
        [
            sds(query.shape, bf16),
            sds(out_weight.shape, bf16),
            sds((1, width), f32),
            sds((block, span), f32),
            sds((block, block), bf16),
            sds((own_rows, width), f32),
            sds((own_rows, LANES), bf16),
        ]
        + [sds((width * 3 // 4, per_expert), bf16)],
        [
            (HBM, a)
            for a in (
                doc_lengths, expert_ids.T, gate_codes.T, query, out_weight, residual,
                norm_gain.reshape(1, width), w_gate[0],
            )
        ],
        scratch=[
            pltpu.SMEM(doc_lengths.shape, jnp.int32),
            pltpu.VMEM((2, block), jnp.int32),
            pltpu.VMEM((2, block), jnp.int32),
            pltpu.VMEM(residual.shape, bf16),
            pltpu.SemaphoreType.DMA((8,)),
        ],
        vmem=6,
        name="prepare",
        cost_us=3.0,
    )
    half = block // pp_count
    keep, send = call(
        functools.partial(attention_kernel, back, kv_heads, group),
        [sds((half, width), f32), sds((block - half, width), bf16)],
        [(VMEM, a) for a in (query_v, mask, order, *pieces, weight_v)],
        scratch=[pltpu.VMEM(query.shape, bf16)],
        name="attention",
        cost_us=2.4,
    )

    (own,), sends = add(
        [keep] + [xor_swap(send, "pp", 1)], [own_rows], [own_rows] * (tp_count - 1), "sum_cores"
    )
    got = [xor_swap(sends[k - 1], "tp", k) for k in range(1, tp_count)]
    up_v, token = load(w_up[0], 0, width * 3 // 4, per_expert, [own], "load_up")
    stream, normed = call(
        functools.partial(norm_kernel, tp_count),
        [sds((own_rows, width), f32), sds((own_rows, width + LANES), bf16)],
        [(VMEM, a) for a in (residual_own, gain_v, info, own, *got)] + [(ANY, token)],
        name="norm",
        cost_us=0.2,
    )

    groups = min(4, sec_count)
    near = {k: xor_swap(normed, "sec", k) if k else normed for k in range(0, sec_count, 2)}
    gate_late, token = load(w_gate[0], width * 3 // 4, width // 4, per_expert, [normed], "load_gate")
    if sec_count > 2:
        near[2] = join([near[2]], "join", [token])
    near.update({k + 1: xor_swap(near[k], "sec", 1) for k in list(near) if k + 1 < sec_count})
    near = [near[k] for k in range(sec_count)]
    per_group = sec_count // groups
    near = [
        jnp.concatenate(near[g * per_group : (g + 1) * per_group], axis=0)
        if per_group > 1
        else near[g]
        for g in range(groups)
    ]
    rows = [[r] + [xor_swap(r, "tp", k) for k in range(1, tp_count)] for r in near]
    rows = [rows[g][k] for k in range(tp_count) for g in range(groups)]
    rows = rows + [xor_swap(r, "pp", k) for k in range(1, pp_count) for r in rows]

    halves = max(1, sec_count // E)
    count = sec_count * block
    capacity = sec_count * MOSTB
    down = w_down[0]
    tile = min(512, down.shape[0] // experts)
    kept = count // pp_count
    slots = experts * capacity
    send, pick, weighted = call(
        functools.partial(experts_kernel, experts, capacity, tile, halves, len(rows)),
        [sds((count - kept, width), bf16), sds((slots, count), bf16), sds((slots, width), bf16)],
        [(VMEM, a) for a in (*rows, *gate_v, gate_late, up_v)]
        + [(HBM, a) for a in (w_gate[0], w_up[0], down)],
        scratch=[
            pltpu.VMEM((count, width + LANES), bf16),
            pltpu.VMEM((slots, down.shape[0] // experts), bf16),
            pltpu.VMEM((capacity, per_expert), f32),
            pltpu.VMEM((capacity, width), f32),
            pltpu.VMEM((width - up_v.shape[0], per_expert), bf16),
            pltpu.VMEM((max(1, experts - 1), width, per_expert), bf16),
            pltpu.VMEM((max(1, experts - 1), width, per_expert), bf16),
            pltpu.VMEM((per_expert, width), bf16),
            pltpu.SemaphoreType.DMA((4 * (3 * experts - 2) + 1,)),
        ],
        vmem=33,
        name="experts",
        cost_us=12.0,
    )

    keep = call(
        keep_kernel,
        sds((kept, width), f32),
        [(VMEM, pick), (VMEM, weighted)],
        name="keep",
        cost_us=0.4,
    )
    piece = kept // (tp_count * groups)
    own, sends = add(
        [keep, xor_swap(send, "pp", 1)], [piece] * groups, [piece] * (groups * (tp_count - 1)), "sum_cores2"
    )
    final = [stream]
    for g in range(groups - 1, -1, -1):
        got = [xor_swap(sends[(k - 1) * groups + g], "tp", k) for k in range(1, tp_count)]
        if g == 0 and per_group == 1:
            final += [own[0]] + got
            continue
        kept_rows = own_rows if g == 0 else 0
        mine, out = add(
            [own[g]] + got,
            [own_rows] if g == 0 else [],
            [own_rows] * (per_group - (g == 0)),
            "sum_x%d" % g,
        )
        final += list(mine)
        for j, o in enumerate(out):
            final.append(xor_swap(o, "sec", g * per_group + j + (g == 0)))
    return call(
        functools.partial(add_kernel, 0, len(final)),
        [sds((own_rows, width), bf16)],
        [(VMEM, a) for a in final],
        name="total",
        cost_us=0.2,
    )[0]


def solution(mesh):
    in_specs = (
        P(("groups", "sec"), ("tp", "pp")),
        P(("groups", "sec"), "tp"),
        P(("groups", "sec"), "tp"),
        P(("groups", "sec"), None),
        P(("tp", "pp"), None),
        P(),
        P(("groups", "sec"), None),
        P(("groups", "sec"), None),
        P("groups"),
        P(("tp", "pp"), None, "sec"),
        P(("tp", "pp"), None, "sec"),
        P(("tp", "pp"), "sec", None),
    )
    out_specs = P(("groups", "sec", "tp", "pp"), None)
    return jax.shard_map(
        per_device, mesh=mesh, in_specs=in_specs, out_specs=out_specs, check_vma=False
    )
```

```python
import functools

import jax
import jax.numpy as jnp
from jax import lax
from jax.experimental import pallas as pl
from jax.experimental.pallas import tpu as pltpu
from jax.sharding import PartitionSpec as P

QUERY_HEAD_COUNT = 32
KEY_VALUE_HEADS = 8
HEAD_DIMENSION = 128
E = 8
MOSTB = 32
LANES = 128

neg_fill = -1e30
norm_eps = 1e-05

VMEM = pl.BlockSpec(memory_space=pltpu.VMEM)
SMEM = pl.BlockSpec(memory_space=pltpu.SMEM)
HBM = pl.BlockSpec(memory_space=pltpu.HBM)
ANY = pl.BlockSpec(memory_space=pl.ANY)
MIB = 2**20


def dot(a, b):
    return jnp.dot(a, b, preferred_element_type=jnp.float32)


def xor_swap(x, axis, k):
    n = lax.axis_size(axis)
    return lax.ppermute(x, axis, [(i, i ^ k) for i in range(n)])


def call(kernel, out_shape, args, scratch=(), vmem=8, name=None, cost_us=1.0):
    args = [
        (s, pltpu.with_memory_space_constraint(a, pltpu.HBM) if s is HBM else a) for s, a in args
    ]
    single = not isinstance(out_shape, (tuple, list))
    return pl.pallas_call(
        kernel,
        out_shape=out_shape,
        in_specs=[s for s, _ in args],
        out_specs=VMEM if single else [VMEM] * len(out_shape),
        scratch_shapes=list(scratch),
        compiler_params=pltpu.CompilerParams(vmem_limit_bytes=vmem * MIB),
        cost_estimate=pl.CostEstimate(
            flops=0, bytes_accessed=int(cost_us * 3.4e6), transcendentals=0
        ),
        name=name,
    )(*[a for _, a in args])


def sds(shape, dtype):
    return jax.ShapeDtypeStruct(shape, dtype)


def position():
    rank = lax.axis_index("tp") * lax.axis_size("pp") + lax.axis_index("pp")
    return lax.axis_index("sec"), rank


def columns(source, targets, first=0):
    per = targets[0].shape[1] if targets else 0
    return [
        (source.at[pl.ds(0, t.shape[0]), pl.ds((first + i) * per, per)], t)
        for i, t in enumerate(targets)
    ]


def prepare_kernel(
    back, tp_count, pp_count, lengths_hbm, ids_hbm, codes_hbm, query_hbm, weight_hbm, residual_hbm,
    gain_hbm, *refs
):
    gate_hbm, query_ref, weight_ref, gain_ref, mask_ref, order_ref, residual_ref, info_ref = refs[
        :8
    ]
    gate_refs = refs[8:-5]
    lengths, ids, codes, residual_all, sem = refs[-5:]
    pairs = [
        (lengths_hbm, lengths),
        (ids_hbm, ids),
        (codes_hbm, codes),
        (residual_hbm, residual_all),
        (query_hbm, query_ref),
        (gain_hbm, gain_ref),
        (weight_hbm, weight_ref),
    ] + columns(gate_hbm, gate_refs)
    copies = [pltpu.make_async_copy(a, b, sem.at[i]) for i, (a, b) in enumerate(pairs)]
    for c in copies:
        c.start()
    sec, rank = position()
    block = query_ref.shape[0]
    own_rows = residual_ref.shape[0]
    at = lax.broadcasted_iota(jnp.int32, (block, block), 0)
    to = lax.broadcasted_iota(jnp.int32, (block, block), 1)
    chunk = lax.div(at, own_rows)
    flip = lax.rem(chunk, tp_count) * pp_count + lax.div(chunk, tp_count)
    source = (rank ^ flip) * own_rows + lax.rem(at, own_rows)
    order_ref[...] = jnp.where(to == source, 1.0, 0.0).astype(jnp.bfloat16)
    own = lax.broadcasted_iota(jnp.int32, (own_rows, block), 0) + rank * own_rows
    own = jnp.where(own == lax.broadcasted_iota(jnp.int32, (own_rows, block), 1), 1.0, 0.0)
    own = own.astype(jnp.bfloat16)
    for c in copies[:4]:
        c.wait()
    span = (back + 1) * block
    rows = sec * block + lax.broadcasted_iota(jnp.int32, (block, span), 0)
    cols = (sec - back) * block + lax.broadcasted_iota(jnp.int32, (block, span), 1)
    first = jnp.zeros((block, span), jnp.int32)
    end = jnp.int32(0)
    for d in range(lengths.shape[0]):
        end = end + lengths[d]
        first = jnp.where(rows >= end, end, first)
    mask_ref[...] = jnp.where((cols <= rows) & (cols >= first), 1.0, 0.0)
    residual_ref[...] = dot(own, residual_all[...])
    info = jnp.concatenate(
        [ids[...], codes[...], jnp.zeros((LANES - 4, block), jnp.int32)], axis=0
    ).astype(jnp.float32)
    info_ref[...] = lax.dot_general(
        own, info.astype(jnp.bfloat16), (((1,), (1,)), ((), ())), preferred_element_type=jnp.float32
    ).astype(jnp.bfloat16)
    for c in copies[4:]:
        c.wait()


def load_kernel(first, n_after, source, *refs):
    target, token_ref, sem = refs[n_after:]
    rows, cols = target.shape
    copy = pltpu.make_async_copy(
        source.at[pl.ds(first, rows), pl.ds(0, cols)], target, sem
    )
    copy.start()
    token_ref[...] = jnp.zeros_like(token_ref)
    copy.wait()


def load(array, first, rows, columns, after, name):
    return call(
        functools.partial(load_kernel, first, len(after)),
        [sds((rows, columns), array.dtype), sds((8, LANES), jnp.float32)],
        [(HBM, array)] + [(ANY, a) for a in after],
        scratch=[pltpu.SemaphoreType.DMA],
        vmem=1,
        name=name,
        cost_us=rows * columns * 2 / 3.4e6,
    )


def join_kernel(n, *refs):
    start = 0
    for r in refs[:n]:
        refs[-1][start : start + r.shape[0], :] = r[...]
        start += r.shape[0]


def join(arrays, name, after=()):
    return call(
        functools.partial(join_kernel, len(arrays)),
        sds((sum(a.shape[0] for a in arrays), arrays[0].shape[1]), arrays[0].dtype),
        [(VMEM, a) for a in arrays] + [(ANY, a) for a in after],
        name=name,
        cost_us=0.1,
    )


def attention_kernel(back, kv_heads, group, q_ref, mask_ref, order_ref, *refs):
    kv_refs = refs[: back + 1]
    weight_ref, keep_ref, send_ref, attended_ref = refs[back + 1 :]
    block = q_ref.shape[0]
    head = HEAD_DIMENSION
    allowed = jnp.concatenate([mask_ref[...]] * group, axis=0) > 0.5
    for g in range(kv_heads):
        q = jnp.concatenate(
            [q_ref[:, (g * group + t) * head : (g * group + t + 1) * head] for t in range(group)],
            axis=0,
        )
        k = jnp.concatenate([r[:, g * head : (g + 1) * head] for r in kv_refs], axis=0)
        v = jnp.concatenate(
            [r[:, (kv_heads + g) * head : (kv_heads + g + 1) * head] for r in kv_refs], axis=0
        )
        scores = lax.dot_general(
            q, k, (((1,), (1,)), ((), ())), preferred_element_type=jnp.float32
        ) * (head**-0.5)
        scores = jnp.where(allowed, scores, neg_fill)
        top = jnp.max(scores, axis=1, keepdims=True)
        weights = jnp.where(allowed, jnp.exp(scores - top), 0.0)
        total = jnp.sum(weights, axis=1, keepdims=True)
        summed = dot(weights.astype(jnp.bfloat16), v) / total
        for t in range(group):
            attended_ref[:, (g * group + t) * head : (g * group + t + 1) * head] = summed[
                t * block : (t + 1) * block
            ].astype(jnp.bfloat16)
    attended = dot(order_ref[...], attended_ref[...]).astype(jnp.bfloat16)
    mixed = dot(attended, weight_ref[...])
    kept = keep_ref.shape[0]
    keep_ref[...] = mixed[:kept]
    send_ref[...] = mixed[kept:].astype(jnp.bfloat16)


def add_kernel(keep_rows, n_in, *refs):
    total = refs[0][...].astype(jnp.float32)
    for r in refs[1:n_in]:
        total = total + r[...].astype(jnp.float32)
    start = 0
    for r in refs[n_in:]:
        r[...] = total[start : start + r.shape[0]].astype(r.dtype)
        start += r.shape[0]


def add(arrays, keep, send, name):
    width = arrays[0].shape[1]
    out = [sds((r, width), jnp.float32) for r in keep]
    out += [sds((r, width), jnp.bfloat16) for r in send]
    out = call(
        functools.partial(add_kernel, sum(keep), len(arrays)),
        out,
        [(VMEM, a) for a in arrays],
        name=name,
        cost_us=0.2,
    )
    return out[: len(keep)], out[len(keep) :]


def norm_kernel(n_parts, residual_ref, gain_ref, info_ref, *refs):
    parts = refs[:n_parts]
    stream_ref, normed_ref = refs[-2:]
    width = residual_ref.shape[1]
    mixed = parts[0][...].astype(jnp.float32)
    for p in parts[1:]:
        mixed = mixed + p[...].astype(jnp.float32)
    stream = residual_ref[...] + mixed
    stream_ref[...] = stream
    meansq = jnp.mean(stream * stream, axis=1, keepdims=True)
    normed_ref[:, :width] = (stream * lax.rsqrt(meansq + norm_eps) * gain_ref[...]).astype(
        jnp.bfloat16
    )
    normed_ref[:, width:] = info_ref[...]


class Stream:
    def __init__(self, groups, sem, window):
        self.copies, self.last, self.window = [], {}, window
        for name, pairs in groups:
            for source, target in pairs:
                at = len(self.copies)
                self.copies.append(pltpu.make_async_copy(source, target, sem.at[at]))
            self.last[name] = len(self.copies)
        self.started = self.ended = 0
        self.limit = len(self.copies)
        self.clock = 0.0

    def fill(self):
        while self.started < self.limit and self.started - self.ended < self.window:
            self.copies[self.started].start()
            self.started += 1

    def end_one(self):
        self.copies[self.ended].wait()
        self.ended += 1
        self.fill()

    def need(self, name, but=0):
        while self.ended < self.last[name] - but:
            self.end_one()

    def step(self, cost):
        self.clock += cost
        while self.ended < self.started and self.ended + 2 <= self.clock:
            self.end_one()


def experts_kernel(experts, capacity, tile, halves, n_rows, *refs):
    rows_in = refs[:n_rows]
    gate_top, gate_low, up_first, gate_hbm, up_hbm, down_hbm = refs[n_rows : n_rows + 6]
    send_ref, pick_ref, packed_ref = refs[n_rows + 6 : n_rows + 9]
    rows_ref, hidden_ref, half_ref, sum_ref, up_low, gate_ref, up_ref, down_ref, sem = refs[
        n_rows + 9 :
    ]
    per_expert, width = down_hbm.shape[0] // experts, down_hbm.shape[1]
    column = min(512, width)
    cuts = 4
    top, high = gate_top.shape[0], up_first.shape[0]

    def pieces(source, target, x, columns):
        rows = target.shape[0] // cuts
        pairs = []
        for i in range(cuts):
            to = pl.ds(i * rows, rows)
            if columns:
                part = source.at[to, pl.ds(x * per_expert, per_expert)]
            else:
                part = source.at[pl.ds(x * per_expert + i * rows, rows)]
            pairs.append((part, target.at[to]))
        return pairs

    groups = []
    if high < width:
        low = up_hbm.at[pl.ds(high, width - high), pl.ds(0, per_expert)]
        groups.append((("up", 0), [(low, up_low)]))
    for x in range(experts):
        if x:
            groups.append((("gate", x), pieces(gate_hbm, gate_ref.at[x - 1], x, True)))
            groups.append((("up", x), pieces(up_hbm, up_ref.at[x - 1], x, True)))
        groups.append((("down", x), pieces(down_hbm, down_ref, x, False)))
    stream = Stream(groups, sem, 6)
    stream.limit = stream.last["up", 1] if experts > 1 else stream.limit
    stream.fill()
    count = 0
    for r in rows_in:
        rows_ref[count : count + r.shape[0], :] = r[...]
        count += r.shape[0]
    at0 = lax.broadcasted_iota(jnp.int32, (count, count), 0)
    at1 = lax.broadcasted_iota(jnp.int32, (count, count), 1)
    eye = jnp.where(at0 == at1, 1.0, 0.0).astype(jnp.bfloat16)
    before = jnp.where(at0 < at1, 1.0, 0.0).astype(jnp.bfloat16)
    info = lax.dot_general(
        rows_ref[:, width:], eye, (((0,), (0,)), ((), ())), preferred_element_type=jnp.float32
    )
    id0, id1, code0, code1 = (info[i : i + 1, :] for i in range(4))
    slot_of = lax.broadcasted_iota(jnp.int32, (capacity, count), 0).astype(jnp.float32)
    first = lax.axis_index("sec") * experts if halves == 1 else lax.axis_index("sec") // halves
    picks, shares = [], []
    for x in range(experts):
        e = (first + x).astype(jnp.float32)
        hit0 = jnp.where(id0 == e, 1.0, 0.0)
        hit1 = jnp.where(id1 == e, 1.0, 0.0)
        member = hit0 + hit1
        share = (hit0 * code0 + hit1 * code1) / (code0 + code1)
        slot = dot(jnp.broadcast_to(member, (8, count)).astype(jnp.bfloat16), before)[:1]
        slot = jnp.where(member > 0.5, slot, -1.0)
        pick = slot == slot_of
        shares.append(jnp.sum(jnp.where(pick, share, 0.0), axis=1, keepdims=True))
        picks.append(jnp.where(pick, 1.0, 0.0).astype(jnp.bfloat16))
    pick_ref[...] = jnp.concatenate(picks, axis=0)
    column = min(512, width)

    for c in range(0, width, column):
        packed_ref[:, c : c + column] = dot(pick_ref[...], rows_ref[:, c : c + column]).astype(
            jnp.bfloat16
        )
    for x in range(experts):
        mine = slice(x * capacity, (x + 1) * capacity)
        if x:
            stream.need(("gate", x))
        for s in range(0, per_expert, tile):
            cut = slice(s, s + tile)
            stream.step(0.85)
            if x:
                gate = dot(packed_ref[mine, :], gate_ref[x - 1, :, cut])
            else:
                gate = dot(packed_ref[mine, :top], gate_top[:, cut])
                gate = gate + dot(packed_ref[mine, top:], gate_low[:, cut])
            half = 0.5 * gate
            half_ref[:, cut] = half + half * jnp.tanh(half)
        stream.need(("up", x))
        for s in range(0, per_expert, tile):
            cut = slice(s, s + tile)
            stream.step(0.85)
            if x:
                up = dot(packed_ref[mine, :], up_ref[x - 1, :, cut])
            else:
                up = dot(packed_ref[mine, :high], up_first[:, cut])
                up = up + dot(packed_ref[mine, high:], up_low[:, cut])
            hidden_ref[mine, cut] = (half_ref[:, cut] * up).astype(jnp.bfloat16)
        rows = per_expert // cuts
        for i in range(cuts):
            stream.need(("down", x), cuts - 1 - i)
            part = slice(i * rows, (i + 1) * rows)
            out = dot(hidden_ref[mine, part], down_ref[part, :])
            if i:
                out = out + sum_ref[...]
            if i < cuts - 1:
                sum_ref[...] = out
            else:
                packed_ref[mine, :] = (out * shares[x]).astype(jnp.bfloat16)
            stream.step(0.85)
        stream.limit = stream.last["up", x + 2] if x + 2 < experts else len(stream.copies)
        stream.fill()
    spread(pick_ref, packed_ref, send_ref, pick_ref.shape[1] - send_ref.shape[0])


def spread(pick_ref, packed_ref, out_ref, first):
    rows, width = out_ref.shape
    column = min(512, width)
    for c in range(0, width, column):
        out_ref[:, c : c + column] = lax.dot_general(
            pick_ref[:, first : first + rows], packed_ref[:, c : c + column],
            (((0,), (0,)), ((), ())), preferred_element_type=jnp.float32,
        ).astype(out_ref.dtype)


def keep_kernel(pick_ref, packed_ref, out_ref):
    spread(pick_ref, packed_ref, out_ref, 0)


def per_device(
    query,
    keys,
    values,
    residual,
    out_weight,
    norm_gain,
    expert_ids,
    gate_codes,
    doc_lengths,
    w_gate,
    w_up,
    w_down,
):
    block, width = residual.shape
    head = HEAD_DIMENSION
    group_width = QUERY_HEAD_COUNT // KEY_VALUE_HEADS
    q_heads = query.shape[1] // head
    sec_count, tp_count, pp_count = (lax.axis_size(a) for a in ("sec", "tp", "pp"))
    own_rows = block // (tp_count * pp_count)
    bf16, f32 = jnp.bfloat16, jnp.float32

    kv_heads = max(1, q_heads // group_width)
    group = q_heads // kv_heads
    kv_start = lax.axis_index("pp") * q_heads // group_width * head
    kv = jnp.concatenate(
        [lax.dynamic_slice_in_dim(a, kv_start, kv_heads * head, 1) for a in (keys, values)], axis=1
    )
    back = -(-(sec_count * block // 2 - 1) // block)
    pieces = [
        lax.ppermute(kv, "sec", [(i, (i + k) % sec_count) for i in range(sec_count)])
        for k in range(back, 0, -1)
    ] + [kv]

    experts = max(1, E // sec_count)
    per_expert = w_gate.shape[2] // experts
    span = (back + 1) * block
    query_v, weight_v, gain_v, mask, order, residual_own, info, *gate_v = call(
        functools.partial(prepare_kernel, back, tp_count, pp_count),
        [
            sds(query.shape, bf16),
            sds(out_weight.shape, bf16),
            sds((1, width), f32),
            sds((block, span), f32),
            sds((block, block), bf16),
            sds((own_rows, width), f32),
            sds((own_rows, LANES), bf16),
        ]
        + [sds((width * 3 // 4, per_expert), bf16)],
        [
            (HBM, a)
            for a in (
                doc_lengths, expert_ids.T, gate_codes.T, query, out_weight, residual,
                norm_gain.reshape(1, width), w_gate[0],
            )
        ],
        scratch=[
            pltpu.SMEM(doc_lengths.shape, jnp.int32),
            pltpu.VMEM((2, block), jnp.int32),
            pltpu.VMEM((2, block), jnp.int32),
            pltpu.VMEM(residual.shape, bf16),
            pltpu.SemaphoreType.DMA((8,)),
        ],
        vmem=6,
        name="prepare",
        cost_us=3.0,
    )
    half = block // pp_count
    keep, send = call(
        functools.partial(attention_kernel, back, kv_heads, group),
        [sds((half, width), f32), sds((block - half, width), bf16)],
        [(VMEM, a) for a in (query_v, mask, order, *pieces, weight_v)],
        scratch=[pltpu.VMEM(query.shape, bf16)],
        name="attention",
        cost_us=2.4,
    )

    (own,), sends = add(
        [keep] + [xor_swap(send, "pp", 1)], [own_rows], [own_rows] * (tp_count - 1), "sum_cores"
    )
    got = [xor_swap(sends[k - 1], "tp", k) for k in range(1, tp_count)]
    up_v, token = load(w_up[0], 0, width * 3 // 4, per_expert, [own], "load_up")
    stream, normed = call(
        functools.partial(norm_kernel, tp_count),
        [sds((own_rows, width), f32), sds((own_rows, width + LANES), bf16)],
        [(VMEM, a) for a in (residual_own, gain_v, info, own, *got)] + [(ANY, token)],
        name="norm",
        cost_us=0.2,
    )

    groups = min(4, sec_count)
    near = {k: xor_swap(normed, "sec", k) if k else normed for k in range(0, sec_count, 2)}
    gate_late, token = load(w_gate[0], width * 3 // 4, width // 4, per_expert, [normed], "load_gate")
    if sec_count > 2:
        near[2] = join([near[2]], "join", [token])
    near.update({k + 1: xor_swap(near[k], "sec", 1) for k in list(near) if k + 1 < sec_count})
    near = [near[k] for k in range(sec_count)]
    per_group = sec_count // groups
    near = [
        jnp.concatenate(near[g * per_group : (g + 1) * per_group], axis=0)
        if per_group > 1
        else near[g]
        for g in range(groups)
    ]
    rows = [[r] + [xor_swap(r, "tp", k) for k in range(1, tp_count)] for r in near]
    rows = [rows[g][k] for k in range(tp_count) for g in range(groups)]
    rows = rows + [xor_swap(r, "pp", k) for k in range(1, pp_count) for r in rows]

    halves = max(1, sec_count // E)
    count = sec_count * block
    capacity = sec_count * MOSTB
    down = w_down[0]
    tile = min(512, down.shape[0] // experts)
    kept = count // pp_count
    slots = experts * capacity
    send, pick, weighted = call(
        functools.partial(experts_kernel, experts, capacity, tile, halves, len(rows)),
        [sds((count - kept, width), bf16), sds((slots, count), bf16), sds((slots, width), bf16)],
        [(VMEM, a) for a in (*rows, *gate_v, gate_late, up_v)]
        + [(HBM, a) for a in (w_gate[0], w_up[0], down)],
        scratch=[
            pltpu.VMEM((count, width + LANES), bf16),
            pltpu.VMEM((slots, down.shape[0] // experts), bf16),
            pltpu.VMEM((capacity, per_expert), f32),
            pltpu.VMEM((capacity, width), f32),
            pltpu.VMEM((width - up_v.shape[0], per_expert), bf16),
            pltpu.VMEM((max(1, experts - 1), width, per_expert), bf16),
            pltpu.VMEM((max(1, experts - 1), width, per_expert), bf16),
            pltpu.VMEM((per_expert, width), bf16),
            pltpu.SemaphoreType.DMA((4 * (3 * experts - 2) + 1,)),
        ],
        vmem=33,
        name="experts",
        cost_us=12.0,
    )

    keep = call(
        keep_kernel,
        sds((kept, width), f32),
        [(VMEM, pick), (VMEM, weighted)],
        name="keep",
        cost_us=0.4,
    )
    piece = kept // (tp_count * groups)
    own, sends = add(
        [keep, xor_swap(send, "pp", 1)], [piece] * groups, [piece] * (groups * (tp_count - 1)), "sum_cores2"
    )
    final = [stream]
    for g in range(groups - 1, -1, -1):
        got = [xor_swap(sends[(k - 1) * groups + g], "tp", k) for k in range(1, tp_count)]
        if g == 0 and per_group == 1:
            final += [own[0]] + got
            continue
        kept_rows = own_rows if g == 0 else 0
        mine, out = add(
            [own[g]] + got,
            [own_rows] if g == 0 else [],
            [own_rows] * (per_group - (g == 0)),
            "sum_x%d" % g,
        )
        final += list(mine)
        for j, o in enumerate(out):
            final.append(xor_swap(o, "sec", g * per_group + j + (g == 0)))
    return call(
        functools.partial(add_kernel, 0, len(final)),
        [sds((own_rows, width), bf16)],
        [(VMEM, a) for a in final],
        name="total",
        cost_us=0.2,
    )[0]


def solution(mesh):
    in_specs = (
        P(("groups", "sec"), ("tp", "pp")),
        P(("groups", "sec"), "tp"),
        P(("groups", "sec"), "tp"),
        P(("groups", "sec"), None),
        P(("tp", "pp"), None),
        P(),
        P(("groups", "sec"), None),
        P(("groups", "sec"), None),
        P("groups"),
        P(("tp", "pp"), None, "sec"),
        P(("tp", "pp"), None, "sec"),
        P(("tp", "pp"), "sec", None),
    )
    out_specs = P(("groups", "sec", "tp", "pp"), None)
    return jax.shard_map(
        per_device, mesh=mesh, in_specs=in_specs, out_specs=out_specs, check_vma=False
    )
```
